128 devices in a mesh: group: 8 (over z, core), local: 16 (over y, x).
Axes of the slice: x: 4, y: 4, z: 4, core: 2. Of those that a mesh axis runs over, the one named last changes fastest.
Arguments:
- tokens: bfloat16 [512, 7168], P('local'), may hold values from -6 to 6
- cotangent: bfloat16 [512, 7168], P('local'), may hold values from -6 to 6
- gate_logits: float32 [512, 24], P('local'), may hold values from -8 to 8
- route_slot: int32 [512, 8], P('local'), may hold values from 0 to 31, all different within a row; in each aligned block of 32 rows (0 to 31, 32 to 63, ...) at most 16 rows name the same one
- slot_expert: int32 [32], replicated, may hold values from 0 to 23, as said below
- w_gate: bfloat16 [32, 7168, 1024], P('local', None, 'group'), as said below
- w_up: bfloat16 [32, 7168, 1024], P('local', None, 'group'), as said below
- w_down: bfloat16 [32, 1024, 7168], P('local', 'group'), as said below
Outputs:
- mixed: bfloat16 [512, 7168], P('local', 'group')
- grad_tokens: bfloat16 [512, 7168], P('local', 'group')
- grad_logits: float32 [512, 24], P('local')
- grad_gate: bfloat16 [32, 7168, 1024], P('local', None, 'group')
- grad_up: bfloat16 [32, 7168, 1024], P('local', None, 'group')
- grad_down: bfloat16 [32, 1024, 7168], P('local', 'group')
The draws below stay inside these ranges and needn't reach their ends.
Inputs may be any that keep to these rules, and one draw needn't show every extreme that they name: `route_slot`: each token names 8 different slots. Of the 32 tokens of one index of local, at most 16 name one slot, a bound that some block reaches of them. `slot_expert`: the even slots hold 16 different experts, the odd slots the remaining ones, each on two odd slots: slot 2i + 1 and slot 2j + 1 hold the same expert where j = i plus or minus half the size of local (the one that stays in range). Every expert is held. `w_gate`: two odd slots that hold the same expert have equal weights; entries have standard deviation D ** -0.5. `w_up`: two odd slots that hold the same expert have equal weights; entries have standard deviation D ** -0.5. `w_down`: two odd slots that hold the same expert have equal weights; entries have standard deviation 1024 ** -0.5.
All inputs are finite; a program needn't handle non-finite values.
Results may differ from the reference program's by a relative error of at most 0.019.
Values may be sent and summed in bfloat16 or wider, within the bound.
No kernel may reach another device: no remote copies, remote signals or barrier semaphores. Data moves between devices by JAX's collectives and lax.ppermute only.
A program may use at most 192 MiB of HBM per device.

```python
import math
import jax
import jax.numpy as jnp
import numpy as np
from jax import lax

D = 7168
TOP = 8
FF = 1024
TOK_DEV = 32
TOKENS = 512
SLOTS = 32
EXPERTS = 24
CAP = 16
N_GROUP = 8
N_LOCAL = 16


def slot_keys():
    slot_index = jnp.arange(SLOTS, dtype=jnp.int32)
    half = SLOTS // 4
    return jnp.where(slot_index % 2 == 0, slot_index, 2 * (slot_index // 2 % half) + 1)


def expert_weight(key, salt, rows, cols, fan):
    base = jax.random.fold_in(key, salt)

    def one_slot(ident):
        return jax.random.normal(jax.random.fold_in(base, ident), (rows, cols), jnp.float32)
    return jax.vmap(one_slot)(slot_keys()) * fan ** (-0.5)


def draw_w_gate(key, part):
    return expert_weight(key, 11, D, FF, D).astype(jnp.bfloat16)


def draw_w_up(key, part):
    return expert_weight(key, 12, D, FF, D).astype(jnp.bfloat16)


def draw_w_down(key, part):
    return expert_weight(key, 13, FF, D, FF).astype(jnp.bfloat16)


def draw_slot_expert(key, part):
    order = jax.random.permutation(jax.random.fold_in(key, 5), EXPERTS)
    slot_index = jnp.arange(SLOTS, dtype=jnp.int32)
    line = slot_index // 2
    half = SLOTS // 4
    cold = order[line]
    hot = order[SLOTS // 2 + line % half]
    return jnp.where(slot_index % 2 == 0, cold, hot).astype(jnp.int32)


def block_levels(own_key, dims, split, smallest, largest):
    gain = 1.0
    for position, parts in split:
        steps = jax.random.uniform(jax.random.fold_in(jax.random.fold_in(own_key, 6), position), (parts,), jnp.float32, smallest / len(split), largest / len(split))
        gain = gain * jnp.repeat(jnp.exp(steps), dims[position] // parts).reshape((-1,) + (1,) * (len(dims) - 1 - position))
    return gain


def assign_block(own_key, own, number, rows, amount, top, reach, lean):
    sequence = jax.random.permutation(own_key, amount)
    packed, usual = portions_of(amount, rows * top, reach, lean, True), portions_of(amount, rows * top, reach, lean, False)
    places = jnp.arange(amount)

    def named(tallies, offset_by):
        used = int((tallies > 0).sum())
        fixed = max(1, used // 4)
        shifted = fixed + (places - fixed + offset_by * (used - fixed)) % max(1, amount - fixed)
        return jnp.zeros((amount,), jnp.int32).at[sequence[jnp.where(places < fixed, places, shifted)]].set(jnp.asarray(tallies, jnp.int32))

    tallies = jnp.where(number % 4 == 0, named(packed, number // 4), named(usual, number - number // 4 - 1))
    mixed = jax.random.permutation(jax.random.fold_in(own, 3), amount)
    giver, sink = mixed[0:amount // 2 * 2:2], mixed[1:amount // 2 * 2:2]
    room = jnp.minimum(tallies[giver] - 1, reach - tallies[sink]) // 2
    room = jnp.where((giver == sequence[0]) | (sink == sequence[0]) | (tallies[sink] == 0), 0, jnp.maximum(room, 0))
    shifted = jax.random.randint(jax.random.fold_in(own, 4), (amount // 2,), 0, 1 << 20) % (room + 1)
    tallies = tallies.at[giver].add(-shifted).at[sink].add(shifted)
    items = jnp.searchsorted(jnp.cumsum(tallies), jnp.arange(rows * top), side="right").astype(jnp.int32)
    listing = items.reshape(top, rows).T
    listing = listing[jax.random.permutation(jax.random.fold_in(own, 1), rows)]
    offset_by = jax.random.randint(jax.random.fold_in(own, 2), (rows, 1), 0, top)
    return jnp.take_along_axis(listing, (jnp.arange(top)[None, :] + offset_by) % top, axis=1)


def portions_of(amount, total, most, slope, full):
    loads = [(1 << 20) // math.isqrt(rank ** slope) + 1 for rank in range(1, amount + 1)]
    largest = most if full else min(most, max(-(-total // amount), total * loads[0] // sum(loads)))
    least = 1 if total - largest >= amount - 1 else 0
    holding, surplus = [largest] + [least] * (amount - 1), total - largest - least * (amount - 1)
    while surplus > 0:
        candidates = [i for i in range(1, amount) if holding[i] < largest] or [i for i in range(1, amount) if holding[i] < most]
        whole, remaining = sum([loads[i] for i in candidates]), surplus
        for i in candidates:
            addition = min(most - holding[i], max(1, remaining * loads[i] // whole), surplus)
            holding[i] = holding[i] + addition
            surplus = surplus - addition
    return np.array(holding)


def noise(key, dims, deviation, reach, pieces=(), kind=jnp.bfloat16):
    level = block_levels(key, dims, pieces, -0.22, 0.18) if pieces else 1.0
    values = jax.random.normal(key, dims, jnp.float32) * deviation * level
    return jnp.minimum(jnp.maximum(values, -reach), reach).astype(kind)


def setup_inputs(seed: int = 0) -> dict:
    key_of = jax.random.split(jax.random.key(seed), 9)
    tokens = noise(key_of[0], (TOKENS, D), 1.0, 6.0, ((0, 16),))
    cotangent = noise(key_of[1], (TOKENS, D), 1.0, 6.0, ((0, 16),))
    gate_logits = noise(key_of[2], (TOKENS, EXPERTS), 2.0, 8.0, ((0, 16),), jnp.float32)
    route_slot_keys = jax.random.split(jax.random.fold_in(key_of[3], 1), TOKENS // TOK_DEV)
    route_slot_turns = jax.random.permutation(jax.random.fold_in(key_of[3], 3), TOKENS // TOK_DEV)
    route_slot = jax.vmap(lambda own, number: assign_block(jax.random.fold_in(key_of[3], 2), own, number, TOK_DEV, SLOTS, TOP, CAP, 2))(route_slot_keys, route_slot_turns).reshape((TOKENS, TOP))
    slot_expert = draw_slot_expert(jax.random.fold_in(key_of[8], 71), 0)
    w_gate = draw_w_gate(jax.random.fold_in(key_of[8], 71), 0)
    w_up = draw_w_up(jax.random.fold_in(key_of[8], 71), 0)
    w_down = draw_w_down(jax.random.fold_in(key_of[8], 71), 0)
    return {"tokens": tokens, "cotangent": cotangent, "gate_logits": gate_logits, "route_slot": route_slot, "slot_expert": slot_expert, "w_gate": w_gate, "w_up": w_up, "w_down": w_down}


ROUTE_SCALE = 2.5

def gate_weights(logits, expert_ids):
    picked = jnp.take_along_axis(logits, expert_ids, axis=1)
    sig = jax.nn.sigmoid(picked)
    return ROUTE_SCALE * sig / lax.optimization_barrier(jnp.sum(sig, axis=1, keepdims=True))

def settle(value):
    return lax.optimization_barrier(value.astype(jnp.bfloat16)).astype(jnp.float32)

def expert_pass(rows_x, rows_g, w_g, w_u, w_d):
    first = jnp.dot(rows_x, w_g, preferred_element_type=jnp.float32)
    second = jnp.dot(rows_x, w_u, preferred_element_type=jnp.float32)
    sig = jax.nn.sigmoid(first)
    silu = first * sig
    hidden = (silu * second).astype(jnp.bfloat16)
    back = jnp.dot(rows_g, w_d.T, preferred_element_type=jnp.float32)
    d_first = (back * second * sig * (1.0 + first * (1.0 - sig))).astype(jnp.bfloat16)
    d_second = (back * silu).astype(jnp.bfloat16)
    piece = FF // N_GROUP
    out_sum = jnp.zeros((rows_x.shape[0], D), jnp.float32)
    grad_sum = jnp.zeros((rows_x.shape[0], D), jnp.float32)
    for block in range(N_GROUP):
        lo = block * piece
        hi = lo + piece
        out_sum = out_sum + settle(jnp.dot(hidden[:, lo:hi], w_d[lo:hi], preferred_element_type=jnp.float32))
        both = jnp.dot(d_first[:, lo:hi], w_g[:, lo:hi].T, preferred_element_type=jnp.float32)
        both = both + jnp.dot(d_second[:, lo:hi], w_u[:, lo:hi].T, preferred_element_type=jnp.float32)
        grad_sum = grad_sum + settle(both)
    own_gate = jnp.dot(rows_x.T, d_first, preferred_element_type=jnp.float32).astype(jnp.bfloat16)
    own_up = jnp.dot(rows_x.T, d_second, preferred_element_type=jnp.float32).astype(jnp.bfloat16)
    own_down = jnp.dot(hidden.T, rows_g, preferred_element_type=jnp.float32).astype(jnp.bfloat16)
    return (out_sum, grad_sum, own_gate, own_up, own_down)

def reference(tokens, cotangent, gate_logits, route_slot, slot_expert, w_gate, w_up, w_down):
    expert_ids = slot_expert[route_slot]
    weights, pull_back = jax.vjp(lambda lg: gate_weights(lg, expert_ids), gate_logits)
    scaled = (weights[:, :, None] * cotangent.astype(jnp.float32)[:, None, :]).astype(jnp.bfloat16)
    count = TOKENS * TOP
    flat = route_slot.reshape(-1)
    onehot = (flat[:, None] == jnp.arange(SLOTS, dtype=jnp.int32)[None, :]).astype(jnp.int32)
    blocks = onehot.reshape(N_LOCAL, TOK_DEV * TOP, SLOTS)
    rank = lax.optimization_barrier(jnp.sum((jnp.cumsum(blocks, axis=1) - blocks) * blocks, axis=2)).reshape(-1)
    source = jnp.arange(count, dtype=jnp.int32) // (TOK_DEV * TOP)
    place = (source * CAP + rank).astype(jnp.int32)
    table = jnp.full((SLOTS, N_LOCAL * CAP), count, jnp.int32)
    table = table.at[flat, place].set(jnp.arange(count, dtype=jnp.int32))
    zero_row = jnp.zeros((1, D), jnp.bfloat16)
    x_copies = jnp.concatenate([jnp.repeat(tokens, TOP, axis=0), zero_row], axis=0)
    g_copies = jnp.concatenate([scaled.reshape(count, D), zero_row], axis=0)

    def one_slot(carry, slot):
        out_acc, grad_acc = carry
        index = table[slot]
        result = expert_pass(x_copies[index], g_copies[index], w_gate[slot], w_up[slot], w_down[slot])
        out_acc = out_acc.at[index].add(result[0])
        grad_acc = grad_acc.at[index].add(result[1])
        return ((out_acc, grad_acc), (result[2], result[3], result[4]))
    start = (jnp.zeros((count + 1, D), jnp.float32), jnp.zeros((count + 1, D), jnp.float32))
    (out_acc, grad_acc), owns = lax.scan(one_slot, start, jnp.arange(SLOTS, dtype=jnp.int32))
    expert_out = out_acc[:count].reshape(TOKENS, TOP, D)
    expert_dx = grad_acc[:count].reshape(TOKENS, TOP, D)
    mixed = lax.optimization_barrier(jnp.sum(weights[:, :, None] * expert_out, axis=1)).astype(jnp.bfloat16)
    grad_tokens = lax.optimization_barrier(jnp.sum(expert_dx, axis=1)).astype(jnp.bfloat16)
    gate_dots = lax.optimization_barrier(jnp.sum(cotangent.astype(jnp.float32)[:, None, :] * expert_out, axis=2))
    grad_logits = pull_back(gate_dots)[0]
    slot_index = jnp.arange(SLOTS, dtype=jnp.int32)
    is_hot = slot_index % 2 == 1
    partner = jnp.where(is_hot, jnp.bitwise_xor(slot_index, N_LOCAL), slot_index)
    summed = []
    for own in owns:
        joined = (own.astype(jnp.float32) + own[partner].astype(jnp.float32)).astype(jnp.bfloat16)
        summed.append(jnp.where(is_hot[:, None, None], joined, own))
    return (mixed, grad_tokens, grad_logits, summed[0], summed[1], summed[2])
```

```python
import functools

import jax
import jax.numpy as jnp
from jax import lax
from jax.experimental import pallas as pl
from jax.experimental.pallas import tpu as pltpu
from jax.sharding import Mesh
from jax.sharding import PartitionSpec as P

ROUTE_SCALE = 2.5
NZ, NC, NY, NX = 4, 2, 4, 4
AXES = ("z", "c", "y", "x")
STEPS = 4
BF, F32 = jnp.bfloat16, jnp.float32
NT = (((1,), (1,)), ((), ()))
TN = (((0,), (0,)), ((), ()))
RING = (0, 1, 3, 2)


def moves(step):
    pairs = []
    for z in range(NZ):
        for c in range(NC):
            for y in range(NY):
                for x in range(NX):
                    z2, c2, y2, x2 = step(z, c, y, x)
                    source = ((z * NC + c) * NY + y) * NX + x
                    target = ((z2 % NZ * NC + c2 % NC) * NY + y2 % NY) * NX + x2 % NX
                    pairs.append((source, target))
    return pairs


def outer(by):
    return moves(lambda z, c, y, x: (z, c, y + by, x) if c == 0 else (z, c, y, x + by))


def inner(by):
    return moves(lambda z, c, y, x: (z, c, y, x + by) if c == 0 else (z, c, y + by, x))


def along_z(by):
    return moves(lambda z, c, y, x: (z + by, c, y, x))


def other_core():
    return moves(lambda z, c, y, x: (z, c + 1, y, x))


def send(value, pairs):
    return lax.ppermute(value, AXES, pairs)


def places(swapped):
    found = []
    for out in range(4):
        for inn in range(4):
            a, b = (inn, out) if swapped else (out, inn)
            found.append((2 * a + b // 2, 64 * (b % 2)))
    return found


def rows_of(refs, swapped, second, tok):
    parts = []
    for piece, row in places(swapped):
        row = row + (tok if second else 0)
        parts.append(refs[piece][row : row + tok, :])
    return jnp.concatenate(parts, axis=0)


def two(ref):
    return jnp.concatenate([ref[0, 0, 0], ref[1, 0, 0]], axis=1)


def partial_sums(swapped, rows, wg, wu, wd):
    tok = rows_of(rows, swapped, False, 32)
    cot = rows_of(rows, swapped, True, 32)
    first = jnp.dot(tok, two(wg), preferred_element_type=F32)
    second = jnp.dot(tok, two(wu), preferred_element_type=F32)
    down = wd[...].reshape(-1, wd.shape[-1])
    back = lax.dot_general(cot, down, NT, preferred_element_type=F32)
    return first, second, back


def own_half_kernel(sel, *refs):
    rows, (wg, wu, wd) = refs[:8], refs[8:11]
    sums = refs[11:14]
    parts = partial_sums(False, rows, wg, wu, wd)

    @pl.when(pl.program_id(0) == 0)
    def _():
        for ref, part in zip(sums, parts):
            ref[...] = part

    @pl.when(pl.program_id(0) > 0)
    def _():
        for ref, part in zip(sums, parts):
            ref[...] += part


def other_half_kernel(sel, *refs):
    rows, (wg, wu, wd) = refs[:8], refs[8:11]
    start, gains = refs[11:14], refs[14]
    h_out, d1_out, d2_out, h_grad, d1_grad, d2_grad, dots = refs[15:22]
    sums = refs[22:25]
    parts = partial_sums(True, rows, wg, wu, wd)

    @pl.when(pl.program_id(0) == 0)
    def _():
        for ref, before, part in zip(sums, start, parts):
            ref[...] = before[...] + part

    @pl.when(pl.program_id(0) > 0)
    def _():
        for ref, part in zip(sums, parts):
            ref[...] += part

    @pl.when(pl.program_id(0) == STEPS - 1)
    def _():
        lane = lax.broadcasted_iota(jnp.int32, dots.shape, 1)
        total = jnp.zeros(dots.shape, F32)
        for slot in range(2):
            units = slice(128 * slot, 128 * slot + 128)
            first, second, back = (ref[:, units] for ref in sums)
            mine = gains[:, slot : slot + 1]
            both = gains[:, 2 * slot : 2 * slot + 1]
            sig = jax.nn.sigmoid(first)
            silu = first * sig
            hidden = silu * second
            total = jnp.where(lane == slot, jnp.sum(hidden * back, axis=1, keepdims=True), total)
            d_first = back * second * sig * (1.0 + first * (1.0 - sig))
            d_second = back * silu
            h_out[:, units] = (hidden * mine).astype(BF)
            d1_out[:, units] = (d_first * mine).astype(BF)
            d2_out[:, units] = (d_second * mine).astype(BF)
            h_grad[:, units] = (hidden * both).astype(BF)
            d1_grad[:, units] = (d_first * both).astype(BF)
            d2_grad[:, units] = (d_second * both).astype(BF)
        dots[...] = total


def results_kernel(swapped, sel, hid, d1, d2, wg, wu, wd, *pieces):
    down = wd[...].reshape(-1, wd.shape[-1])
    out = jnp.dot(hid[...], down, preferred_element_type=F32)
    grad = lax.dot_general(d1[...], two(wg), NT, preferred_element_type=F32)
    grad += lax.dot_general(d2[...], two(wu), NT, preferred_element_type=F32)
    for block, (piece, row) in enumerate(places(swapped)):
        here = slice(32 * block, 32 * block + 32)
        pieces[piece][row : row + 32, :] = out[here].astype(BF)
        pieces[piece][row + 32 : row + 64, :] = grad[here].astype(BF)


def grads_kernel(sel, *refs):
    own, other = refs[:8], refs[8:16]
    hid, d1, d2 = refs[16:19]
    grad_gate, grad_up, grad_down = refs[19:22]

    def form(rows, swapped):
        tok = rows_of(rows, swapped, False, 32)
        cot = rows_of(rows, swapped, True, 32)
        gate = lax.dot_general(tok, d1[...], TN, preferred_element_type=F32).astype(BF)
        up = lax.dot_general(tok, d2[...], TN, preferred_element_type=F32).astype(BF)
        down = lax.dot_general(hid[...], cot, TN, preferred_element_type=F32).astype(BF)
        for slot in range(2):
            units = slice(128 * slot, 128 * slot + 128)
            grad_gate[slot, 0, 0] = gate[:, units]
            grad_up[slot, 0, 0] = up[:, units]
            grad_down[slot] = down[units]

    @pl.when(pl.program_id(0) == 0)
    def _():
        form(own, False)

    @pl.when(pl.program_id(0) == 1)
    def _():
        form(other, True)


def whole(shape):
    return pl.BlockSpec(shape, lambda *_: (0,) * len(shape))


def weight_specs(width):
    up_spec = pl.BlockSpec((2, 1, 1, width, 128), lambda k, sel: (0, k, sel[0], 0, 0))
    down_spec = pl.BlockSpec((2, 128, width), lambda k, sel: (0, 0, 2 * k + sel[0]))
    return [up_spec, up_spec, down_spec]


def params():
    return pltpu.CompilerParams(vmem_limit_bytes=48 * 2**20)


def own_half(sel, rows, weights):
    width = rows[0].shape[1] // STEPS
    row_spec = pl.BlockSpec((128, width), lambda k, sel: (0, k))
    return pl.pallas_call(
        own_half_kernel,
        grid_spec=pltpu.PrefetchScalarGridSpec(
            num_scalar_prefetch=1,
            grid=(STEPS,),
            in_specs=[row_spec] * 8 + weight_specs(width),
            out_specs=[whole((512, 256))] * 3,
        ),
        out_shape=[jax.ShapeDtypeStruct((512, 256), F32)] * 3,
        compiler_params=params(),
        cost_estimate=pl.CostEstimate(
            flops=2 * 512 * 768 * width * STEPS, bytes_accessed=13 * 2**20, transcendentals=0
        ),
        name="own_half",
    )(sel, *rows, *weights)


def other_half(sel, rows, weights, sums, gains):
    width = rows[0].shape[1] // STEPS
    row_spec = pl.BlockSpec((128, width), lambda k, sel: (0, k))
    return pl.pallas_call(
        other_half_kernel,
        grid_spec=pltpu.PrefetchScalarGridSpec(
            num_scalar_prefetch=1,
            grid=(STEPS,),
            in_specs=[row_spec] * 8
            + weight_specs(width)
            + [whole((512, 256))] * 3
            + [whole((512, 128))],
            out_specs=[whole((512, 256))] * 6 + [whole((512, 128))],
            scratch_shapes=[pltpu.VMEM((512, 256), F32)] * 3,
        ),
        out_shape=[jax.ShapeDtypeStruct((512, 256), BF)] * 6
        + [jax.ShapeDtypeStruct((512, 128), F32)],
        compiler_params=params(),
        cost_estimate=pl.CostEstimate(
            flops=2 * 512 * 768 * width * STEPS, bytes_accessed=15 * 2**20, transcendentals=512 * 256
        ),
        name="other_half",
    )(sel, *rows, *weights, *sums, gains)


def results(swapped, sel, hid, d1, d2, weights, half):
    width = half // STEPS
    return pl.pallas_call(
        functools.partial(results_kernel, swapped),
        grid_spec=pltpu.PrefetchScalarGridSpec(
            num_scalar_prefetch=1,
            grid=(STEPS,),
            in_specs=[whole((512, 256))] * 3 + weight_specs(width),
            out_specs=[pl.BlockSpec((128, width), lambda k, sel: (0, k))] * 8,
        ),
        out_shape=[jax.ShapeDtypeStruct((128, half), BF)] * 8,
        compiler_params=params(),
        cost_estimate=pl.CostEstimate(
            flops=2 * 512 * 768 * half, bytes_accessed=14 * 2**20, transcendentals=0
        ),
        name="results_other" if swapped else "results_own",
    )(sel, hid, d1, d2, *weights)


def weight_grads(core, own, other, hid, d1, d2):
    half = own[0].shape[1]
    width = half // STEPS
    place = lambda p, k, sel: (0, k, sel[p], 0, 0)
    up_spec = pl.BlockSpec((2, 1, 1, width, 128), place)
    down_spec = pl.BlockSpec((2, 128, width), lambda p, k, sel: (0, 0, 2 * k + sel[p]))
    first_rows = pl.BlockSpec((128, width), lambda p, k, sel: (0, jnp.where(p == 0, k, STEPS - 1)))
    last_rows = pl.BlockSpec((128, width), lambda p, k, sel: (0, jnp.where(p == 0, 0, k)))
    up_shape = jax.ShapeDtypeStruct((2, STEPS, 2, width, 128), BF)
    return pl.pallas_call(
        grads_kernel,
        grid_spec=pltpu.PrefetchScalarGridSpec(
            num_scalar_prefetch=1,
            grid=(2, STEPS),
            in_specs=[first_rows] * 8 + [last_rows] * 8 + [whole((512, 256))] * 3,
            out_specs=[up_spec, up_spec, down_spec],
        ),
        out_shape=[up_shape, up_shape, jax.ShapeDtypeStruct((2, 128, 2 * half), BF)],
        compiler_params=params(),
        cost_estimate=pl.CostEstimate(
            flops=4 * 512 * 768 * half, bytes_accessed=26 * 2**20, transcendentals=0
        ),
        name="weight_grads",
    )(jnp.stack([core, 1 - core]), *own, *other, hid, d1, d2)


def gate_weights(logits, slot_expert, chosen):
    experts = logits.shape[1]
    held = jnp.arange(experts, dtype=jnp.int32)[:, None] == slot_expert[None, :]
    picked = jnp.sum(jnp.where(held[None], logits[:, :, None], 0.0), axis=1)
    sig = jnp.where(chosen, jax.nn.sigmoid(picked), 0.0)
    return ROUTE_SCALE * sig / jnp.sum(sig, axis=1, keepdims=True)


def add(*values):
    total = values[0].astype(F32)
    for value in values[1:]:
        total = total + value.astype(F32)
    return total.astype(BF)


def per_device(tokens, cotangent, gate_logits, route_slot, slot_expert, w_gate, w_up, w_down):
    tok, wide = tokens.shape
    half = wide // 2
    width = half // STEPS
    slots = slot_expert.shape[0]
    z, core, y, x = (lax.axis_index(a) for a in AXES)
    line = y * NX + x
    own_sel, other_sel = core[None], (1 - core)[None]
    weights = (
        w_gate.reshape(2, STEPS, 2, width, 128),
        w_up.reshape(2, STEPS, 2, width, 128),
        w_down,
    )

    def mine(rows):
        return jnp.where(
            core == 0, rows.reshape(tok, STEPS, 2, width)[:, :, 0], rows.reshape(tok, STEPS, 2, width)[:, :, 1]
        ).reshape(tok, half)

    own = jnp.concatenate([mine(tokens), mine(cotangent)], axis=0)
    minus, plus, far = send(own, inner(1)), send(own, inner(-1)), send(own, inner(2))
    a = jnp.concatenate([own, plus], axis=0)
    b = jnp.concatenate([minus, far], axis=0)
    a_minus, b_plus = send(a, outer(1)), send(b, outer(-1))
    b_minus, a_plus = send(b, outer(1)), send(a, outer(-1))
    a_far, b_far = send(a_minus, outer(1)), send(b_plus, outer(-1))
    rows = [a, b, a_plus, b_plus, a_minus, b_minus, a_far, b_far]
    rows_other = [send(piece, other_core()) for piece in rows]

    chosen = jnp.any(
        route_slot[:, :, None] == jnp.arange(slots, dtype=jnp.int32)[None, None, :], axis=1
    )
    gate, pull_back = jax.vjp(lambda lg: gate_weights(lg, slot_expert, chosen), gate_logits)
    all_gates = lax.all_gather(gate, ("y", "x"), tiled=False).reshape(NY * NX, tok, slots)
    ring = jnp.array(RING, jnp.int32)
    out_y = ((y + ring) % NY)[:, None] * NX + ((x + ring) % NX)[None, :]
    out_x = ((y + ring) % NY)[None, :] * NX + ((x + ring) % NX)[:, None]
    order = jnp.where(core == 0, out_y, out_x).reshape(-1)
    pick_line = order[:, None] == jnp.arange(NY * NX, dtype=jnp.int32)[None, :]
    columns = jnp.stack([2 * line, 2 * line + 1, 2 * (line ^ (NY * NX // 2)) + 1])
    pick_slot = jnp.arange(slots, dtype=jnp.int32)[:, None] == columns[None, :]
    cols = jnp.sum(jnp.where(pick_slot[None, None], all_gates[..., None], 0.0), axis=2)
    cols = jnp.sum(jnp.where(pick_line[:, :, None, None], cols[None], 0.0), axis=1)
    cols = cols.reshape(NY * NX * tok, 3)
    gains = jnp.stack([cols[:, 0], cols[:, 1], cols[:, 1] + cols[:, 2]], axis=1)
    gains = jnp.pad(gains, ((0, 0), (0, 125)))

    sums = own_half(own_sel, rows, weights)
    h_out, d1_out, d2_out, h_grad, d1_grad, d2_grad, dots = other_half(
        other_sel, rows_other, weights, sums, gains
    )

    away = results(True, other_sel, h_out, d1_out, d2_out, weights, half)
    here = results(False, own_sel, h_out, d1_out, d2_out, weights, half)
    got = [None] * 8
    for piece in (6, 7, 3, 4, 2, 5, 0, 1):
        got[piece] = send(away[piece], other_core())
    part = [None] * 8
    for piece in (6, 7, 3, 4):
        part[piece] = add(here[piece], got[piece])
    from_a, from_b = send(part[6], outer(1)), send(part[7], outer(-1))
    b_early, a_early = send(part[3], outer(1)), send(part[4], outer(-1))
    a_late = send(add(here[2], got[2], from_a), outer(1))
    b_late = send(add(here[5], got[5], from_b), outer(-1))

    def final(piece, early, late):
        f = here[piece].astype(F32) + got[piece].astype(F32)
        return f + early.astype(F32) + late.astype(F32)

    sum_a, sum_b = final(0, a_early, a_late), final(1, b_early, b_late)
    keep = sum_a[:64]
    to_plus, to_minus, to_far = (v.astype(BF) for v in (sum_a[64:], sum_b[:64], sum_b[64:]))
    total = add(
        keep, send(to_plus, inner(1)), send(to_minus, inner(-1)), send(to_far, inner(2))
    )

    def block_for(by):
        return lax.dynamic_slice(total, (0, (z + by) % NZ * width), (64, width))

    last = add(
        block_for(0),
        send(block_for(1), along_z(1)),
        send(block_for(3), along_z(-1)),
        send(block_for(2), along_z(2)),
    )
    mixed, grad_tokens = last[:tok], last[tok:]

    grads = weight_grads(core, rows, rows_other, h_grad, d1_grad, d2_grad)

    dots = dots[:, :2].reshape(NY * NX, tok, 2)
    home = jnp.sum(jnp.where(pick_line[:, :, None, None], dots[:, None], 0.0), axis=0)
    home = lax.all_to_all(home, ("y", "x"), split_axis=0, concat_axis=0, tiled=True)
    home = jnp.transpose(home, (1, 0, 2)).reshape(tok, slots)
    home = lax.psum(home, ("z", "c"))
    grad_logits = pull_back(home)[0]
    return (
        mixed,
        grad_tokens,
        grad_logits,
        grads[0].reshape(w_gate.shape),
        grads[1].reshape(w_up.shape),
        grads[2],
    )


def solution(mesh):
    split = Mesh(mesh.devices.reshape(NZ, NC, NY, NX), AXES)
    local, group = ("y", "x"), ("z", "c")
    return jax.shard_map(
        per_device,
        mesh=split,
        in_specs=(
            P(local, None),
            P(local, None),
            P(local, None),
            P(local, None),
            P(),
            P(local, None, group),
            P(local, None, group),
            P(local, group, None),
        ),
        out_specs=(
            P(local, group),
            P(local, group),
            P(local, None),
            P(local, None, group),
            P(local, None, group),
            P(local, group, None),
        ),
        check_vma=False,
    )
```

```python
import functools

import jax
import jax.numpy as jnp
from jax import lax
from jax.experimental import pallas as pl
from jax.experimental.pallas import tpu as pltpu
from jax.sharding import Mesh
from jax.sharding import PartitionSpec as P

ROUTE_SCALE = 2.5
NZ, NC, NY, NX = 4, 2, 4, 4
AXES = ("z", "c", "y", "x")
STEPS = 4
BF, F32 = jnp.bfloat16, jnp.float32
NT = (((1,), (1,)), ((), ()))
TN = (((0,), (0,)), ((), ()))
RING = (0, 1, 3, 2)


def moves(step):
    pairs = []
    for z in range(NZ):
        for c in range(NC):
            for y in range(NY):
                for x in range(NX):
                    z2, c2, y2, x2 = step(z, c, y, x)
                    source = ((z * NC + c) * NY + y) * NX + x
                    target = ((z2 % NZ * NC + c2 % NC) * NY + y2 % NY) * NX + x2 % NX
                    pairs.append((source, target))
    return pairs


def outer(by):
    return moves(lambda z, c, y, x: (z, c, y + by, x) if c == 0 else (z, c, y, x + by))


def inner(by):
    return moves(lambda z, c, y, x: (z, c, y, x + by) if c == 0 else (z, c, y + by, x))


def along_z(by):
    return moves(lambda z, c, y, x: (z + by, c, y, x))


def other_core():
    return moves(lambda z, c, y, x: (z, c + 1, y, x))


def send(value, pairs):
    return lax.ppermute(value, AXES, pairs)


def joined(parts, axis=0):
    return jnp.concatenate(parts, axis=axis)


def rows_of(refs, blocks, second, first_piece=0):
    parts = []
    for outer_at, inner_at in blocks:
        row = 64 * (inner_at % 2) + (32 if second else 0)
        parts.append(refs[2 * outer_at + inner_at // 2 - first_piece][row : row + 32, :])
    return joined(parts)


def turned(blocks):
    return [(b, a) for a, b in blocks]


ALL = [(a, b) for a in range(4) for b in range(4)]
NEAR_OWN = [(a, b) for a in range(3) for b in range(4)]
FAR_OWN = [(3, b) for b in range(4)]
NEAR_OTHER = [(a, b) for a in range(4) for b in range(3)]
FAR_OTHER = [(a, 3) for a in range(4)]


def up_block(ref, k, half):
    return joined([ref[0, k, half], ref[1, k, half]], axis=1)


def down_block(ref, k, half, width):
    at = pl.multiple_of((2 * k + half) * width, 128)
    return ref[:, :, pl.ds(at, width)].reshape(-1, width)


def products(tok, cot, k, half, wg, wu, wd):
    first = jnp.dot(tok, up_block(wg, k, half), preferred_element_type=F32)
    second = jnp.dot(tok, up_block(wu, k, half), preferred_element_type=F32)
    down = down_block(wd, k, half, tok.shape[1])
    back = lax.dot_general(cot, down, NT, preferred_element_type=F32)
    return first, second, back


def pack_kernel(sel, tok, cot, packed):
    rows = tok.shape[0]
    packed[:rows] = tok[...]
    packed[rows:] = cot[...]


def pack_weights_kernel(sel, wg, wu, wd, wall, sems):
    away = sel[1]
    copies = []

    def copy(source, target):
        copies.append(pltpu.make_async_copy(source, target, sems.at[len(copies)]))
        copies[-1].start()

    for base, ref in ((0, wg), (56, wu)):
        for slot in range(2):
            for k in range(STEPS):
                copy(ref.at[slot, k, away], wall.at[pl.ds(base + (slot * STEPS + k) * 7, 7)])
    for k in range(STEPS):
        for q in range(7):
            at = pl.multiple_of((2 * k + away) * 896 + q * 128, 128)
            for slot in range(2):
                copy(wd.at[slot, :, pl.ds(at, 128)], wall.at[112 + 2 * (7 * k + q) + slot])
    for one in copies:
        one.wait()


def near_kernel(sel, *refs):
    own, other, (wg, wu, wd) = refs[:6], refs[6:12], refs[12:15]
    sums = refs[15:18]
    k = pl.program_id(0)
    a = products(
        rows_of(own, NEAR_OWN, False), rows_of(own, NEAR_OWN, True), k, sel[0], wg, wu, wd
    )
    there = turned(NEAR_OTHER)
    b = products(rows_of(other, there, False), rows_of(other, there, True), k, sel[1], wg, wu, wd)

    @pl.when(k == 0)
    def _():
        for ref in sums:
            ref[...] = jnp.zeros_like(ref)

    for ref, one, two in zip(sums, a, b):
        ref[:384] += one
        for out in range(4):
            ref[128 * out : 128 * out + 96] += two[96 * out : 96 * out + 96]


def far_kernel(sel, *refs):
    own, other, (wg, wu, wd) = refs[:2], refs[2:4], refs[4:7]
    start, gains = refs[7:10], refs[10]
    acts, acts_grad, dots = refs[11:14]
    sums = refs[14:17]
    width = own[0].shape[1] // STEPS
    a, b = None, None
    for k in range(STEPS):
        cols = pl.ds(k * width, width)
        mine = [ref.at[:, cols] for ref in own]
        there = [ref.at[:, cols] for ref in other]
        blocks = turned(FAR_OTHER)
        a_k = products(
            rows_of(mine, FAR_OWN, False, 6), rows_of(mine, FAR_OWN, True, 6), k, sel[0], wg, wu, wd
        )
        b_k = products(
            rows_of(there, blocks, False, 6), rows_of(there, blocks, True, 6), k, sel[1], wg, wu, wd
        )
        a = a_k if a is None else [u + v for u, v in zip(a, a_k)]
        b = b_k if b is None else [u + v for u, v in zip(b, b_k)]
    for ref, before, one, two in zip(sums, start, a, b):
        ref[...] = before[...]
        ref[384:] += one
        for out in range(4):
            ref[128 * out + 96 : 128 * out + 128] += two[32 * out : 32 * out + 32]
    lane = lax.broadcasted_iota(jnp.int32, dots.shape, 1)
    total = jnp.zeros(dots.shape, F32)
    for slot in range(2):
        units = slice(128 * slot, 128 * slot + 128)
        first, second, back = (ref[:, units] for ref in sums)
        mine = gains[:, slot : slot + 1]
        both = gains[:, 2 * slot : 2 * slot + 1]
        sig = jax.nn.sigmoid(first)
        silu = first * sig
        hidden = silu * second
        total = jnp.where(lane == slot, jnp.sum(hidden * back, axis=1, keepdims=True), total)
        d_first = back * second * sig * (1.0 + first * (1.0 - sig))
        d_second = back * silu
        for at, value in ((0, hidden), (256, d_first), (512, d_second)):
            units = slice(at + 128 * slot, at + 128 * slot + 128)
            acts[:, units] = (value * mine).astype(BF)
            acts_grad[:, units] = (value * both).astype(BF)
    dots[...] = total


def results_kernel(pieces, sel, acts, acts_other, wg, wu, wd, wall, *outs):
    half = sel[0]
    blocks = [(p // 2, 2 * (p % 2) + b) for p in pieces for b in range(2)]
    own = joined([acts[32 * (4 * a + b) : 32 * (4 * a + b) + 32, :] for a, b in blocks])
    other = joined([acts_other[32 * (4 * b + a) : 32 * (4 * b + a) + 32, :] for a, b in blocks])
    hidden = joined([own[:, :256], other[:, :256]], axis=1)
    grads = joined([own[:, 256:], other[:, 256:]], axis=1)
    width = outs[0].shape[1] // STEPS
    for k in range(STEPS):
        cols = slice(k * width, k * width + width)
        down = joined([wall[112 + 2 * (7 * k + q) : 114 + 2 * (7 * k + q)].reshape(256, 128) for q in range(7)], axis=1)
        down = joined([down_block(wd, k, half, width), down])
        up = [up_block(wg, k, half), up_block(wu, k, half)]
        for base in (0, 56):
            for slot in range(2):
                at = base + (slot * STEPS + k) * 7
                up.append(wall[at : at + 7].reshape(width, 128))
        out = jnp.dot(hidden, down, preferred_element_type=F32)
        grad = lax.dot_general(grads, joined(up, axis=1), NT, preferred_element_type=F32)
        for block in range(len(blocks)):
            here = slice(32 * block, 32 * block + 32)
            row = 64 * (block % 2)
            outs[block // 2][row : row + 32, cols] = out[here].astype(BF)
            outs[block // 2][row + 32 : row + 64, cols] = grad[here].astype(BF)


def grads_kernel(swapped, sel, *refs):
    rows, acts = refs[:8], refs[8]
    grad_gate, grad_up, grad_down = refs[-3:]
    blocks = turned(ALL) if swapped else ALL
    tok, cot = rows_of(rows, blocks, False), rows_of(rows, blocks, True)
    hid, d1, d2 = acts[:, :256], acts[:, 256:512], acts[:, 512:]
    gate = lax.dot_general(tok, d1, TN, preferred_element_type=F32).astype(BF)
    up = lax.dot_general(tok, d2, TN, preferred_element_type=F32).astype(BF)
    down = lax.dot_general(hid, cot, TN, preferred_element_type=F32).astype(BF)
    for slot in range(2):
        units = slice(128 * slot, 128 * slot + 128)
        grad_gate[slot, 0, 0] = gate[:, units]
        grad_up[slot, 0, 0] = up[:, units]
        grad_down[slot] = down[units]


VM = pl.BlockSpec(memory_space=pltpu.VMEM)
SM = pl.BlockSpec(memory_space=pltpu.SMEM)
HB = pl.BlockSpec(memory_space=pl.ANY)


def whole(shape):
    return pl.BlockSpec(shape, lambda *_: (0,) * len(shape))


def params(mib):
    return pltpu.CompilerParams(vmem_limit_bytes=mib * 2**20)


def cost(flops, mib):
    return pl.CostEstimate(flops=int(flops), bytes_accessed=int(mib * 2**20), transcendentals=0)


def shape(dims, dtype=BF):
    return jax.ShapeDtypeStruct(dims, dtype)


def pack(sel, tokens, cotangent):
    tok, wide = tokens.shape
    half = wide // 2
    width = half // STEPS
    spec = pl.BlockSpec((tok, width), lambda k, sel: (0, 2 * k + sel[0]))
    return pl.pallas_call(
        pack_kernel,
        grid_spec=pltpu.PrefetchScalarGridSpec(
            num_scalar_prefetch=1,
            grid=(STEPS,),
            in_specs=[spec, spec],
            out_specs=pl.BlockSpec((2 * tok, width), lambda k, sel: (0, k)),
        ),
        out_shape=shape((2 * tok, half)),
        compiler_params=params(4),
        cost_estimate=cost(0, 2),
        name="pack",
    )(sel, tokens, cotangent)


def pack_weights(sel, w_gate, w_up, w_down):
    views = [w.reshape(2, STEPS, 2, 7, 128, 128) for w in (w_gate, w_up)]
    return pl.pallas_call(
        pack_weights_kernel,
        in_specs=[SM, HB, HB, HB],
        out_specs=HB,
        out_shape=shape((168, 128, 128)),
        scratch_shapes=[pltpu.SemaphoreType.DMA((72,))],
        compiler_params=params(1),
        cost_estimate=cost(0, 11),
        name="pack_weights",
    )(sel, *views, w_down)


def near_sums(sel, own, other, weights):
    width = own[0].shape[1] // STEPS
    row_spec = pl.BlockSpec((128, width), lambda k, sel: (0, k))
    return pl.pallas_call(
        near_kernel,
        grid_spec=pltpu.PrefetchScalarGridSpec(
            num_scalar_prefetch=1,
            grid=(STEPS,),
            in_specs=[row_spec] * 12 + [VM] * 3,
            out_specs=[whole((512, 256))] * 3,
        ),
        out_shape=[shape((512, 256), F32)] * 3,
        compiler_params=params(20),
        cost_estimate=cost(4 * 384 * 768 * width * STEPS, 12),
        name="near_sums",
    )(sel, *own, *other, *weights)


def activations(sel, own, other, weights, sums, gains):
    return pl.pallas_call(
        far_kernel,
        in_specs=[SM] + [VM] * 11,
        out_specs=[VM] * 3,
        out_shape=[shape((512, 768)), shape((512, 768)), shape((512, 128), F32)],
        scratch_shapes=[pltpu.VMEM((512, 256), F32)] * 3,
        compiler_params=params(12),
        cost_estimate=cost(4 * 128 * 768 * own[0].shape[1], 12),
        name="activations",
    )(sel, *own, *other, *weights, *sums, gains)


def results(pieces, sel, acts, acts_other, weights, wall, half):
    return pl.pallas_call(
        functools.partial(results_kernel, pieces),
        in_specs=[SM] + [VM] * 6,
        out_specs=[VM] * len(pieces),
        out_shape=[shape((128, half))] * len(pieces),
        compiler_params=params(12),
        cost_estimate=cost(2 * 32 * 2 * len(pieces) * 1536 * half, 12),
        name="results",
    )(sel, acts, acts_other, *weights, wall)


def weight_grads(swapped, sel, rows, acts, before):
    half = rows[0].shape[1]
    width = half // STEPS
    at = 1 if swapped else 0
    up_spec = pl.BlockSpec((2, 1, 1, width, 128), lambda k, sel: (0, k, sel[at], 0, 0))
    down_spec = pl.BlockSpec((2, 128, width), lambda k, sel: (0, 0, 2 * k + sel[at]))
    row_spec = pl.BlockSpec((128, width), lambda k, sel: (0, k))
    up_shape = shape((2, STEPS, 2, width, 128))
    return pl.pallas_call(
        functools.partial(grads_kernel, swapped),
        grid_spec=pltpu.PrefetchScalarGridSpec(
            num_scalar_prefetch=1,
            grid=(STEPS,),
            in_specs=[row_spec] * 8 + [whole((512, 768))] + [HB] * len(before),
            out_specs=[up_spec, up_spec, down_spec],
        ),
        out_shape=[up_shape, up_shape, shape((2, 128, 2 * half))],
        input_output_aliases={10 + i: i for i in range(len(before))},
        compiler_params=params(20),
        cost_estimate=cost(2 * 512 * 768 * half, 13),
        name="weight_grads",
    )(sel, *rows, acts, *before)


def gate_weights(logits, slot_expert, chosen):
    experts = logits.shape[1]
    held = jnp.arange(experts, dtype=jnp.int32)[:, None] == slot_expert[None, :]
    picked = jnp.sum(jnp.where(held[None], logits[:, :, None], 0.0), axis=1)
    sig = jnp.where(chosen, jax.nn.sigmoid(picked), 0.0)
    return ROUTE_SCALE * sig / jnp.sum(sig, axis=1, keepdims=True)


def add(*values):
    total = values[0].astype(F32)
    for value in values[1:]:
        total = total + value.astype(F32)
    return total.astype(BF)


def per_device(tokens, cotangent, gate_logits, route_slot, slot_expert, w_gate, w_up, w_down):
    tok, wide = tokens.shape
    half = wide // 2
    width = half // STEPS
    slots = slot_expert.shape[0]
    z, core, y, x = (lax.axis_index(a) for a in AXES)
    sel = jnp.stack([core, 1 - core])
    weights = (
        w_gate.reshape(2, STEPS, 2, width, 128),
        w_up.reshape(2, STEPS, 2, width, 128),
        w_down,
    )

    own = pack(sel, tokens, cotangent)
    minus, plus, far = send(own, inner(1)), send(own, inner(-1)), send(own, inner(2))
    a = jnp.concatenate([own, plus], axis=0)
    b = jnp.concatenate([minus, far], axis=0)
    a_minus, b_plus = send(a, outer(1)), send(b, outer(-1))
    b_minus, a_plus = send(b, outer(1)), send(a, outer(-1))
    a_far, b_far = send(a_minus, outer(1)), send(b_plus, outer(-1))
    rows = [a, b, a_plus, b_plus, a_minus, b_minus, a_far, b_far]
    rows_other = [send(piece, other_core()) for piece in rows]
    wall = send(pack_weights(sel, w_gate, w_up, w_down), other_core())

    chosen = jnp.any(
        route_slot[:, :, None] == jnp.arange(slots, dtype=jnp.int32)[None, None, :], axis=1
    )
    gate, pull_back = jax.vjp(lambda lg: gate_weights(lg, slot_expert, chosen), gate_logits)
    lines = jnp.arange(NY * NX, dtype=jnp.int32)
    columns = jnp.stack([2 * lines, 2 * lines + 1, 2 * (lines ^ (NY * NX // 2)) + 1], axis=1)
    pick_slot = columns[:, :, None] == jnp.arange(slots, dtype=jnp.int32)[None, None, :]
    cols = jnp.sum(jnp.where(pick_slot[:, None], gate[None, :, None, :], 0.0), axis=3)
    cols = lax.all_to_all(cols, ("y", "x"), split_axis=0, concat_axis=0, tiled=True)
    ring = jnp.array(RING, jnp.int32)
    out_y = ((y + ring) % NY)[:, None] * NX + ((x + ring) % NX)[None, :]
    out_x = ((y + ring) % NY)[None, :] * NX + ((x + ring) % NX)[:, None]
    order = jnp.where(core == 0, out_y, out_x).reshape(-1)
    pick_line = order[:, None] == lines[None, :]
    cols = jnp.sum(jnp.where(pick_line[:, :, None, None], cols[None], 0.0), axis=1)
    cols = cols.reshape(NY * NX * tok, 3)
    gains = jnp.stack([cols[:, 0], cols[:, 1], cols[:, 1] + cols[:, 2]], axis=1)
    gains = jnp.pad(gains, ((0, 0), (0, 125)))

    sums = near_sums(sel, rows[:6], rows_other[:6], weights)
    acts, acts_grad, dots = activations(sel, rows[6:], rows_other[6:], weights, sums, gains)
    acts_other = send(acts, other_core())
    grads = weight_grads(False, sel, rows, acts_grad, [])
    acts_other, grads = lax.optimization_barrier((acts_other, grads))

    part = [None] * 8
    part[6], part[7], part[3], part[4] = results(
        (6, 7, 3, 4), sel, acts, acts_other, weights, wall, half
    )
    part[0], part[1], part[2], part[5] = results(
        (0, 1, 2, 5), sel, acts, acts_other, weights, wall, half
    )
    part[0], grads, dots = lax.optimization_barrier((part[0], grads, dots))
    from_a, from_b = send(part[6], outer(1)), send(part[7], outer(-1))
    b_early, a_early = send(part[3], outer(1)), send(part[4], outer(-1))
    a_late = send(add(part[2], from_a), outer(1))
    b_late = send(add(part[5], from_b), outer(-1))

    def final(piece, early, late):
        return part[piece].astype(F32) + early.astype(F32) + late.astype(F32)

    grads = weight_grads(True, sel, rows_other, acts_grad, grads)
    (a_late, b_late), grads = lax.optimization_barrier(((a_late, b_late), grads))
    sum_a, sum_b = final(0, a_early, a_late), final(1, b_early, b_late)
    keep = sum_a[:64]
    to_plus, to_minus, to_far = (v.astype(BF) for v in (sum_a[64:], sum_b[:64], sum_b[64:]))
    total = add(
        keep, send(to_plus, inner(1)), send(to_minus, inner(-1)), send(to_far, inner(2))
    )

    def block_for(by):
        return lax.dynamic_slice(total, (0, (z + by) % NZ * width), (64, width))

    last = add(
        block_for(0),
        send(block_for(1), along_z(1)),
        send(block_for(3), along_z(-1)),
        send(block_for(2), along_z(2)),
    )
    mixed, grad_tokens = last[:tok], last[tok:]

    dots = dots[:, :2].reshape(NY * NX, tok, 2)
    home = jnp.sum(jnp.where(pick_line[:, :, None, None], dots[:, None], 0.0), axis=0)
    home = lax.all_to_all(home, ("y", "x"), split_axis=0, concat_axis=0, tiled=True)
    home = jnp.transpose(home, (1, 0, 2)).reshape(tok, slots)
    home = home + send(home, other_core())
    home = home + send(home, along_z(1)) + send(home, along_z(-1)) + send(home, along_z(2))
    grad_logits = pull_back(home)[0]
    return (
        mixed,
        grad_tokens,
        grad_logits,
        grads[0].reshape(w_gate.shape),
        grads[1].reshape(w_up.shape),
        grads[2],
    )


def solution(mesh):
    split = Mesh(mesh.devices.reshape(NZ, NC, NY, NX), AXES)
    local, group = ("y", "x"), ("z", "c")
    return jax.shard_map(
        per_device,
        mesh=split,
        in_specs=(
            P(local, None),
            P(local, None),
            P(local, None),
            P(local, None),
            P(),
            P(local, None, group),
            P(local, None, group),
            P(local, group, None),
        ),
        out_specs=(
            P(local, group),
            P(local, group),
            P(local, None),
            P(local, None, group),
            P(local, None, group),
            P(local, group, None),
        ),
        check_vma=False,
    )
```

```python
import functools

import jax
import jax.numpy as jnp
from jax import lax
from jax.experimental import pallas as pl
from jax.experimental.pallas import tpu as pltpu
from jax.sharding import Mesh
from jax.sharding import PartitionSpec as P

ROUTE_SCALE = 2.5
NZ, NC, NY, NX = 4, 2, 4, 4
AXES = ("z", "c", "y", "x")
STEPS = 4
BF, F32 = jnp.bfloat16, jnp.float32
NT = (((1,), (1,)), ((), ()))
TN = (((0,), (0,)), ((), ()))
RING = (0, 1, 3, 2)


def moves(step):
    pairs = []
    for z in range(NZ):
        for c in range(NC):
            for y in range(NY):
                for x in range(NX):
                    z2, c2, y2, x2 = step(z, c, y, x)
                    source = ((z * NC + c) * NY + y) * NX + x
                    target = ((z2 % NZ * NC + c2 % NC) * NY + y2 % NY) * NX + x2 % NX
                    pairs.append((source, target))
    return pairs


def outer(by):
    return moves(lambda z, c, y, x: (z, c, y + by, x) if c == 0 else (z, c, y, x + by))


def inner(by):
    return moves(lambda z, c, y, x: (z, c, y, x + by) if c == 0 else (z, c, y + by, x))


def along_z(by):
    return moves(lambda z, c, y, x: (z + by, c, y, x))


def other_core():
    return moves(lambda z, c, y, x: (z, c + 1, y, x))


def send(value, pairs):
    return lax.ppermute(value, AXES, pairs)


def joined(parts, axis=0):
    return jnp.concatenate(parts, axis=axis)


def rows_of(refs, blocks, second):
    parts = []
    for outer_at, inner_at in blocks:
        ref, row = refs[outer_at] if outer_at < 3 else refs[-2 + inner_at // 2], 64 * inner_at
        if outer_at == 3:
            row = 64 * (inner_at % 2)
        if second:
            row += 32
        parts.append(ref[row : row + 32, :])
    return joined(parts)


def turned(blocks):
    return [(b, a) for a, b in blocks]


ALL = [(a, b) for a in range(4) for b in range(4)]
NEAR_OWN = [(a, b) for a in range(3) for b in range(4)]
FAR_OWN = [(3, b) for b in range(4)]
NEAR_OTHER = [(a, b) for a in range(4) for b in range(3)]
FAR_OTHER = [(a, 3) for a in range(4)]


def pair(first, second):
    return joined([first, second], axis=1)


def weight_block(wg, wu, wd):
    gate, up = (pair(ref[0, 0, 0], ref[1, 0, 0]) for ref in (wg, wu))
    return gate, up, wd[...].reshape(-1, wd.shape[2])


def products(tok, cot, gate, up, down):
    first = jnp.dot(tok, gate, preferred_element_type=F32)
    second = jnp.dot(tok, up, preferred_element_type=F32)
    back = lax.dot_general(cot, down, NT, preferred_element_type=F32)
    return first, second, back


def pack_kernel(sel, tok, cot, packed, sems):
    rows, width = tok.shape[0], tok.shape[1] // (2 * STEPS)
    copies = []
    for k in range(STEPS):
        at = pl.multiple_of((2 * k + sel[0]) * width, 128)
        for base, ref in enumerate((tok, cot)):
            target = packed.at[pl.ds(base * rows, rows), pl.ds(k * width, width)]
            copies.append(pltpu.make_async_copy(ref.at[:, pl.ds(at, width)], target, sems.at[len(copies)]))
            copies[-1].start()
    for one in copies:
        one.wait()


def pack_weights_kernel(sel, wg, wu, wd, wall, sems):
    away = sel[1]
    copies = []

    def copy(source, target):
        copies.append(pltpu.make_async_copy(source, target, sems.at[len(copies)]))
        copies[-1].start()

    for k in range(STEPS):
        for base, ref in ((0, wg), (14, wu)):
            for slot in range(2):
                copy(ref.at[slot, k, away], wall.at[k, pl.ds(base + 7 * slot, 7)])
        for q in range(7):
            at = pl.multiple_of((2 * k + away) * 896 + q * 128, 128)
            for slot in range(2):
                copy(wd.at[slot, :, pl.ds(at, 128)], wall.at[k, 28 + 2 * q + slot])
    for one in copies:
        one.wait()


def accumulate(sums, own, other, mine, theirs, own_blocks, other_blocks):
    there = turned(other_blocks)
    a = products(
        rows_of(own, own_blocks, False), rows_of(own, own_blocks, True), *weight_block(*mine)
    )
    b = products(rows_of(other, there, False), rows_of(other, there, True), *weight_block(*theirs))
    for ref, one, two in zip(sums, a, b):
        for blocks, value in ((own_blocks, one), (other_blocks, two)):
            for outer_at in sorted({o for o, _ in blocks}):
                inners = [i for o, i in blocks if o == outer_at]
                low = 32 * blocks.index((outer_at, inners[0]))
                to = 32 * (4 * outer_at + inners[0])
                ref[to : to + 32 * len(inners)] += value[low : low + 32 * len(inners)]


def near_kernel(sel, *refs):
    own, other, mine, theirs, sums = refs[:3], refs[3:6], refs[6:9], refs[9:12], refs[12:15]

    @pl.when(pl.program_id(0) == 0)
    def _():
        for ref in sums:
            ref[...] = jnp.zeros_like(ref)

    accumulate(sums, own, other, mine, theirs, NEAR_OWN, NEAR_OTHER)


def thirds(value):
    high = value.astype(BF).astype(F32)
    middle = (value - high).astype(BF).astype(F32)
    return high, middle, value - high - middle


def far_kernel(sel, *refs):
    own, other, mine, theirs = refs[:2], refs[2:4], refs[4:7], refs[7:10]
    start, gains = refs[10:13], refs[13]
    acts, acts_grad = refs[14:16]
    sums = refs[16:19]

    @pl.when(pl.program_id(0) == 0)
    def _():
        for ref, before in zip(sums, start):
            ref[...] = before[...]

    accumulate(sums, own, other, mine, theirs, FAR_OWN, FAR_OTHER)

    @pl.when(pl.program_id(0) == STEPS - 1)
    def _():
        finish(sums, gains, acts, acts_grad)


def finish(sums, gains, acts, acts_grad):
    lane = lax.broadcasted_iota(jnp.int32, (512, 128), 1)
    dots = jnp.zeros((512, 128), F32)
    for slot in range(2):
        units = slice(128 * slot, 128 * slot + 128)
        first, second, back = (ref[:, units] for ref in sums)
        mine = gains[:, slot : slot + 1]
        both = gains[:, 2 * slot : 2 * slot + 1]
        sig = jax.nn.sigmoid(first)
        silu = first * sig
        hidden = silu * second
        for at, part in enumerate(thirds(jnp.sum(hidden * back, axis=1, keepdims=True))):
            dots = jnp.where(lane == 2 * at + slot, part, dots)
        d_first = back * second * sig * (1.0 + first * (1.0 - sig))
        d_second = back * silu
        for at, value in ((0, hidden), (256, d_first), (512, d_second)):
            units = slice(at + 128 * slot, at + 128 * slot + 128)
            acts[:, units] = (value * mine).astype(BF)
            acts_grad[:, units] = (value * both).astype(BF)
    acts[:, 768:] = dots.astype(BF)


def results_kernel(pieces, sel, acts, acts_other, wg, wu, wd, wall, *outs):
    blocks = [(p // 2, 2 * (p % 2) + b) for group in pieces for p in group for b in range(2)]
    places = [(at, 64 * row) for at, group in enumerate(pieces) for row in range(2 * len(group))]
    own = joined([acts[32 * (4 * a + b) : 32 * (4 * a + b) + 32, :] for a, b in blocks])
    other = joined([acts_other[32 * (4 * b + a) : 32 * (4 * b + a) + 32, :] for a, b in blocks])
    hidden = pair(own[:, :256], other[:, :256])
    grads = pair(own[:, 256:768], other[:, 256:768])
    total = outs[0].shape[1] - 128
    width = total // STEPS
    k = pl.program_id(0)

    @pl.when(k == STEPS - 1)
    def _():
        lane = lax.broadcasted_iota(jnp.int32, (own.shape[0], 128), 1)
        dots = jnp.zeros((own.shape[0], 128), F32)
        last = own[:, 768:].astype(F32) + other[:, 768:].astype(F32)
        for slot in range(2):
            mine = jnp.sum(jnp.where((lane < 6) & (lane % 2 == slot), last, 0.0), axis=1, keepdims=True)
            for at, part in enumerate(thirds(mine)):
                dots = jnp.where(lane == 32 * at + 2 * sel[2] + slot, part, dots)
        for block, (at, row) in enumerate(places):
            outs[at][row : row + 32, total:] = dots[32 * block : 32 * block + 32].astype(BF)
            outs[at][row + 32 : row + 64, total:] = jnp.zeros((32, 128), BF)

    tiles = [
        joined([wall[0, 28 + 2 * q : 30 + 2 * q].reshape(256, 128) for q in range(7)], axis=1)
    ]
    gate, up, down = weight_block(wg, wu, wd)
    down = joined([down, *tiles])
    ups = [gate, up] + [wall[0, at : at + 7].reshape(width, 128) for at in (0, 7, 14, 21)]
    out = jnp.dot(hidden, down, preferred_element_type=F32)
    grad = lax.dot_general(grads, joined(ups, axis=1), NT, preferred_element_type=F32)
    cols = pl.ds(pl.multiple_of(k * width, 128), width)
    for block, (at, row) in enumerate(places):
        here = slice(32 * block, 32 * block + 32)
        outs[at][row : row + 32, cols] = out[here].astype(BF)
        outs[at][row + 32 : row + 64, cols] = grad[here].astype(BF)


def grads_kernel(swapped, sel, *refs):
    rows, acts = refs[:5], refs[5]
    grad_gate, grad_up, grad_down = refs[-3:]
    blocks = turned(ALL) if swapped else ALL
    tok, cot = rows_of(rows, blocks, False), rows_of(rows, blocks, True)
    hid, d1, d2 = acts[:, :256], acts[:, 256:512], acts[:, 512:768]
    gate = lax.dot_general(tok, d1, TN, preferred_element_type=F32).astype(BF)
    up = lax.dot_general(tok, d2, TN, preferred_element_type=F32).astype(BF)
    down = lax.dot_general(hid, cot, TN, preferred_element_type=F32).astype(BF)
    for slot in range(2):
        units = slice(128 * slot, 128 * slot + 128)
        grad_gate[slot, 0, 0] = gate[:, units]
        grad_up[slot, 0, 0] = up[:, units]
        grad_down[slot] = down[units]


VM = pl.BlockSpec(memory_space=pltpu.VMEM)
SM = pl.BlockSpec(memory_space=pltpu.SMEM)
HB = pl.BlockSpec(memory_space=pltpu.HBM)


def whole(shape):
    return pl.BlockSpec(shape, lambda *_: (0,) * len(shape))


def params(mib):
    return pltpu.CompilerParams(vmem_limit_bytes=mib * 2**20)


def cost(flops, mib):
    return pl.CostEstimate(flops=int(flops), bytes_accessed=int(mib * 2**20), transcendentals=0)


def shape(dims, dtype=BF):
    return jax.ShapeDtypeStruct(dims, dtype)


def pack(sel, tokens, cotangent):
    return pl.pallas_call(
        pack_kernel,
        in_specs=[SM, HB, HB],
        out_specs=HB,
        out_shape=shape((2 * tokens.shape[0], tokens.shape[1] // 2)),
        scratch_shapes=[pltpu.SemaphoreType.DMA((2 * STEPS,))],
        compiler_params=params(60),
        cost_estimate=cost(0, 2),
        name="pack",
    )(sel, tokens, cotangent)


def pack_weights(sel, w_gate, w_up, w_down):
    views = [w.reshape(2, STEPS, 2, 7, 128, 128) for w in (w_gate, w_up)]
    return pl.pallas_call(
        pack_weights_kernel,
        in_specs=[SM, HB, HB, HB],
        out_specs=HB,
        out_shape=shape((STEPS, 42, 128, 128)),
        scratch_shapes=[pltpu.SemaphoreType.DMA((72,))],
        compiler_params=params(60),
        cost_estimate=cost(0, 11),
        name="pack_weights",
    )(sel, *views, w_down)


def weight_specs(width, which):
    up_spec = pl.BlockSpec((2, 1, 1, width, 128), lambda k, sel: (0, k, sel[which], 0, 0))
    down_spec = pl.BlockSpec((2, 128, width), lambda k, sel: (0, 0, 2 * k + sel[which]))
    return [up_spec, up_spec, down_spec]


def row_specs(rows, width, first=0):
    return [pl.BlockSpec((r.shape[0], width), lambda k, sel: (0, first + k)) for r in rows]


def near_sums(sel, own, other, weights):
    width = own[0].shape[1] // STEPS
    return pl.pallas_call(
        near_kernel,
        grid_spec=pltpu.PrefetchScalarGridSpec(
            num_scalar_prefetch=1,
            grid=(STEPS,),
            in_specs=row_specs(own + other, width) + weight_specs(width, 0) + weight_specs(width, 1),
            out_specs=[whole((512, 256))] * 3,
        ),
        out_shape=[shape((512, 256), F32)] * 3,
        compiler_params=params(58),
        cost_estimate=cost(4 * 384 * 768 * width * STEPS, 22),
        name="near_sums",
    )(sel, *own, *other, *weights, *weights)


def activations(sel, own, other, weights, sums, gains):
    width = own[0].shape[1] // STEPS
    return pl.pallas_call(
        far_kernel,
        grid_spec=pltpu.PrefetchScalarGridSpec(
            num_scalar_prefetch=1,
            grid=(STEPS,),
            in_specs=row_specs(own + other, width)
            + weight_specs(width, 0)
            + weight_specs(width, 1)
            + [whole((512, 256))] * 3
            + [whole((512, 128))],
            out_specs=[whole((512, 896)), whole((512, 768))],
            scratch_shapes=[pltpu.VMEM((512, 256), F32)] * 3,
        ),
        out_shape=[shape((512, 896)), shape((512, 768))],
        compiler_params=params(58),
        cost_estimate=cost(4 * 128 * 768 * own[0].shape[1], 15),
        name="activations",
    )(sel, *own, *other, *weights, *weights, *sums, gains)


def results(pieces, sel, acts, acts_other, weights, wall, half):
    width = half // STEPS
    sizes = [128 * len(group) for group in pieces]
    return pl.pallas_call(
        functools.partial(results_kernel, pieces),
        grid_spec=pltpu.PrefetchScalarGridSpec(
            num_scalar_prefetch=1,
            grid=(STEPS,),
            in_specs=[whole((512, 896))] * 2
            + weight_specs(width, 0)
            + [pl.BlockSpec((1, 42, 128, 128), lambda k, sel: (k, 0, 0, 0))],
            out_specs=[VM] * len(sizes),
        ),
        out_shape=[shape((size, half + 128)) for size in sizes],
        compiler_params=params(60 - sum(sizes) // 128),
        cost_estimate=cost(sum(sizes) * 1536 * half, 12 + sum(sizes) // 128),
        name="results",
    )(sel, acts, acts_other, *weights, wall)


def weight_grads(swapped, first, count, sel, rows, acts, before):
    half = rows[0].shape[1]
    width = half // STEPS
    at = 1 if swapped else 0
    up_spec = pl.BlockSpec((2, 1, 1, width, 128), lambda k, sel: (0, first + k, sel[at], 0, 0))
    down_spec = pl.BlockSpec((2, 128, width), lambda k, sel: (0, 0, 2 * (first + k) + sel[at]))
    up_shape = shape((2, STEPS, 2, width, 128))
    return pl.pallas_call(
        functools.partial(grads_kernel, swapped),
        grid_spec=pltpu.PrefetchScalarGridSpec(
            num_scalar_prefetch=1,
            grid=(count,),
            in_specs=row_specs(rows, width, first) + [whole((512, 768))] + [HB] * len(before),
            out_specs=[up_spec, up_spec, down_spec],
        ),
        out_shape=[up_shape, up_shape, shape((2, 128, 2 * half))],
        input_output_aliases={2 + len(rows) + i: i for i in range(len(before))},
        compiler_params=params(56),
        cost_estimate=cost(2 * 512 * 768 * width * count, 3.5 * count),
        name="weight_grads",
    )(sel, *rows, acts, *before)


def gate_weights(logits, slot_expert, chosen):
    experts = logits.shape[1]
    held = jnp.arange(experts, dtype=jnp.int32)[:, None] == slot_expert[None, :]
    picked = jnp.sum(jnp.where(held[None], logits[:, :, None], 0.0), axis=1)
    sig = jnp.where(chosen, jax.nn.sigmoid(picked), 0.0)
    return ROUTE_SCALE * sig / jnp.sum(sig, axis=1, keepdims=True)


def add(*values):
    total = values[0].astype(F32)
    for value in values[1:]:
        total = total + value.astype(F32)
    return total.astype(BF)


def per_device(tokens, cotangent, gate_logits, route_slot, slot_expert, w_gate, w_up, w_down):
    tok, wide = tokens.shape
    half = wide // 2
    width = half // STEPS
    slots = slot_expert.shape[0]
    z, core, y, x = (lax.axis_index(a) for a in AXES)
    sel = jnp.stack([core, 1 - core, y * NX + x])
    weights = (
        w_gate.reshape(2, STEPS, 2, width, 128),
        w_up.reshape(2, STEPS, 2, width, 128),
        w_down,
    )
    own = pack(sel, tokens, cotangent)
    minus, plus, far = send(own, inner(1)), send(own, inner(-1)), send(own, inner(2))
    chosen = jnp.any(
        route_slot[:, :, None] == jnp.arange(slots, dtype=jnp.int32)[None, None, :], axis=1
    )
    gate, pull_back = jax.vjp(lambda lg: gate_weights(lg, slot_expert, chosen), gate_logits)
    lines = jnp.arange(NY * NX, dtype=jnp.int32)
    columns = jnp.stack([2 * lines, 2 * lines + 1, 2 * (lines ^ (NY * NX // 2)) + 1], axis=1)
    pick_slot = columns[:, :, None] == jnp.arange(slots, dtype=jnp.int32)[None, None, :]
    cols = jnp.sum(jnp.where(pick_slot[:, None], gate[None, :, None, :], 0.0), axis=3)
    stack = joined([own, plus, minus, far])
    stack, cols = lax.optimization_barrier((stack, cols))
    from_minus, from_plus = send(stack, outer(1)), send(stack, outer(-1))
    a_far, b_far = send(from_minus[:128], outer(1)), send(from_plus[128:], outer(-1))
    rows = [stack, from_plus, from_minus, a_far, b_far]
    rows_other = [send(piece, other_core()) for piece in rows]
    wall = send(pack_weights(sel, w_gate, w_up, w_down), other_core())

    cols = lax.all_to_all(cols, ("y", "x"), split_axis=0, concat_axis=0, tiled=True)
    ring = jnp.array(RING, jnp.int32)
    out_y = ((y + ring) % NY)[:, None] * NX + ((x + ring) % NX)[None, :]
    out_x = ((y + ring) % NY)[None, :] * NX + ((x + ring) % NX)[:, None]
    order = jnp.where(core == 0, out_y, out_x).reshape(-1)
    pick_line = order[:, None] == lines[None, :]
    cols = jnp.sum(jnp.where(pick_line[:, :, None, None], cols[None], 0.0), axis=1)
    cols = cols.reshape(NY * NX * tok, 3)
    gains = jnp.stack([cols[:, 0], cols[:, 1], cols[:, 1] + cols[:, 2]], axis=1)
    gains = jnp.pad(gains, ((0, 0), (0, 125)))

    sums = near_sums(sel, rows[:3], rows_other[:3], weights)
    acts, acts_grad = activations(sel, rows[3:], rows_other[3:], weights, sums, gains)
    acts_other = send(acts, other_core())
    grads = weight_grads(False, 0, 2, sel, rows, acts_grad, [])
    acts_other, grads = lax.optimization_barrier((acts_other, grads))

    far_a, far_b = results(((6,), (7,)), sel, acts, acts_other, weights, wall, half)
    own_a, own_b, to_plus, to_minus = results(
        ((0,), (1,), (2, 3), (5, 4)), sel, acts, acts_other, weights, wall, half
    )
    own_a, grads = lax.optimization_barrier((own_a, grads))
    from_a, from_b = send(far_a, outer(1)), send(far_b, outer(-1))
    to_plus = lax.dynamic_update_slice(to_plus, add(to_plus[:128], from_a), (0, 0))
    to_minus = lax.dynamic_update_slice(to_minus, add(to_minus[:128], from_b), (0, 0))
    got_p, got_m = send(to_plus, outer(1)), send(to_minus, outer(-1))
    grads = weight_grads(False, 2, 2, sel, rows, acts_grad, grads)
    grads = weight_grads(True, 0, 4, sel, rows_other, acts_grad, grads)
    (got_p, got_m), grads = lax.optimization_barrier(((got_p, got_m), grads))
    keep = (own_a[:64], got_p[:64], got_m[128:192])
    to_plus = add(own_a[64:], got_p[64:128], got_m[192:])
    to_minus = add(own_b[:64], got_p[128:192], got_m[:64])
    to_far = add(own_b[64:], got_p[192:], got_m[64:128])
    total = add(
        *keep, send(to_plus, inner(1)), send(to_minus, inner(-1)), send(to_far, inner(2))
    )

    def block_for(by):
        block = lax.dynamic_slice(total, (0, (z + by) % NZ * width), (2 * tok, width))
        return joined([block, total[:, half:]], axis=1)

    last = block_for(0).astype(F32)
    for by in (1, 3, 2):
        last = last + send(block_for(by), along_z(by)).astype(F32)
    mixed, grad_tokens = last[:tok, :width].astype(BF), last[tok:, :width].astype(BF)
    home = sum(last[:tok, width + at : width + at + slots] for at in (0, slots, 2 * slots))
    grad_logits = pull_back(home)[0]
    return (
        mixed,
        grad_tokens,
        grad_logits,
        grads[0].reshape(w_gate.shape),
        grads[1].reshape(w_up.shape),
        grads[2],
    )


def solution(mesh):
    split = Mesh(mesh.devices.reshape(NZ, NC, NY, NX), AXES)
    local, group = ("y", "x"), ("z", "c")
    return jax.shard_map(
        per_device,
        mesh=split,
        in_specs=(
            P(local, None),
            P(local, None),
            P(local, None),
            P(local, None),
            P(),
            P(local, None, group),
            P(local, None, group),
            P(local, group, None),
        ),
        out_specs=(
            P(local, group),
            P(local, group),
            P(local, None),
            P(local, None, group),
            P(local, None, group),
            P(local, group, None),
        ),
        check_vma=False,
    )
```

```python
import functools

import jax
import jax.numpy as jnp
from jax import lax
from jax.experimental import pallas as pl
from jax.experimental.pallas import tpu as pltpu
from jax.sharding import Mesh
from jax.sharding import PartitionSpec as P

ROUTE_SCALE = 2.5
NZ, NC, NY, NX = 4, 2, 4, 4
AXES = ("z", "c", "y", "x")
STEPS = 4
BF, F32 = jnp.bfloat16, jnp.float32
NT = (((1,), (1,)), ((), ()))
TN = (((0,), (0,)), ((), ()))
RING = (0, 1, 3, 2)


def moves(step):
    pairs = []
    for z in range(NZ):
        for c in range(NC):
            for y in range(NY):
                for x in range(NX):
                    z2, c2, y2, x2 = step(z, c, y, x)
                    source = ((z * NC + c) * NY + y) * NX + x
                    target = ((z2 % NZ * NC + c2 % NC) * NY + y2 % NY) * NX + x2 % NX
                    pairs.append((source, target))
    return pairs


def outer(by):
    return moves(lambda z, c, y, x: (z, c, y + by, x) if c == 0 else (z, c, y, x + by))


def inner(by):
    return moves(lambda z, c, y, x: (z, c, y, x + by) if c == 0 else (z, c, y + by, x))


def along_z(by):
    return moves(lambda z, c, y, x: (z + by, c, y, x))


def other_core():
    return moves(lambda z, c, y, x: (z, c + 1, y, x))


def send(value, pairs):
    return lax.ppermute(value, AXES, pairs)


def joined(parts, axis=0):
    return jnp.concatenate(parts, axis=axis)


def rows_of(refs, blocks, second):
    parts = []
    for outer_at, inner_at in blocks:
        row = 64 * (inner_at % 2) + (32 if second else 0)
        parts.append(refs[2 * outer_at + inner_at // 2][row : row + 32, :])
    return joined(parts)


def turned(blocks):
    return [(b, a) for a, b in blocks]


ALL = [(a, b) for a in range(4) for b in range(4)]
NEAR_OWN = [(a, b) for a in range(3) for b in range(4)]
FAR_OWN = [(3, b) for b in range(4)]
NEAR_OTHER = [(a, b) for a in range(4) for b in range(3)]
FAR_OTHER = [(a, 3) for a in range(4)]


def pair(first, second):
    return joined([first, second], axis=1)


def weight_block(wg, wu, wd):
    gate, up = (pair(ref[0, 0, 0], ref[1, 0, 0]) for ref in (wg, wu))
    return gate, up, wd[...].reshape(-1, wd.shape[2])


def up_block(ref, k, half):
    return pair(ref[0, k, half], ref[1, k, half])


def down_block(ref, k, half, width):
    at = pl.multiple_of((2 * k + half) * width, 128)
    return ref[:, :, pl.ds(at, width)].reshape(-1, width)


def products(tok, cot, gate, up, down):
    first = jnp.dot(tok, gate, preferred_element_type=F32)
    second = jnp.dot(tok, up, preferred_element_type=F32)
    back = lax.dot_general(cot, down, NT, preferred_element_type=F32)
    return first, second, back


def pack_kernel(sel, tok, cot, packed):
    rows = tok.shape[0]
    packed[:rows] = tok[...]
    packed[rows:] = cot[...]


def pack_weights_kernel(sel, wg, wu, wd, wall):
    for base, ref in ((0, wg), (14, wu)):
        for slot in range(2):
            at = base + 7 * slot
            wall[0, at : at + 7] = ref[slot, 0, 0].reshape(7, 128, 128)
    for q in range(7):
        wall[0, 28 + 2 * q : 30 + 2 * q] = wd[:, :, 128 * q : 128 * q + 128]


def multiply(sums, rows, weights, blocks, swapped):
    where = turned(blocks) if swapped else blocks
    parts = products(
        rows_of(rows, where, False), rows_of(rows, where, True), *weight_block(*weights)
    )
    for ref, part in zip(sums, parts):
        for outer_at in sorted({o for o, _ in blocks}):
            inners = [i for o, i in blocks if o == outer_at]
            low = 32 * blocks.index((outer_at, inners[0]))
            to = 32 * (4 * outer_at + inners[0])
            ref[to : to + 32 * len(inners)] += part[low : low + 32 * len(inners)]


def near_kernel(sel, *refs):
    own, other, mine, theirs, sums = refs[:6], refs[6:12], refs[12:15], refs[15:18], refs[18:21]

    @pl.when(pl.program_id(0) == 0)
    def _():
        for ref in sums:
            ref[...] = jnp.zeros_like(ref)

    multiply(sums, own, mine, NEAR_OWN, False)
    multiply(sums, other, theirs, NEAR_OTHER, True)


def far_own_kernel(sel, *refs):
    own, mine, start, sums = dict(zip((6, 7), refs)), refs[2:5], refs[5:8], refs[8:11]

    @pl.when(pl.program_id(0) == 0)
    def _():
        for ref, before in zip(sums, start):
            ref[...] = before[...]

    multiply(sums, own, mine, FAR_OWN, False)


def thirds(value):
    high = value.astype(BF).astype(F32)
    middle = (value - high).astype(BF).astype(F32)
    return high, middle, value - high - middle


def far_other_kernel(sel, *refs):
    other, theirs, start, gains = dict(zip((6, 7), refs)), refs[2:5], refs[5:8], refs[8]
    acts, acts_grad = refs[9:11]
    sums = refs[11:14]

    @pl.when(pl.program_id(0) == 0)
    def _():
        for ref, before in zip(sums, start):
            ref[...] = before[...]

    multiply(sums, other, theirs, FAR_OTHER, True)

    @pl.when(pl.program_id(0) == STEPS - 1)
    def _():
        finish(sums, gains, acts, acts_grad)


def finish(sums, gains, acts, acts_grad):
    lane = lax.broadcasted_iota(jnp.int32, (512, 128), 1)
    dots = jnp.zeros((512, 128), F32)
    for slot in range(2):
        units = slice(128 * slot, 128 * slot + 128)
        first, second, back = (ref[:, units] for ref in sums)
        mine = gains[:, slot : slot + 1]
        both = gains[:, 2 * slot : 2 * slot + 1]
        sig = jax.nn.sigmoid(first)
        silu = first * sig
        hidden = silu * second
        for at, part in enumerate(thirds(jnp.sum(hidden * back, axis=1, keepdims=True))):
            dots = jnp.where(lane == 2 * at + slot, part, dots)
        d_first = back * second * sig * (1.0 + first * (1.0 - sig))
        d_second = back * silu
        for at, value in ((0, hidden), (256, d_first), (512, d_second)):
            units = slice(at + 128 * slot, at + 128 * slot + 128)
            acts[:, units] = (value * mine).astype(BF)
            acts_grad[:, units] = (value * both).astype(BF)
    acts[:, 768:] = dots.astype(BF)


def results_kernel(pieces, sel, acts, acts_other, wg, wu, wd, wall, *outs):
    half = sel[0]
    blocks = [(p // 2, 2 * (p % 2) + b) for group in pieces for p in group for b in range(2)]
    places = [(at, 64 * row) for at, group in enumerate(pieces) for row in range(2 * len(group))]
    own = joined([acts[32 * (4 * a + b) : 32 * (4 * a + b) + 32, :] for a, b in blocks])
    other = joined([acts_other[32 * (4 * b + a) : 32 * (4 * b + a) + 32, :] for a, b in blocks])
    hidden = pair(own[:, :256], other[:, :256])
    grads = pair(own[:, 256:768], other[:, 256:768])
    total = outs[0].shape[1] - 128
    width = total // STEPS
    lane = lax.broadcasted_iota(jnp.int32, (own.shape[0], 128), 1)
    dots = jnp.zeros((own.shape[0], 128), F32)
    last = own[:, 768:].astype(F32) + other[:, 768:].astype(F32)
    for slot in range(2):
        mine = jnp.sum(jnp.where((lane < 6) & (lane % 2 == slot), last, 0.0), axis=1, keepdims=True)
        for at, part in enumerate(thirds(mine)):
            dots = jnp.where(lane == 32 * at + 2 * sel[2] + slot, part, dots)
    for block, (at, row) in enumerate(places):
        outs[at][row : row + 32, total:] = dots[32 * block : 32 * block + 32].astype(BF)
        outs[at][row + 32 : row + 64, total:] = jnp.zeros((32, 128), BF)
    for k in range(STEPS):
        cols = slice(k * width, k * width + width)
        down = joined([wall[k, 28 + 2 * q : 30 + 2 * q].reshape(256, 128) for q in range(7)], axis=1)
        down = joined([down_block(wd, k, half, width), down])
        up = [up_block(wg, k, half), up_block(wu, k, half)]
        up += [wall[k, at : at + 7].reshape(width, 128) for at in (0, 7, 14, 21)]
        out = jnp.dot(hidden, down, preferred_element_type=F32)
        grad = lax.dot_general(grads, joined(up, axis=1), NT, preferred_element_type=F32)
        for block, (at, row) in enumerate(places):
            here = slice(32 * block, 32 * block + 32)
            outs[at][row : row + 32, cols] = out[here].astype(BF)
            outs[at][row + 32 : row + 64, cols] = grad[here].astype(BF)


def grads_kernel(swapped, sel, *refs):
    rows, acts = refs[:8], refs[8]
    grad_gate, grad_up, grad_down = refs[-3:]
    blocks = turned(ALL) if swapped else ALL
    tok, cot = rows_of(rows, blocks, False), rows_of(rows, blocks, True)
    hid, d1, d2 = acts[:, :256], acts[:, 256:512], acts[:, 512:768]
    gate = lax.dot_general(tok, d1, TN, preferred_element_type=F32).astype(BF)
    up = lax.dot_general(tok, d2, TN, preferred_element_type=F32).astype(BF)
    down = lax.dot_general(hid, cot, TN, preferred_element_type=F32).astype(BF)
    for slot in range(2):
        units = slice(128 * slot, 128 * slot + 128)
        grad_gate[slot, 0, 0] = gate[:, units]
        grad_up[slot, 0, 0] = up[:, units]
        grad_down[slot] = down[units]


VM = pl.BlockSpec(memory_space=pltpu.VMEM)
SM = pl.BlockSpec(memory_space=pltpu.SMEM)
HB = pl.BlockSpec(memory_space=pltpu.HBM)


def whole(shape):
    return pl.BlockSpec(shape, lambda *_: (0,) * len(shape))


def params(mib):
    return pltpu.CompilerParams(vmem_limit_bytes=mib * 2**20)


def cost(flops, mib):
    return pl.CostEstimate(flops=int(flops), bytes_accessed=int(mib * 2**20), transcendentals=0)


def shape(dims, dtype=BF):
    return jax.ShapeDtypeStruct(dims, dtype)


def pack(sel, tokens, cotangent):
    tok, wide = tokens.shape
    width = wide // (2 * STEPS)
    spec = pl.BlockSpec((tok, width), lambda k, sel: (0, 2 * k + sel[0]))
    return pl.pallas_call(
        pack_kernel,
        grid_spec=pltpu.PrefetchScalarGridSpec(
            num_scalar_prefetch=1,
            grid=(STEPS,),
            in_specs=[spec, spec],
            out_specs=pl.BlockSpec((2 * tok, width), lambda k, sel: (0, k)),
        ),
        out_shape=shape((2 * tok, wide // 2)),
        compiler_params=params(60),
        cost_estimate=cost(0, 2),
        name="pack",
    )(sel, tokens, cotangent)


def pack_weights(sel, weights):
    width = weights[0].shape[3]
    up_spec = pl.BlockSpec((2, 1, 1, width, 128), lambda k, sel: (0, k, sel[1], 0, 0))
    down_spec = pl.BlockSpec((2, 128, width), lambda k, sel: (0, 0, 2 * k + sel[1]))
    return pl.pallas_call(
        pack_weights_kernel,
        grid_spec=pltpu.PrefetchScalarGridSpec(
            num_scalar_prefetch=1,
            grid=(STEPS,),
            in_specs=[up_spec, up_spec, down_spec],
            out_specs=pl.BlockSpec((1, 42, 128, 128), lambda k, sel: (k, 0, 0, 0)),
        ),
        out_shape=shape((STEPS, 42, 128, 128)),
        compiler_params=params(60),
        cost_estimate=cost(0, 0.1),
        name="pack_weights",
    )(sel, *weights)


def weight_specs(width, which):
    up_spec = pl.BlockSpec((2, 1, 1, width, 128), lambda k, sel: (0, k, sel[which], 0, 0))
    down_spec = pl.BlockSpec((2, 128, width), lambda k, sel: (0, 0, 2 * k + sel[which]))
    return [up_spec, up_spec, down_spec]


def row_specs(rows, width, first=0):
    return [pl.BlockSpec((r.shape[0], width), lambda k, sel: (0, first + k)) for r in rows]


def near_sums(sel, own, other, weights):
    width = own[0].shape[1] // STEPS
    return pl.pallas_call(
        near_kernel,
        grid_spec=pltpu.PrefetchScalarGridSpec(
            num_scalar_prefetch=1,
            grid=(STEPS,),
            in_specs=row_specs(own + other, width) + weight_specs(width, 0) + weight_specs(width, 1),
            out_specs=[whole((512, 256))] * 3,
        ),
        out_shape=[shape((512, 256), F32)] * 3,
        compiler_params=params(58),
        cost_estimate=cost(0, 0.1),
        name="near_sums",
    )(sel, *own, *other, *weights, *weights)


def far_sums(sel, own, weights, sums):
    width = own[0].shape[1] // STEPS
    return pl.pallas_call(
        far_own_kernel,
        grid_spec=pltpu.PrefetchScalarGridSpec(
            num_scalar_prefetch=1,
            grid=(STEPS,),
            in_specs=row_specs(own, width) + weight_specs(width, 0) + [whole((512, 256))] * 3,
            out_specs=[whole((512, 256))] * 3,
        ),
        out_shape=[shape((512, 256), F32)] * 3,
        compiler_params=params(50),
        cost_estimate=cost(2 * 128 * 768 * width * STEPS, 10),
        name="far_sums",
    )(sel, *own, *weights, *sums)


def activations(sel, other, weights, sums, gains):
    width = other[0].shape[1] // STEPS
    return pl.pallas_call(
        far_other_kernel,
        grid_spec=pltpu.PrefetchScalarGridSpec(
            num_scalar_prefetch=1,
            grid=(STEPS,),
            in_specs=row_specs(other, width)
            + weight_specs(width, 1)
            + [whole((512, 256))] * 3
            + [whole((512, 128))],
            out_specs=[whole((512, 896)), whole((512, 768))],
            scratch_shapes=[pltpu.VMEM((512, 256), F32)] * 3,
        ),
        out_shape=[shape((512, 896)), shape((512, 768))],
        compiler_params=params(50),
        cost_estimate=cost(2 * 128 * 768 * width * STEPS, 10),
        name="activations",
    )(sel, *other, *weights, *sums, gains)


def results(pieces, sel, acts, acts_other, weights, wall, half):
    return pl.pallas_call(
        functools.partial(results_kernel, pieces),
        in_specs=[SM] + [VM] * 6,
        out_specs=[VM] * len(pieces),
        out_shape=[shape((128 * len(group), half + 128)) for group in pieces],
        compiler_params=params(12),
        cost_estimate=cost(2 * 64 * sum(map(len, pieces)) * 1536 * half, 12),
        name="results",
    )(sel, acts, acts_other, *weights, wall)


def weight_grads(swapped, first, count, sel, rows, acts, before):
    half = rows[0].shape[1]
    width = half // STEPS
    at = 1 if swapped else 0
    up_spec = pl.BlockSpec((2, 1, 1, width, 128), lambda k, sel: (0, first + k, sel[at], 0, 0))
    down_spec = pl.BlockSpec((2, 128, width), lambda k, sel: (0, 0, 2 * (first + k) + sel[at]))
    up_shape = shape((2, STEPS, 2, width, 128))
    return pl.pallas_call(
        functools.partial(grads_kernel, swapped),
        grid_spec=pltpu.PrefetchScalarGridSpec(
            num_scalar_prefetch=1,
            grid=(count,),
            in_specs=row_specs(rows, width, first) + [whole((512, 768))] + [HB] * len(before),
            out_specs=[up_spec, up_spec, down_spec],
        ),
        out_shape=[up_shape, up_shape, shape((2, 128, 2 * half))],
        input_output_aliases={2 + len(rows) + i: i for i in range(len(before))},
        compiler_params=params(20),
        cost_estimate=cost(2 * 512 * 768 * width * count, 3.5 * count),
        name="weight_grads",
    )(sel, *rows, acts, *before)


def gate_weights(logits, slot_expert, chosen):
    experts = logits.shape[1]
    held = jnp.arange(experts, dtype=jnp.int32)[:, None] == slot_expert[None, :]
    picked = jnp.sum(jnp.where(held[None], logits[:, :, None], 0.0), axis=1)
    sig = jnp.where(chosen, jax.nn.sigmoid(picked), 0.0)
    return ROUTE_SCALE * sig / jnp.sum(sig, axis=1, keepdims=True)


def add(*values):
    total = values[0].astype(F32)
    for value in values[1:]:
        total = total + value.astype(F32)
    return total.astype(BF)


def per_device(tokens, cotangent, gate_logits, route_slot, slot_expert, w_gate, w_up, w_down):
    tok, wide = tokens.shape
    half = wide // 2
    width = half // STEPS
    slots = slot_expert.shape[0]
    z, core, y, x = (lax.axis_index(a) for a in AXES)
    sel = jnp.stack([core, 1 - core, y * NX + x])
    weights = (
        w_gate.reshape(2, STEPS, 2, width, 128),
        w_up.reshape(2, STEPS, 2, width, 128),
        w_down,
    )
    own = pack(sel, tokens, cotangent)
    minus, plus, far = send(own, inner(1)), send(own, inner(-1)), send(own, inner(2))
    chosen = jnp.any(
        route_slot[:, :, None] == jnp.arange(slots, dtype=jnp.int32)[None, None, :], axis=1
    )
    gate, pull_back = jax.vjp(lambda lg: gate_weights(lg, slot_expert, chosen), gate_logits)
    lines = jnp.arange(NY * NX, dtype=jnp.int32)
    columns = jnp.stack([2 * lines, 2 * lines + 1, 2 * (lines ^ (NY * NX // 2)) + 1], axis=1)
    pick_slot = columns[:, :, None] == jnp.arange(slots, dtype=jnp.int32)[None, None, :]
    cols = jnp.sum(jnp.where(pick_slot[:, None], gate[None, :, None, :], 0.0), axis=3)
    a, b = joined([own, plus]), joined([minus, far])
    a, b, cols = lax.optimization_barrier((a, b, cols))
    cols = lax.all_to_all(cols, ("y", "x"), split_axis=0, concat_axis=0, tiled=True)
    ring = jnp.array(RING, jnp.int32)
    out_y = ((y + ring) % NY)[:, None] * NX + ((x + ring) % NX)[None, :]
    out_x = ((y + ring) % NY)[None, :] * NX + ((x + ring) % NX)[:, None]
    order = jnp.where(core == 0, out_y, out_x).reshape(-1)
    pick_line = order[:, None] == lines[None, :]
    cols = jnp.sum(jnp.where(pick_line[:, :, None, None], cols[None], 0.0), axis=1)
    cols = cols.reshape(NY * NX * tok, 3)
    gains = jnp.stack([cols[:, 0], cols[:, 1], cols[:, 1] + cols[:, 2]], axis=1)
    gains = jnp.pad(gains, ((0, 0), (0, 125)))

    a_minus, b_plus = send(a, outer(1)), send(b, outer(-1))
    b_minus, a_plus = send(b, outer(1)), send(a, outer(-1))
    a_far, b_far = send(a_minus, outer(1)), send(b_plus, outer(-1))
    wall = send(pack_weights(sel, weights), other_core())

    near = [a, b, a_plus, b_plus, a_minus, b_minus]
    near_other = [send(piece, other_core()) for piece in near]
    sums = near_sums(sel, near, near_other, weights)
    (a_on, b_on), sums, gains, wall = lax.optimization_barrier(((a_far, b_far), sums, gains, wall))
    far_rows, far_other = [a_far, b_far], [send(a_on, other_core()), send(b_on, other_core())]
    rows, rows_other = near + far_rows, near_other + far_other
    sums = far_sums(sel, far_rows, weights, sums)
    acts, acts_grad = activations(sel, far_other, weights, sums, gains)
    acts_other = send(acts, other_core())
    grads = weight_grads(False, 0, 2, sel, rows, acts_grad, [])
    acts_other, grads = lax.optimization_barrier((acts_other, grads))

    far_a, far_b = results(((6,), (7,)), sel, acts, acts_other, weights, wall, half)
    own_a, own_b, to_plus, to_minus = results(
        ((0,), (1,), (2, 3), (5, 4)), sel, acts, acts_other, weights, wall, half
    )
    own_a, grads = lax.optimization_barrier((own_a, grads))
    from_a, from_b = send(far_a, outer(1)), send(far_b, outer(-1))
    to_plus = lax.dynamic_update_slice(to_plus, add(to_plus[:128], from_a), (0, 0))
    to_minus = lax.dynamic_update_slice(to_minus, add(to_minus[:128], from_b), (0, 0))
    got_p, got_m = send(to_plus, outer(1)), send(to_minus, outer(-1))
    grads = weight_grads(False, 2, 2, sel, rows, acts_grad, grads)
    grads = weight_grads(True, 0, 4, sel, rows_other, acts_grad, grads)
    (got_p, got_m), grads = lax.optimization_barrier(((got_p, got_m), grads))
    keep = (own_a[:64], got_p[:64], got_m[128:192])
    to_plus = add(own_a[64:], got_p[64:128], got_m[192:])
    to_minus = add(own_b[:64], got_p[128:192], got_m[:64])
    to_far = add(own_b[64:], got_p[192:], got_m[64:128])
    total = add(
        *keep, send(to_plus, inner(1)), send(to_minus, inner(-1)), send(to_far, inner(2))
    )

    def block_for(by):
        block = lax.dynamic_slice(total, (0, (z + by) % NZ * width), (2 * tok, width))
        return joined([block, total[:, half:]], axis=1)

    last = block_for(0).astype(F32)
    for by in (1, 3, 2):
        last = last + send(block_for(by), along_z(by)).astype(F32)
    mixed, grad_tokens = last[:tok, :width].astype(BF), last[tok:, :width].astype(BF)
    home = sum(last[:tok, width + at : width + at + slots] for at in (0, slots, 2 * slots))
    grad_logits = pull_back(home)[0]
    return (
        mixed,
        grad_tokens,
        grad_logits,
        grads[0].reshape(w_gate.shape),
        grads[1].reshape(w_up.shape),
        grads[2],
    )


def solution(mesh):
    split = Mesh(mesh.devices.reshape(NZ, NC, NY, NX), AXES)
    local, group = ("y", "x"), ("z", "c")
    return jax.shard_map(
        per_device,
        mesh=split,
        in_specs=(
            P(local, None),
            P(local, None),
            P(local, None),
            P(local, None),
            P(),
            P(local, None, group),
            P(local, None, group),
            P(local, group, None),
        ),
        out_specs=(
            P(local, group),
            P(local, group),
            P(local, None),
            P(local, None, group),
            P(local, None, group),
            P(local, group, None),
        ),
        check_vma=False,
    )
```

```python
import functools

import jax
import jax.numpy as jnp
from jax import lax
from jax.experimental import pallas as pl
from jax.experimental.pallas import tpu as pltpu
from jax.sharding import Mesh
from jax.sharding import PartitionSpec as P

ROUTE_SCALE = 2.5
TOP = 8
ROUTE = 3 * 24
NZ, NC, NY, NX = 4, 2, 4, 4
AXES = ("z", "c", "y", "x")
STEPS = 4
BF, F32 = jnp.bfloat16, jnp.float32
NT = (((1,), (1,)), ((), ()))
TN = (((0,), (0,)), ((), ()))
RING = (0, 1, 3, 2)


def moves(step):
    pairs = []
    for z in range(NZ):
        for c in range(NC):
            for y in range(NY):
                for x in range(NX):
                    z2, c2, y2, x2 = step(z, c, y, x)
                    source = ((z * NC + c) * NY + y) * NX + x
                    target = ((z2 % NZ * NC + c2 % NC) * NY + y2 % NY) * NX + x2 % NX
                    pairs.append((source, target))
    return pairs


def outer(by):
    return moves(lambda z, c, y, x: (z, c, y + by, x) if c == 0 else (z, c, y, x + by))


def inner(by):
    return moves(lambda z, c, y, x: (z, c, y, x + by) if c == 0 else (z, c, y + by, x))


def along_z(by):
    return moves(lambda z, c, y, x: (z + by, c, y, x))


def other_core():
    return moves(lambda z, c, y, x: (z, c + 1, y, x))


def send(value, pairs):
    return lax.ppermute(value, AXES, pairs)


def joined(parts, axis=0):
    return jnp.concatenate(parts, axis=axis)


def rows_of(refs, blocks, second):
    parts = []
    for outer_at, inner_at in blocks:
        row = 64 * (inner_at % 2) + (32 if second else 0)
        parts.append(refs[2 * outer_at + inner_at // 2][row : row + 32, :])
    return joined(parts)


def turned(blocks):
    return [(b, a) for a, b in blocks]


ALL = [(a, b) for a in range(4) for b in range(4)]
NEAR_OWN = [(a, b) for a in range(3) for b in range(4)]
FAR_OWN = [(3, b) for b in range(4)]
NEAR_OTHER = [(a, b) for a in range(4) for b in range(3)]
FAR_OTHER = [(a, 3) for a in range(4)]


def pair(first, second):
    return joined([first, second], axis=1)


def weight_block(wg, wu, wd):
    gate, up = (pair(ref[0, 0, 0], ref[1, 0, 0]) for ref in (wg, wu))
    return gate, up, wd[...].reshape(-1, wd.shape[2])


def up_block(ref, k, half):
    return pair(ref[0, k, half], ref[1, k, half])


def down_block(ref, k, half, width):
    at = pl.multiple_of((2 * k + half) * width, 128)
    return ref[:, :, pl.ds(at, width)].reshape(-1, width)


def products(tok, cot, gate, up, down):
    first = jnp.dot(tok, gate, preferred_element_type=F32)
    second = jnp.dot(tok, up, preferred_element_type=F32)
    back = lax.dot_general(cot, down, NT, preferred_element_type=F32)
    return first, second, back


def pack_kernel(sel, tok, cot, extra, packed, sems):
    rows, half = extra.shape[0], packed.shape[1] - 128
    width = half // STEPS
    copies = []
    for k in range(STEPS):
        at = pl.multiple_of((2 * k + sel[0]) * width, 128)
        for base, ref in enumerate((tok, cot)):
            target = packed.at[pl.ds(base * rows, rows), pl.ds(k * width, width)]
            copies.append(
                pltpu.make_async_copy(ref.at[:, pl.ds(at, width)], target, sems.at[len(copies)])
            )
            copies[-1].start()
    packed[:rows, half:] = extra[...]
    packed[rows:, half:] = jnp.zeros_like(extra)
    for one in copies:
        one.wait()


def pack_weights_kernel(sel, wg, wu, wd, wall):
    for base, ref in ((0, wg), (14, wu)):
        for slot in range(2):
            at = base + 7 * slot
            wall[0, at : at + 7] = ref[slot, 0, 0].reshape(7, 128, 128)
    for q in range(7):
        wall[0, 28 + 2 * q : 30 + 2 * q] = wd[:, :, 128 * q : 128 * q + 128]


def multiply(sums, rows, weights, blocks, swapped):
    where = turned(blocks) if swapped else blocks
    parts = products(
        rows_of(rows, where, False), rows_of(rows, where, True), *weight_block(*weights)
    )
    for ref, part in zip(sums, parts):
        for outer_at in sorted({o for o, _ in blocks}):
            inners = [i for o, i in blocks if o == outer_at]
            low = 32 * blocks.index((outer_at, inners[0]))
            to = 32 * (4 * outer_at + inners[0])
            ref[to : to + 32 * len(inners)] += part[low : low + 32 * len(inners)]


def near_kernel(sel, *refs):
    own, other, mine, theirs, sums = refs[:6], refs[6:12], refs[12:15], refs[15:18], refs[18:21]

    @pl.when(pl.program_id(0) == 0)
    def _():
        for ref in sums:
            ref[...] = jnp.zeros_like(ref)

    multiply(sums, own, mine, NEAR_OWN, False)
    multiply(sums, other, theirs, NEAR_OTHER, True)


def line_weights(extra, held, sel, gains):
    rows = rows_of(extra, ALL, False)
    picked = jnp.dot(rows, held[...], preferred_element_type=F32)
    lane = lax.broadcasted_iota(jnp.int32, picked.shape, 1)
    slot = lane.astype(F32)
    chosen = slot < 0
    for at in range(TOP):
        chosen = chosen | (slot == rows[:, ROUTE + at : ROUTE + at + 1].astype(F32))
    sig = jnp.where(chosen, jax.nn.sigmoid(picked), 0.0)
    weight = ROUTE_SCALE * sig / jnp.sum(sig, axis=1, keepdims=True)

    def column(at):
        return jnp.sum(jnp.where(lane == at, weight, 0.0), axis=1, keepdims=True)

    cold, hot, partner = column(2 * sel[2]), column(2 * sel[2] + 1), column(sel[3])
    gains[...] = jnp.where(lane == 0, cold, jnp.where(lane == 1, hot, hot + partner))


def thirds(value):
    high = value.astype(BF).astype(F32)
    middle = (value - high).astype(BF).astype(F32)
    return high, middle, value - high - middle


def far_kernel(sel, *refs):
    own, other = dict(zip((6, 7), refs)), dict(zip((6, 7), refs[2:]))
    mine, theirs, start, extra, held = refs[4:7], refs[7:10], refs[10:13], refs[13:21], refs[21]
    acts, acts_grad = refs[22:24]
    sums, gains = refs[24:27], refs[27]

    @pl.when(pl.program_id(0) == 0)
    def _():
        for ref, before in zip(sums, start):
            ref[...] = before[...]
        line_weights(extra, held, sel, gains)

    multiply(sums, own, mine, FAR_OWN, False)
    multiply(sums, other, theirs, FAR_OTHER, True)

    @pl.when(pl.program_id(0) == STEPS - 1)
    def _():
        finish(sums, gains, acts, acts_grad)


def finish(sums, gains, acts, acts_grad):
    lane = lax.broadcasted_iota(jnp.int32, (512, 128), 1)
    dots = jnp.zeros((512, 128), F32)
    for slot in range(2):
        units = slice(128 * slot, 128 * slot + 128)
        first, second, back = (ref[:, units] for ref in sums)
        mine = gains[:, slot : slot + 1]
        both = gains[:, 2 * slot : 2 * slot + 1]
        sig = jax.nn.sigmoid(first)
        silu = first * sig
        hidden = silu * second
        for at, part in enumerate(thirds(jnp.sum(hidden * back, axis=1, keepdims=True))):
            dots = jnp.where(lane == 2 * at + slot, part, dots)
        d_first = back * second * sig * (1.0 + first * (1.0 - sig))
        d_second = back * silu
        for at, value in ((0, hidden), (256, d_first), (512, d_second)):
            units = slice(at + 128 * slot, at + 128 * slot + 128)
            acts[:, units] = (value * mine).astype(BF)
            acts_grad[:, units] = (value * both).astype(BF)
    acts[:, 768:] = dots.astype(BF)


def results_kernel(pieces, sel, acts, acts_other, wg, wu, wd, wall, *outs):
    half = sel[0]
    blocks = [(p // 2, 2 * (p % 2) + b) for group in pieces for p in group for b in range(2)]
    places = [(at, 64 * row) for at, group in enumerate(pieces) for row in range(2 * len(group))]
    own = joined([acts[32 * (4 * a + b) : 32 * (4 * a + b) + 32, :] for a, b in blocks])
    other = joined([acts_other[32 * (4 * b + a) : 32 * (4 * b + a) + 32, :] for a, b in blocks])
    hidden = pair(own[:, :256], other[:, :256])
    grads = pair(own[:, 256:768], other[:, 256:768])
    total = outs[0].shape[1] - 128
    width = total // STEPS
    lane = lax.broadcasted_iota(jnp.int32, (own.shape[0], 128), 1)
    dots = jnp.zeros((own.shape[0], 128), F32)
    last = own[:, 768:].astype(F32) + other[:, 768:].astype(F32)
    for slot in range(2):
        mine = jnp.sum(jnp.where((lane < 6) & (lane % 2 == slot), last, 0.0), axis=1, keepdims=True)
        for at, part in enumerate(thirds(mine)):
            dots = jnp.where(lane == 32 * at + 2 * sel[2] + slot, part, dots)
    for block, (at, row) in enumerate(places):
        outs[at][row : row + 32, total:] = dots[32 * block : 32 * block + 32].astype(BF)
        outs[at][row + 32 : row + 64, total:] = jnp.zeros((32, 128), BF)
    for k in range(STEPS):
        cols = slice(k * width, k * width + width)
        down = joined([wall[k, 28 + 2 * q : 30 + 2 * q].reshape(256, 128) for q in range(7)], axis=1)
        down = joined([down_block(wd, k, half, width), down])
        up = [up_block(wg, k, half), up_block(wu, k, half)]
        up += [wall[k, at : at + 7].reshape(width, 128) for at in (0, 7, 14, 21)]
        out = jnp.dot(hidden, down, preferred_element_type=F32)
        grad = lax.dot_general(grads, joined(up, axis=1), NT, preferred_element_type=F32)
        for block, (at, row) in enumerate(places):
            here = slice(32 * block, 32 * block + 32)
            outs[at][row : row + 32, cols] = out[here].astype(BF)
            outs[at][row + 32 : row + 64, cols] = grad[here].astype(BF)


def grads_kernel(swapped, sel, *refs):
    rows, acts = refs[:8], refs[8]
    grad_gate, grad_up, grad_down = refs[-3:]
    blocks = turned(ALL) if swapped else ALL
    tok, cot = rows_of(rows, blocks, False), rows_of(rows, blocks, True)
    hid, d1, d2 = acts[:, :256], acts[:, 256:512], acts[:, 512:768]
    gate = lax.dot_general(tok, d1, TN, preferred_element_type=F32).astype(BF)
    up = lax.dot_general(tok, d2, TN, preferred_element_type=F32).astype(BF)
    down = lax.dot_general(hid, cot, TN, preferred_element_type=F32).astype(BF)
    for slot in range(2):
        units = slice(128 * slot, 128 * slot + 128)
        grad_gate[slot, 0, 0] = gate[:, units]
        grad_up[slot, 0, 0] = up[:, units]
        grad_down[slot] = down[units]


VM = pl.BlockSpec(memory_space=pltpu.VMEM)
SM = pl.BlockSpec(memory_space=pltpu.SMEM)
HB = pl.BlockSpec(memory_space=pltpu.HBM)


def whole(shape):
    return pl.BlockSpec(shape, lambda *_: (0,) * len(shape))


def params(mib):
    return pltpu.CompilerParams(vmem_limit_bytes=mib * 2**20)


def cost(flops, mib):
    return pl.CostEstimate(flops=int(flops), bytes_accessed=int(mib * 2**20), transcendentals=0)


def shape(dims, dtype=BF):
    return jax.ShapeDtypeStruct(dims, dtype)


def pack(sel, tokens, cotangent, extra):
    tok, wide = tokens.shape
    return pl.pallas_call(
        pack_kernel,
        in_specs=[SM, HB, HB, VM],
        out_specs=VM,
        out_shape=shape((2 * tok, wide // 2 + 128)),
        scratch_shapes=[pltpu.SemaphoreType.DMA((2 * STEPS,))],
        compiler_params=params(56),
        cost_estimate=cost(0, 2),
        name="pack",
    )(sel, tokens, cotangent, extra)


def pack_weights(sel, weights):
    width = weights[0].shape[3]
    up_spec = pl.BlockSpec((2, 1, 1, width, 128), lambda k, sel: (0, k, sel[1], 0, 0))
    down_spec = pl.BlockSpec((2, 128, width), lambda k, sel: (0, 0, 2 * k + sel[1]))
    return pl.pallas_call(
        pack_weights_kernel,
        grid_spec=pltpu.PrefetchScalarGridSpec(
            num_scalar_prefetch=1,
            grid=(STEPS,),
            in_specs=[up_spec, up_spec, down_spec],
            out_specs=pl.BlockSpec((1, 42, 128, 128), lambda k, sel: (k, 0, 0, 0)),
        ),
        out_shape=shape((STEPS, 42, 128, 128)),
        compiler_params=params(56),
        cost_estimate=cost(0, 11),
        name="pack_weights",
    )(sel, *weights)


def weight_specs(width, which):
    up_spec = pl.BlockSpec((2, 1, 1, width, 128), lambda k, sel: (0, k, sel[which], 0, 0))
    down_spec = pl.BlockSpec((2, 128, width), lambda k, sel: (0, 0, 2 * k + sel[which]))
    return [up_spec, up_spec, down_spec]


def row_specs(rows, width, first=0):
    return [pl.BlockSpec((r.shape[0], width), lambda k, sel: (0, first + k)) for r in rows]


WIDTH = 896


def near_sums(sel, own, other, weights):
    return pl.pallas_call(
        near_kernel,
        grid_spec=pltpu.PrefetchScalarGridSpec(
            num_scalar_prefetch=1,
            grid=(STEPS,),
            in_specs=row_specs(own + other, WIDTH) + weight_specs(WIDTH, 0) + weight_specs(WIDTH, 1),
            out_specs=[whole((512, 256))] * 3,
        ),
        out_shape=[shape((512, 256), F32)] * 3,
        compiler_params=params(56),
        cost_estimate=cost(0, 0.1),
        name="near_sums",
    )(sel, *own, *other, *weights, *weights)


def activations(sel, own, other, weights, sums, held):
    extra = pl.BlockSpec((128, 128), lambda k, sel: (0, STEPS * WIDTH // 128))
    return pl.pallas_call(
        far_kernel,
        grid_spec=pltpu.PrefetchScalarGridSpec(
            num_scalar_prefetch=1,
            grid=(STEPS,),
            in_specs=row_specs(own[6:] + other, WIDTH)
            + weight_specs(WIDTH, 0)
            + weight_specs(WIDTH, 1)
            + [whole((512, 256))] * 3
            + [extra] * 8
            + [whole((128, 128))],
            out_specs=[whole((512, 896)), whole((512, 768))],
            scratch_shapes=[pltpu.VMEM((512, 256), F32)] * 3 + [pltpu.VMEM((512, 128), F32)],
        ),
        out_shape=[shape((512, 896)), shape((512, 768))],
        compiler_params=params(56),
        cost_estimate=cost(4 * 128 * 768 * WIDTH * STEPS, 15),
        name="activations",
    )(sel, *own[6:], *other, *weights, *weights, *sums, *own, held)


def results(pieces, sel, acts, acts_other, weights, wall, half):
    return pl.pallas_call(
        functools.partial(results_kernel, pieces),
        in_specs=[SM] + [VM] * 6,
        out_specs=[VM] * len(pieces),
        out_shape=[shape((128 * len(group), half + 128)) for group in pieces],
        compiler_params=params(18),
        cost_estimate=cost(2 * 64 * sum(map(len, pieces)) * 1536 * half, 12),
        name="results",
    )(sel, acts, acts_other, *weights, wall)


def weight_grads(swapped, first, count, sel, rows, acts, before):
    width, half = WIDTH, WIDTH * STEPS
    at = 1 if swapped else 0
    up_spec = pl.BlockSpec((2, 1, 1, width, 128), lambda k, sel: (0, first + k, sel[at], 0, 0))
    down_spec = pl.BlockSpec((2, 128, width), lambda k, sel: (0, 0, 2 * (first + k) + sel[at]))
    up_shape = shape((2, STEPS, 2, width, 128))
    return pl.pallas_call(
        functools.partial(grads_kernel, swapped),
        grid_spec=pltpu.PrefetchScalarGridSpec(
            num_scalar_prefetch=1,
            grid=(count,),
            in_specs=row_specs(rows, width, first) + [whole((512, 768))] + [HB] * len(before),
            out_specs=[up_spec, up_spec, down_spec],
        ),
        out_shape=[up_shape, up_shape, shape((2, 128, 2 * half))],
        input_output_aliases={2 + len(rows) + i: i for i in range(len(before))},
        compiler_params=params(20),
        cost_estimate=cost(2 * 512 * 768 * width * count, 3.5 * count),
        name="weight_grads",
    )(sel, *rows, acts, *before)


def gate_weights(logits, slot_expert, chosen):
    experts = logits.shape[1]
    held = jnp.arange(experts, dtype=jnp.int32)[:, None] == slot_expert[None, :]
    picked = jnp.sum(jnp.where(held[None], logits[:, :, None], 0.0), axis=1)
    sig = jnp.where(chosen, jax.nn.sigmoid(picked), 0.0)
    return ROUTE_SCALE * sig / jnp.sum(sig, axis=1, keepdims=True)


def add(*values):
    total = values[0].astype(F32)
    for value in values[1:]:
        total = total + value.astype(F32)
    return total.astype(BF)


def per_device(tokens, cotangent, gate_logits, route_slot, slot_expert, w_gate, w_up, w_down):
    tok, wide = tokens.shape
    half = wide // 2
    width = half // STEPS
    slots = slot_expert.shape[0]
    z, core, y, x = (lax.axis_index(a) for a in AXES)
    line = y * NX + x
    sel = jnp.stack([core, 1 - core, line, 2 * (line ^ (NY * NX // 2)) + 1])
    weights = (
        w_gate.reshape(2, STEPS, 2, width, 128),
        w_up.reshape(2, STEPS, 2, width, 128),
        w_down,
    )
    high = lax.reduce_precision(gate_logits, 8, 7)
    middle = lax.reduce_precision(gate_logits - high, 8, 7)
    extra = joined([high, middle, gate_logits - high - middle, route_slot.astype(F32)], axis=1)
    extra = jnp.pad(extra, ((0, 0), (0, 128 - extra.shape[1]))).astype(BF)
    own = pack(sel, tokens, cotangent, extra)
    own, later = lax.optimization_barrier((own, sel))
    minus, plus, far = send(own, inner(1)), send(own, inner(-1)), send(own, inner(2))
    a, b = joined([own, plus]), joined([minus, far])
    a_minus, b_plus = send(a, outer(1)), send(b, outer(-1))
    b_minus, a_plus = send(b, outer(1)), send(a, outer(-1))
    a_far, b_far = send(a_minus, outer(1)), send(b_plus, outer(-1))
    wall = send(pack_weights(later, weights), other_core())

    near = [a, b, a_plus, b_plus, a_minus, b_minus]
    near_other = [send(piece, other_core()) for piece in near]
    sums = near_sums(sel, near, near_other, weights)
    (a_on, b_on), sums = lax.optimization_barrier(((a_far, b_far), sums))
    far_rows, far_other = [a_far, b_far], [send(a_on, other_core()), send(b_on, other_core())]
    rows, rows_other = near + far_rows, near_other + far_other
    experts = jnp.tile(jnp.arange(24, dtype=jnp.int32), 3)
    held = experts[:, None] == slot_expert[None, :]
    held = jnp.pad(held.astype(F32), ((0, 128 - 72), (0, 128 - slots))).astype(BF)
    acts, acts_grad = activations(sel, rows, far_other, weights, sums, held)
    acts_other = send(acts, other_core())
    grads = weight_grads(False, 0, 2, sel, rows, acts_grad, [])
    acts_other, grads = lax.optimization_barrier((acts_other, grads))

    far_a, far_b = results(((6,), (7,)), sel, acts, acts_other, weights, wall, half)
    own_a, own_b, to_plus, to_minus = results(
        ((0,), (1,), (2, 3), (5, 4)), sel, acts, acts_other, weights, wall, half
    )
    own_a, grads = lax.optimization_barrier((own_a, grads))
    from_a, from_b = send(far_a, outer(1)), send(far_b, outer(-1))
    to_plus = lax.dynamic_update_slice(to_plus, add(to_plus[:128], from_a), (0, 0))
    to_minus = lax.dynamic_update_slice(to_minus, add(to_minus[:128], from_b), (0, 0))
    got_p, got_m = send(to_plus, outer(1)), send(to_minus, outer(-1))
    grads = weight_grads(False, 2, 2, sel, rows, acts_grad, grads)
    grads = weight_grads(True, 0, 4, sel, rows_other, acts_grad, grads)
    (got_p, got_m), grads = lax.optimization_barrier(((got_p, got_m), grads))
    keep = (own_a[:64], got_p[:64], got_m[128:192])
    to_plus = add(own_a[64:], got_p[64:128], got_m[192:])
    to_minus = add(own_b[:64], got_p[128:192], got_m[:64])
    to_far = add(own_b[64:], got_p[192:], got_m[64:128])
    total = add(
        *keep, send(to_plus, inner(1)), send(to_minus, inner(-1)), send(to_far, inner(2))
    )

    def block_for(by):
        block = lax.dynamic_slice(total, (0, (z + by) % NZ * width), (2 * tok, width))
        return joined([block, total[:, half:]], axis=1)

    last = block_for(0).astype(F32)
    for by in (1, 3, 2):
        last = last + send(block_for(by), along_z(by)).astype(F32)
    mixed, grad_tokens = last[:tok, :width].astype(BF), last[tok:, :width].astype(BF)
    home = sum(last[:tok, width + at : width + at + slots] for at in (0, slots, 2 * slots))
    chosen = jnp.any(
        route_slot[:, :, None] == jnp.arange(slots, dtype=jnp.int32)[None, None, :], axis=1
    )
    _, pull_back = jax.vjp(lambda lg: gate_weights(lg, slot_expert, chosen), gate_logits)
    grad_logits = pull_back(home)[0]
    return (
        mixed,
        grad_tokens,
        grad_logits,
        grads[0].reshape(w_gate.shape),
        grads[1].reshape(w_up.shape),
        grads[2],
    )


def solution(mesh):
    split = Mesh(mesh.devices.reshape(NZ, NC, NY, NX), AXES)
    local, group = ("y", "x"), ("z", "c")
    return jax.shard_map(
        per_device,
        mesh=split,
        in_specs=(
            P(local, None),
            P(local, None),
            P(local, None),
            P(local, None),
            P(),
            P(local, None, group),
            P(local, None, group),
            P(local, group, None),
        ),
        out_specs=(
            P(local, group),
            P(local, group),
            P(local, None),
            P(local, None, group),
            P(local, None, group),
            P(local, group, None),
        ),
        check_vma=False,
    )
```

```python
import functools

import jax
import jax.numpy as jnp
from jax import lax
from jax.experimental import pallas as pl
from jax.experimental.pallas import tpu as pltpu
from jax.sharding import Mesh
from jax.sharding import PartitionSpec as P

ROUTE_SCALE = 2.5
TOP = 8
ROUTE = 3 * 24
NZ, NC, NY, NX = 4, 2, 4, 4
AXES = ("z", "c", "y", "x")
STEPS = 4
BF, F32 = jnp.bfloat16, jnp.float32
NT = (((1,), (1,)), ((), ()))
TN = (((0,), (0,)), ((), ()))
RING = (0, 1, 3, 2)


def moves(step):
    pairs = []
    for z in range(NZ):
        for c in range(NC):
            for y in range(NY):
                for x in range(NX):
                    z2, c2, y2, x2 = step(z, c, y, x)
                    source = ((z * NC + c) * NY + y) * NX + x
                    target = ((z2 % NZ * NC + c2 % NC) * NY + y2 % NY) * NX + x2 % NX
                    pairs.append((source, target))
    return pairs


def outer(by):
    return moves(lambda z, c, y, x: (z, c, y + by, x) if c == 0 else (z, c, y, x + by))


def inner(by):
    return moves(lambda z, c, y, x: (z, c, y, x + by) if c == 0 else (z, c, y + by, x))


def along_z(by):
    return moves(lambda z, c, y, x: (z + by, c, y, x))


def other_core():
    return moves(lambda z, c, y, x: (z, c + 1, y, x))


def send(value, pairs):
    return lax.ppermute(value, AXES, pairs)


def joined(parts, axis=0):
    return jnp.concatenate(parts, axis=axis)


def rows_of(refs, blocks, second):
    parts = []
    for outer_at, inner_at in blocks:
        row = 64 * (inner_at % 2) + (32 if second else 0)
        parts.append(refs[2 * outer_at + inner_at // 2][row : row + 32, :])
    return joined(parts)


def turned(blocks):
    return [(b, a) for a, b in blocks]


ALL = [(a, b) for a in range(4) for b in range(4)]
NEAR_OWN = [(a, b) for a in range(3) for b in range(4)]
FAR_OWN = [(3, b) for b in range(4)]
NEAR_OTHER = [(a, b) for a in range(4) for b in range(3)]
FAR_OTHER = [(a, 3) for a in range(4)]


def pair(first, second):
    return joined([first, second], axis=1)


def weight_block(wg, wu, wd):
    gate, up = (pair(ref[0, 0, 0], ref[1, 0, 0]) for ref in (wg, wu))
    return gate, up, wd[...].reshape(-1, wd.shape[2])


def up_block(ref, k, half):
    return pair(ref[0, k, half], ref[1, k, half])


def down_block(ref, k, half, width):
    at = pl.multiple_of((2 * k + half) * width, 128)
    return ref[:, :, pl.ds(at, width)].reshape(-1, width)


def products(tok, cot, gate, up, down):
    first = jnp.dot(tok, gate, preferred_element_type=F32)
    second = jnp.dot(tok, up, preferred_element_type=F32)
    back = lax.dot_general(cot, down, NT, preferred_element_type=F32)
    return first, second, back


def pack_kernel(sel, tok, cot, extra, packed, sems):
    rows, half = extra.shape[0], packed.shape[1] - 128
    width = half // STEPS
    copies = []
    for k in range(STEPS):
        at = pl.multiple_of((2 * k + sel[0]) * width, 128)
        for base, ref in enumerate((tok, cot)):
            target = packed.at[pl.ds(base * rows, rows), pl.ds(k * width, width)]
            copies.append(
                pltpu.make_async_copy(ref.at[:, pl.ds(at, width)], target, sems.at[len(copies)])
            )
            copies[-1].start()
    packed[:rows, half:] = extra[...]
    packed[rows:, half:] = jnp.zeros_like(extra)
    for one in copies:
        one.wait()


def pack_weights_kernel(sel, wg, wu, wd, wall):
    for base, ref in ((0, wg), (14, wu)):
        for slot in range(2):
            at = base + 7 * slot
            wall[0, at : at + 7] = ref[slot, 0, 0].reshape(7, 128, 128)
    for q in range(7):
        wall[0, 28 + 2 * q : 30 + 2 * q] = wd[:, :, 128 * q : 128 * q + 128]


def multiply(sums, rows, weights, blocks, swapped):
    where = turned(blocks) if swapped else blocks
    parts = products(
        rows_of(rows, where, False), rows_of(rows, where, True), *weight_block(*weights)
    )
    for ref, part in zip(sums, parts):
        for outer_at in sorted({o for o, _ in blocks}):
            inners = [i for o, i in blocks if o == outer_at]
            low = 32 * blocks.index((outer_at, inners[0]))
            to = 32 * (4 * outer_at + inners[0])
            ref[to : to + 32 * len(inners)] += part[low : low + 32 * len(inners)]


def near_kernel(sel, *refs):
    own, other, mine, theirs, sums = refs[:6], refs[6:12], refs[12:15], refs[15:18], refs[18:21]

    @pl.when(pl.program_id(0) == 0)
    def _():
        for ref in sums:
            ref[...] = jnp.zeros_like(ref)

    multiply(sums, own, mine, NEAR_OWN, False)
    multiply(sums, other, theirs, NEAR_OTHER, True)


def line_weights(extra, held, sel, gains):
    rows = rows_of(extra, ALL, False)
    picked = jnp.dot(rows, held[...], preferred_element_type=F32)
    lane = lax.broadcasted_iota(jnp.int32, picked.shape, 1)
    slot = lane.astype(F32)
    chosen = slot < 0
    for at in range(TOP):
        chosen = chosen | (slot == rows[:, ROUTE + at : ROUTE + at + 1].astype(F32))
    sig = jnp.where(chosen, jax.nn.sigmoid(picked), 0.0)
    weight = ROUTE_SCALE * sig / jnp.sum(sig, axis=1, keepdims=True)

    def column(at):
        return jnp.sum(jnp.where(lane == at, weight, 0.0), axis=1, keepdims=True)

    cold, hot, partner = column(2 * sel[2]), column(2 * sel[2] + 1), column(sel[3])
    gains[...] = jnp.where(lane == 0, cold, jnp.where(lane == 1, hot, hot + partner))


def thirds(value):
    high = value.astype(BF).astype(F32)
    middle = (value - high).astype(BF).astype(F32)
    return high, middle, value - high - middle


def far_kernel(sel, *refs):
    own, other = dict(zip((6, 7), refs)), dict(zip((6, 7), refs[2:]))
    mine, theirs, start, extra, held = refs[4:7], refs[7:10], refs[10:13], refs[13:21], refs[21]
    acts, acts_grad = refs[22:24]
    sums, gains = refs[24:27], refs[27]

    @pl.when(pl.program_id(0) == 0)
    def _():
        for ref, before in zip(sums, start):
            ref[...] = before[...]
        line_weights(extra, held, sel, gains)

    multiply(sums, own, mine, FAR_OWN, False)
    multiply(sums, other, theirs, FAR_OTHER, True)

    @pl.when(pl.program_id(0) == STEPS - 1)
    def _():
        finish(sums, gains, acts, acts_grad)


def finish(sums, gains, acts, acts_grad):
    lane = lax.broadcasted_iota(jnp.int32, (512, 128), 1)
    dots = jnp.zeros((512, 128), F32)
    for slot in range(2):
        units = slice(128 * slot, 128 * slot + 128)
        first, second, back = (ref[:, units] for ref in sums)
        mine = gains[:, slot : slot + 1]
        both = gains[:, 2 * slot : 2 * slot + 1]
        sig = jax.nn.sigmoid(first)
        silu = first * sig
        hidden = silu * second
        for at, part in enumerate(thirds(jnp.sum(hidden * back, axis=1, keepdims=True))):
            dots = jnp.where(lane == 2 * at + slot, part, dots)
        d_first = back * second * sig * (1.0 + first * (1.0 - sig))
        d_second = back * silu
        for at, value in ((0, hidden), (256, d_first), (512, d_second)):
            units = slice(at + 128 * slot, at + 128 * slot + 128)
            acts[:, units] = (value * mine).astype(BF)
            acts_grad[:, units] = (value * both).astype(BF)
    acts[:, 768:] = dots.astype(BF)


def results_kernel(pieces, sel, acts, acts_other, wg, wu, wd, wall, *outs):
    half = sel[0]
    blocks = [(p // 2, 2 * (p % 2) + b) for group in pieces for p in group for b in range(2)]
    places = [(at, 64 * row) for at, group in enumerate(pieces) for row in range(2 * len(group))]
    own = joined([acts[32 * (4 * a + b) : 32 * (4 * a + b) + 32, :] for a, b in blocks])
    other = joined([acts_other[32 * (4 * b + a) : 32 * (4 * b + a) + 32, :] for a, b in blocks])
    hidden = pair(own[:, :256], other[:, :256])
    grads = pair(own[:, 256:768], other[:, 256:768])
    total = outs[0].shape[1] - 128
    width = total // STEPS
    lane = lax.broadcasted_iota(jnp.int32, (own.shape[0], 128), 1)
    dots = jnp.zeros((own.shape[0], 128), F32)
    last = own[:, 768:].astype(F32) + other[:, 768:].astype(F32)
    for slot in range(2):
        mine = jnp.sum(jnp.where((lane < 6) & (lane % 2 == slot), last, 0.0), axis=1, keepdims=True)
        for at, part in enumerate(thirds(mine)):
            dots = jnp.where(lane == 32 * at + 2 * sel[2] + slot, part, dots)
    for block, (at, row) in enumerate(places):
        outs[at][row : row + 32, total:] = dots[32 * block : 32 * block + 32].astype(BF)
        outs[at][row + 32 : row + 64, total:] = jnp.zeros((32, 128), BF)
    for k in range(STEPS):
        cols = slice(k * width, k * width + width)
        down = joined([wall[k, 28 + 2 * q : 30 + 2 * q].reshape(256, 128) for q in range(7)], axis=1)
        down = joined([down_block(wd, k, half, width), down])
        up = [up_block(wg, k, half), up_block(wu, k, half)]
        up += [wall[k, at : at + 7].reshape(width, 128) for at in (0, 7, 14, 21)]
        out = jnp.dot(hidden, down, preferred_element_type=F32)
        grad = lax.dot_general(grads, joined(up, axis=1), NT, preferred_element_type=F32)
        for block, (at, row) in enumerate(places):
            here = slice(32 * block, 32 * block + 32)
            outs[at][row : row + 32, cols] = out[here].astype(BF)
            outs[at][row + 32 : row + 64, cols] = grad[here].astype(BF)


def grads_kernel(swapped, sel, *refs):
    rows, acts = refs[:8], refs[8]
    grad_gate, grad_up, grad_down = refs[-3:]
    blocks = turned(ALL) if swapped else ALL
    tok, cot = rows_of(rows, blocks, False), rows_of(rows, blocks, True)
    hid, d1, d2 = acts[:, :256], acts[:, 256:512], acts[:, 512:768]
    gate = lax.dot_general(tok, d1, TN, preferred_element_type=F32).astype(BF)
    up = lax.dot_general(tok, d2, TN, preferred_element_type=F32).astype(BF)
    down = lax.dot_general(hid, cot, TN, preferred_element_type=F32).astype(BF)
    for slot in range(2):
        units = slice(128 * slot, 128 * slot + 128)
        grad_gate[slot, 0, 0] = gate[:, units]
        grad_up[slot, 0, 0] = up[:, units]
        grad_down[slot] = down[units]


VM = pl.BlockSpec(memory_space=pltpu.VMEM)
SM = pl.BlockSpec(memory_space=pltpu.SMEM)
HB = pl.BlockSpec(memory_space=pltpu.HBM)


def whole(shape):
    return pl.BlockSpec(shape, lambda *_: (0,) * len(shape))


def params(mib):
    return pltpu.CompilerParams(vmem_limit_bytes=mib * 2**20)


def cost(flops, mib):
    return pl.CostEstimate(flops=int(flops), bytes_accessed=int(mib * 2**20), transcendentals=0)


def shape(dims, dtype=BF):
    return jax.ShapeDtypeStruct(dims, dtype)


def pack(sel, tokens, cotangent, extra):
    tok, wide = tokens.shape
    return pl.pallas_call(
        pack_kernel,
        in_specs=[SM, HB, HB, VM],
        out_specs=VM,
        out_shape=shape((2 * tok, wide // 2 + 128)),
        scratch_shapes=[pltpu.SemaphoreType.DMA((2 * STEPS,))],
        compiler_params=params(56),
        cost_estimate=cost(0, 2),
        name="pack",
    )(sel, tokens, cotangent, extra)


def pack_weights(sel, weights):
    width = weights[0].shape[3]
    up_spec = pl.BlockSpec((2, 1, 1, width, 128), lambda k, sel: (0, k, sel[1], 0, 0))
    down_spec = pl.BlockSpec((2, 128, width), lambda k, sel: (0, 0, 2 * k + sel[1]))
    return pl.pallas_call(
        pack_weights_kernel,
        grid_spec=pltpu.PrefetchScalarGridSpec(
            num_scalar_prefetch=1,
            grid=(STEPS,),
            in_specs=[up_spec, up_spec, down_spec],
            out_specs=pl.BlockSpec((1, 42, 128, 128), lambda k, sel: (k, 0, 0, 0)),
        ),
        out_shape=shape((STEPS, 42, 128, 128)),
        compiler_params=params(56),
        cost_estimate=cost(0, 11),
        name="pack_weights",
    )(sel, *weights)


def weight_specs(width, which):
    up_spec = pl.BlockSpec((2, 1, 1, width, 128), lambda k, sel: (0, k, sel[which], 0, 0))
    down_spec = pl.BlockSpec((2, 128, width), lambda k, sel: (0, 0, 2 * k + sel[which]))
    return [up_spec, up_spec, down_spec]


def row_specs(rows, width, first=0):
    return [pl.BlockSpec((r.shape[0], width), lambda k, sel: (0, first + k)) for r in rows]


WIDTH = 896


def near_sums(sel, own, other, weights):
    return pl.pallas_call(
        near_kernel,
        grid_spec=pltpu.PrefetchScalarGridSpec(
            num_scalar_prefetch=1,
            grid=(STEPS,),
            in_specs=row_specs(own + other, WIDTH) + weight_specs(WIDTH, 0) + weight_specs(WIDTH, 1),
            out_specs=[whole((512, 256))] * 3,
        ),
        out_shape=[shape((512, 256), F32)] * 3,
        compiler_params=params(56),
        cost_estimate=cost(0, 0.1),
        name="near_sums",
    )(sel, *own, *other, *weights, *weights)


def activations(sel, own, other, weights, sums, held):
    extra = pl.BlockSpec((128, 128), lambda k, sel: (0, STEPS * WIDTH // 128))
    return pl.pallas_call(
        far_kernel,
        grid_spec=pltpu.PrefetchScalarGridSpec(
            num_scalar_prefetch=1,
            grid=(STEPS,),
            in_specs=row_specs(own[6:] + other, WIDTH)
            + weight_specs(WIDTH, 0)
            + weight_specs(WIDTH, 1)
            + [whole((512, 256))] * 3
            + [extra] * 8
            + [whole((128, 128))],
            out_specs=[whole((512, 896)), whole((512, 768))],
            scratch_shapes=[pltpu.VMEM((512, 256), F32)] * 3 + [pltpu.VMEM((512, 128), F32)],
        ),
        out_shape=[shape((512, 896)), shape((512, 768))],
        compiler_params=params(56),
        cost_estimate=cost(4 * 128 * 768 * WIDTH * STEPS, 15),
        name="activations",
    )(sel, *own[6:], *other, *weights, *weights, *sums, *own, held)


def results(pieces, sel, acts, acts_other, weights, wall, half):
    return pl.pallas_call(
        functools.partial(results_kernel, pieces),
        in_specs=[SM] + [VM] * 6,
        out_specs=[VM] * len(pieces),
        out_shape=[shape((128 * len(group), half + 128)) for group in pieces],
        compiler_params=params(14),
        cost_estimate=cost(2 * 64 * sum(map(len, pieces)) * 1536 * half, 12),
        name="results",
    )(sel, acts, acts_other, *weights, wall)


def weight_grads(swapped, first, count, sel, rows, acts, before, room):
    width, half = WIDTH, WIDTH * STEPS
    at = 1 if swapped else 0
    up_spec = pl.BlockSpec((2, 1, 1, width, 128), lambda k, sel: (0, first + k, sel[at], 0, 0))
    down_spec = pl.BlockSpec((2, 128, width), lambda k, sel: (0, 0, 2 * (first + k) + sel[at]))
    up_shape = shape((2, STEPS, 2, width, 128))
    return pl.pallas_call(
        functools.partial(grads_kernel, swapped),
        grid_spec=pltpu.PrefetchScalarGridSpec(
            num_scalar_prefetch=1,
            grid=(count,),
            in_specs=row_specs(rows, width, first) + [whole((512, 768))] + [HB] * len(before),
            out_specs=[up_spec, up_spec, down_spec],
        ),
        out_shape=[up_shape, up_shape, shape((2, 128, 2 * half))],
        input_output_aliases={2 + len(rows) + i: i for i in range(len(before))},
        compiler_params=params(room),
        cost_estimate=cost(2 * 512 * 768 * width * count, 3.5 * count),
        name="weight_grads",
    )(sel, *rows, acts, *before)


def gate_weights(logits, slot_expert, chosen):
    experts = logits.shape[1]
    held = jnp.arange(experts, dtype=jnp.int32)[:, None] == slot_expert[None, :]
    picked = jnp.sum(jnp.where(held[None], logits[:, :, None], 0.0), axis=1)
    sig = jnp.where(chosen, jax.nn.sigmoid(picked), 0.0)
    return ROUTE_SCALE * sig / jnp.sum(sig, axis=1, keepdims=True)


def add(*values):
    total = values[0].astype(F32)
    for value in values[1:]:
        total = total + value.astype(F32)
    return total.astype(BF)


def per_device(tokens, cotangent, gate_logits, route_slot, slot_expert, w_gate, w_up, w_down):
    tok, wide = tokens.shape
    half = wide // 2
    width = half // STEPS
    slots = slot_expert.shape[0]
    z, core, y, x = (lax.axis_index(a) for a in AXES)
    line = y * NX + x
    sel = jnp.stack([core, 1 - core, line, 2 * (line ^ (NY * NX // 2)) + 1])
    weights = (
        w_gate.reshape(2, STEPS, 2, width, 128),
        w_up.reshape(2, STEPS, 2, width, 128),
        w_down,
    )
    high = lax.reduce_precision(gate_logits, 8, 7)
    middle = lax.reduce_precision(gate_logits - high, 8, 7)
    parts = (high, middle, gate_logits - high - middle, route_slot.astype(F32))
    extra = sum(
        lax.pad(part, 0.0, ((0, 0, 0), (24 * at, 128 - 24 * at - part.shape[1], 0)))
        for at, part in enumerate(parts)
    ).astype(BF)
    own = pack(sel, tokens, cotangent, extra)
    own, later = lax.optimization_barrier((own, sel))
    minus, plus, far = send(own, inner(1)), send(own, inner(-1)), send(own, inner(2))
    a, b = joined([own, plus]), joined([minus, far])
    a_minus, b_plus = send(a, outer(1)), send(b, outer(-1))
    b_minus, a_plus = send(b, outer(1)), send(a, outer(-1))
    a_far, b_far = send(a_minus, outer(1)), send(b_plus, outer(-1))
    wall = send(pack_weights(later, weights), other_core())

    near = [a, b, a_plus, b_plus, a_minus, b_minus]
    near_other = [send(piece, other_core()) for piece in near]
    sums = near_sums(sel, near, near_other, weights)
    (a_on, b_on), sums = lax.optimization_barrier(((a_far, b_far), sums))
    far_rows, far_other = [a_far, b_far], [send(a_on, other_core()), send(b_on, other_core())]
    rows, rows_other = near + far_rows, near_other + far_other
    experts = jnp.tile(jnp.arange(24, dtype=jnp.int32), 3)
    held = experts[:, None] == slot_expert[None, :]
    held = jnp.pad(held.astype(F32), ((0, 128 - 72), (0, 128 - slots))).astype(BF)
    acts, acts_grad = activations(sel, rows, far_other, weights, sums, held)
    acts_other = send(acts, other_core())

    far_a, far_b = results(((6,), (7,)), sel, acts, acts_other, weights, wall, half)
    own_a, own_b, plus_a, plus_b, minus_b, minus_a = results(
        ((0,), (1,), (2,), (3,), (5,), (4,)), sel, acts, acts_other, weights, wall, half
    )
    own_a, acts_grad = lax.optimization_barrier((own_a, acts_grad))
    from_a, from_b = send(far_a, outer(1)), send(far_b, outer(-1))
    b_early, a_early = send(plus_b, outer(1)), send(minus_a, outer(-1))
    a_late = send(add(plus_a, from_a), outer(1))
    b_late = send(add(minus_b, from_b), outer(-1))
    grads = weight_grads(False, 0, 4, sel, rows, acts_grad, [], 52)
    grads = weight_grads(True, 0, 4, sel, rows_other, acts_grad, grads, 52)
    (a_late, b_late), grads = lax.optimization_barrier(((a_late, b_late), grads))
    keep = (own_a[:64], a_late[:64], a_early[:64])
    to_plus = add(own_a[64:], a_late[64:], a_early[64:])
    to_minus = add(own_b[:64], b_late[:64], b_early[:64])
    to_far = add(own_b[64:], b_late[64:], b_early[64:])
    total = add(
        *keep, send(to_plus, inner(1)), send(to_minus, inner(-1)), send(to_far, inner(2))
    )

    def block_for(by):
        block = lax.dynamic_slice(total, (0, (z + by) % NZ * width), (2 * tok, width))
        return joined([block, total[:, half:]], axis=1)

    last = block_for(0).astype(F32)
    for by in (1, 3, 2):
        last = last + send(block_for(by), along_z(by)).astype(F32)
    mixed, grad_tokens = last[:tok, :width].astype(BF), last[tok:, :width].astype(BF)
    home = sum(last[:tok, width + at : width + at + slots] for at in (0, slots, 2 * slots))
    chosen = jnp.any(
        route_slot[:, :, None] == jnp.arange(slots, dtype=jnp.int32)[None, None, :], axis=1
    )
    _, pull_back = jax.vjp(lambda lg: gate_weights(lg, slot_expert, chosen), gate_logits)
    grad_logits = pull_back(home)[0]
    return (
        mixed,
        grad_tokens,
        grad_logits,
        grads[0].reshape(w_gate.shape),
        grads[1].reshape(w_up.shape),
        grads[2],
    )


def solution(mesh):
    split = Mesh(mesh.devices.reshape(NZ, NC, NY, NX), AXES)
    local, group = ("y", "x"), ("z", "c")
    return jax.shard_map(
        per_device,
        mesh=split,
        in_specs=(
            P(local, None),
            P(local, None),
            P(local, None),
            P(local, None),
            P(),
            P(local, None, group),
            P(local, None, group),
            P(local, group, None),
        ),
        out_specs=(
            P(local, group),
            P(local, group),
            P(local, None),
            P(local, None, group),
            P(local, None, group),
            P(local, group, None),
        ),
        check_vma=False,
    )
```

```python
import functools

import jax
import jax.numpy as jnp
from jax import lax
from jax.experimental import pallas as pl
from jax.experimental.pallas import tpu as pltpu
from jax.sharding import Mesh
from jax.sharding import PartitionSpec as P

ROUTE_SCALE = 2.5
TOP = 8
ROUTE = 3 * 24
NZ, NC, NY, NX = 4, 2, 4, 4
AXES = ("z", "c", "y", "x")
STEPS = 4
BF, F32 = jnp.bfloat16, jnp.float32
NT = (((1,), (1,)), ((), ()))
TN = (((0,), (0,)), ((), ()))
RING = (0, 1, 3, 2)


def moves(step):
    pairs = []
    for z in range(NZ):
        for c in range(NC):
            for y in range(NY):
                for x in range(NX):
                    z2, c2, y2, x2 = step(z, c, y, x)
                    source = ((z * NC + c) * NY + y) * NX + x
                    target = ((z2 % NZ * NC + c2 % NC) * NY + y2 % NY) * NX + x2 % NX
                    pairs.append((source, target))
    return pairs


def outer(by):
    return moves(lambda z, c, y, x: (z, c, y + by, x) if c == 0 else (z, c, y, x + by))


def inner(by):
    return moves(lambda z, c, y, x: (z, c, y, x + by) if c == 0 else (z, c, y + by, x))


def along_z(by):
    return moves(lambda z, c, y, x: (z + by, c, y, x))


def other_core():
    return moves(lambda z, c, y, x: (z, c + 1, y, x))


def send(value, pairs):
    return lax.ppermute(value, AXES, pairs)


def joined(parts, axis=0):
    return jnp.concatenate(parts, axis=axis)


def rows_of(refs, blocks, second):
    parts = []
    for outer_at, inner_at in blocks:
        row = 64 * (inner_at % 2) + (32 if second else 0)
        parts.append(refs[2 * outer_at + inner_at // 2][row : row + 32, :])
    return joined(parts)


def turned(blocks):
    return [(b, a) for a, b in blocks]


ALL = [(a, b) for a in range(4) for b in range(4)]
NEAR_OWN = [(a, b) for a in range(3) for b in range(4)]
FAR_OWN = [(3, b) for b in range(4)]
NEAR_OTHER = [(a, b) for a in range(4) for b in range(3)]
FAR_OTHER = [(a, 3) for a in range(4)]


def pair(first, second):
    return joined([first, second], axis=1)


def weight_block(wg, wu, wd):
    gate, up = (pair(ref[0, 0, 0], ref[1, 0, 0]) for ref in (wg, wu))
    return gate, up, wd[...].reshape(-1, wd.shape[2])


def up_block(ref, k, half):
    return pair(ref[0, k, half], ref[1, k, half])


def down_block(ref, k, half, width):
    at = pl.multiple_of((2 * k + half) * width, 128)
    return ref[:, :, pl.ds(at, width)].reshape(-1, width)


def products(tok, cot, gate, up, down):
    first = jnp.dot(tok, gate, preferred_element_type=F32)
    second = jnp.dot(tok, up, preferred_element_type=F32)
    back = lax.dot_general(cot, down, NT, preferred_element_type=F32)
    return first, second, back


def pack_kernel(sel, tok, cot, extra, packed, sems):
    rows, half = extra.shape[0], packed.shape[1] - 128
    width = half // STEPS
    copies = []
    for k in range(STEPS):
        at = pl.multiple_of((2 * k + sel[0]) * width, 128)
        for base, ref in enumerate((tok, cot)):
            target = packed.at[pl.ds(base * rows, rows), pl.ds(k * width, width)]
            copies.append(
                pltpu.make_async_copy(ref.at[:, pl.ds(at, width)], target, sems.at[len(copies)])
            )
            copies[-1].start()
    packed[:rows, half:] = extra[...]
    packed[rows:, half:] = jnp.zeros_like(extra)
    for one in copies:
        one.wait()


def pack_weights_kernel(sel, wg, wu, wd, wall):
    for base, ref in ((0, wg), (14, wu)):
        for slot in range(2):
            at = base + 7 * slot
            wall[0, at : at + 7] = ref[slot, 0, 0].reshape(7, 128, 128)
    for q in range(7):
        wall[0, 28 + 2 * q : 30 + 2 * q] = wd[:, :, 128 * q : 128 * q + 128]


def multiply(sums, rows, weights, blocks, swapped):
    where = turned(blocks) if swapped else blocks
    parts = products(
        rows_of(rows, where, False), rows_of(rows, where, True), *weight_block(*weights)
    )
    for ref, part in zip(sums, parts):
        for outer_at in sorted({o for o, _ in blocks}):
            inners = [i for o, i in blocks if o == outer_at]
            low = 32 * blocks.index((outer_at, inners[0]))
            to = 32 * (4 * outer_at + inners[0])
            ref[to : to + 32 * len(inners)] += part[low : low + 32 * len(inners)]


def near_kernel(sel, *refs):
    own, other, mine, theirs, sums = refs[:6], refs[6:12], refs[12:15], refs[15:18], refs[18:21]

    @pl.when(pl.program_id(0) == 0)
    def _():
        for ref in sums:
            ref[...] = jnp.zeros_like(ref)

    multiply(sums, own, mine, NEAR_OWN, False)
    multiply(sums, other, theirs, NEAR_OTHER, True)


def sums_kernel(numbers, blocks, swapped, has_start, with_gains, sel, *refs):
    count = len(numbers)
    rows, weights, refs = dict(zip(numbers, refs)), refs[count : count + 3], refs[count + 3 :]
    start, refs = (refs[:3], refs[3:]) if has_start else (None, refs)
    if with_gains:
        extra, held, refs = refs[:8], refs[8], refs[9:]
    sums = refs[:3]

    @pl.when(pl.program_id(0) == 0)
    def _():
        for at, ref in enumerate(sums):
            ref[...] = start[at][...] if has_start else jnp.zeros_like(ref)
        if with_gains:
            line_weights(extra, held, sel, refs[3])

    multiply(sums, rows, weights, blocks, swapped)


def line_weights(extra, held, sel, gains):
    rows = rows_of(extra, ALL, False)
    picked = jnp.dot(rows, held[...], preferred_element_type=F32)
    lane = lax.broadcasted_iota(jnp.int32, picked.shape, 1)
    slot = lane.astype(F32)
    chosen = slot < 0
    for at in range(TOP):
        chosen = chosen | (slot == rows[:, ROUTE + at : ROUTE + at + 1].astype(F32))
    sig = jnp.where(chosen, jax.nn.sigmoid(picked), 0.0)
    weight = ROUTE_SCALE * sig / jnp.sum(sig, axis=1, keepdims=True)

    def column(at):
        return jnp.sum(jnp.where(lane == at, weight, 0.0), axis=1, keepdims=True)

    cold, hot, partner = column(2 * sel[2]), column(2 * sel[2] + 1), column(sel[3])
    gains[...] = jnp.where(lane == 0, cold, jnp.where(lane == 1, hot, hot + partner))


def thirds(value):
    high = value.astype(BF).astype(F32)
    middle = (value - high).astype(BF).astype(F32)
    return high, middle, value - high - middle


def last_kernel(sel, *refs):
    other, theirs, start, gains = dict(zip((6, 7), refs)), refs[2:5], refs[5:8], refs[8]
    acts, acts_grad = refs[9:11]
    sums = refs[11:14]

    @pl.when(pl.program_id(0) == 0)
    def _():
        for ref, before in zip(sums, start):
            ref[...] = before[...]

    multiply(sums, other, theirs, FAR_OTHER, True)

    @pl.when(pl.program_id(0) == STEPS - 1)
    def _():
        finish(sums, gains, acts, acts_grad)


def finish(sums, gains, acts, acts_grad):
    lane = lax.broadcasted_iota(jnp.int32, (512, 128), 1)
    dots = jnp.zeros((512, 128), F32)
    for slot in range(2):
        units = slice(128 * slot, 128 * slot + 128)
        first, second, back = (ref[:, units] for ref in sums)
        mine = gains[:, slot : slot + 1]
        both = gains[:, 2 * slot : 2 * slot + 1]
        sig = jax.nn.sigmoid(first)
        silu = first * sig
        hidden = silu * second
        for at, part in enumerate(thirds(jnp.sum(hidden * back, axis=1, keepdims=True))):
            dots = jnp.where(lane == 2 * at + slot, part, dots)
        d_first = back * second * sig * (1.0 + first * (1.0 - sig))
        d_second = back * silu
        for at, value in ((0, hidden), (256, d_first), (512, d_second)):
            units = slice(at + 128 * slot, at + 128 * slot + 128)
            acts[:, units] = (value * mine).astype(BF)
            acts_grad[:, units] = (value * both).astype(BF)
    acts[:, 768:] = dots.astype(BF)


def results_kernel(pieces, sel, acts, acts_other, wg, wu, wd, wall, *outs):
    half = sel[0]
    blocks = [(p // 2, 2 * (p % 2) + b) for group in pieces for p in group for b in range(2)]
    places = [(at, 64 * row) for at, group in enumerate(pieces) for row in range(2 * len(group))]
    own = joined([acts[32 * (4 * a + b) : 32 * (4 * a + b) + 32, :] for a, b in blocks])
    other = joined([acts_other[32 * (4 * b + a) : 32 * (4 * b + a) + 32, :] for a, b in blocks])
    hidden = pair(own[:, :256], other[:, :256])
    grads = pair(own[:, 256:768], other[:, 256:768])
    total = outs[0].shape[1] - 128
    width = total // STEPS
    lane = lax.broadcasted_iota(jnp.int32, (own.shape[0], 128), 1)
    dots = jnp.zeros((own.shape[0], 128), F32)
    last = own[:, 768:].astype(F32) + other[:, 768:].astype(F32)
    for slot in range(2):
        mine = jnp.sum(jnp.where((lane < 6) & (lane % 2 == slot), last, 0.0), axis=1, keepdims=True)
        for at, part in enumerate(thirds(mine)):
            dots = jnp.where(lane == 32 * at + 2 * sel[2] + slot, part, dots)
    for block, (at, row) in enumerate(places):
        outs[at][row : row + 32, total:] = dots[32 * block : 32 * block + 32].astype(BF)
        outs[at][row + 32 : row + 64, total:] = jnp.zeros((32, 128), BF)
    for k in range(STEPS):
        cols = slice(k * width, k * width + width)
        down = joined([wall[k, 28 + 2 * q : 30 + 2 * q].reshape(256, 128) for q in range(7)], axis=1)
        down = joined([down_block(wd, k, half, width), down])
        up = [up_block(wg, k, half), up_block(wu, k, half)]
        up += [wall[k, at : at + 7].reshape(width, 128) for at in (0, 7, 14, 21)]
        out = jnp.dot(hidden, down, preferred_element_type=F32)
        grad = lax.dot_general(grads, joined(up, axis=1), NT, preferred_element_type=F32)
        for block, (at, row) in enumerate(places):
            here = slice(32 * block, 32 * block + 32)
            outs[at][row : row + 32, cols] = out[here].astype(BF)
            outs[at][row + 32 : row + 64, cols] = grad[here].astype(BF)


def grads_kernel(swapped, sel, *refs):
    rows, acts = refs[:8], refs[8]
    grad_gate, grad_up, grad_down = refs[-3:]
    blocks = turned(ALL) if swapped else ALL
    tok, cot = rows_of(rows, blocks, False), rows_of(rows, blocks, True)
    hid, d1, d2 = acts[:, :256], acts[:, 256:512], acts[:, 512:768]
    gate = lax.dot_general(tok, d1, TN, preferred_element_type=F32).astype(BF)
    up = lax.dot_general(tok, d2, TN, preferred_element_type=F32).astype(BF)
    down = lax.dot_general(hid, cot, TN, preferred_element_type=F32).astype(BF)
    for slot in range(2):
        units = slice(128 * slot, 128 * slot + 128)
        grad_gate[slot, 0, 0] = gate[:, units]
        grad_up[slot, 0, 0] = up[:, units]
        grad_down[slot] = down[units]


VM = pl.BlockSpec(memory_space=pltpu.VMEM)
SM = pl.BlockSpec(memory_space=pltpu.SMEM)
HB = pl.BlockSpec(memory_space=pltpu.HBM)


def whole(shape):
    return pl.BlockSpec(shape, lambda *_: (0,) * len(shape))


def params(mib):
    return pltpu.CompilerParams(vmem_limit_bytes=mib * 2**20)


def cost(flops, mib):
    return pl.CostEstimate(flops=int(flops), bytes_accessed=int(mib * 2**20), transcendentals=0)


def shape(dims, dtype=BF):
    return jax.ShapeDtypeStruct(dims, dtype)


def pack(sel, tokens, cotangent, extra):
    tok, wide = tokens.shape
    return pl.pallas_call(
        pack_kernel,
        in_specs=[SM, HB, HB, VM],
        out_specs=VM,
        out_shape=shape((2 * tok, wide // 2 + 128)),
        scratch_shapes=[pltpu.SemaphoreType.DMA((2 * STEPS,))],
        compiler_params=params(56),
        cost_estimate=cost(0, 2),
        name="pack",
    )(sel, tokens, cotangent, extra)


def pack_weights(sel, weights):
    width = weights[0].shape[3]
    up_spec = pl.BlockSpec((2, 1, 1, width, 128), lambda k, sel: (0, k, sel[1], 0, 0))
    down_spec = pl.BlockSpec((2, 128, width), lambda k, sel: (0, 0, 2 * k + sel[1]))
    return pl.pallas_call(
        pack_weights_kernel,
        grid_spec=pltpu.PrefetchScalarGridSpec(
            num_scalar_prefetch=1,
            grid=(STEPS,),
            in_specs=[up_spec, up_spec, down_spec],
            out_specs=pl.BlockSpec((1, 42, 128, 128), lambda k, sel: (k, 0, 0, 0)),
        ),
        out_shape=shape((STEPS, 42, 128, 128)),
        compiler_params=params(56),
        cost_estimate=cost(0, 11),
        name="pack_weights",
    )(sel, *weights)


def weight_specs(width, which):
    up_spec = pl.BlockSpec((2, 1, 1, width, 128), lambda k, sel: (0, k, sel[which], 0, 0))
    down_spec = pl.BlockSpec((2, 128, width), lambda k, sel: (0, 0, 2 * k + sel[which]))
    return [up_spec, up_spec, down_spec]


def row_specs(rows, width, first=0):
    return [pl.BlockSpec((r.shape[0], width), lambda k, sel: (0, first + k)) for r in rows]


WIDTH = 896


def near_sums(sel, own, other, weights):
    return pl.pallas_call(
        near_kernel,
        grid_spec=pltpu.PrefetchScalarGridSpec(
            num_scalar_prefetch=1,
            grid=(STEPS,),
            in_specs=row_specs(own + other, WIDTH) + weight_specs(WIDTH, 0) + weight_specs(WIDTH, 1),
            out_specs=[whole((512, 256))] * 3,
        ),
        out_shape=[shape((512, 256), F32)] * 3,
        compiler_params=params(56),
        cost_estimate=cost(0, 0.1),
        name="near_sums",
    )(sel, *own, *other, *weights, *weights)


def add_sums(name, numbers, blocks, swapped, sel, rows, weights, start=(), gains=()):
    extra = pl.BlockSpec((128, 128), lambda k, sel: (0, STEPS * WIDTH // 128))
    shapes = [shape((512, 256), F32)] * 3 + [shape((512, 128), F32)] * bool(gains)
    return pl.pallas_call(
        functools.partial(sums_kernel, numbers, blocks, swapped, bool(start), bool(gains)),
        grid_spec=pltpu.PrefetchScalarGridSpec(
            num_scalar_prefetch=1,
            grid=(STEPS,),
            in_specs=row_specs(rows, WIDTH)
            + weight_specs(WIDTH, int(swapped))
            + [whole((512, 256))] * len(start)
            + ([extra] * 8 + [whole((128, 128))] if gains else []),
            out_specs=[whole(s.shape) for s in shapes],
        ),
        out_shape=shapes,
        compiler_params=params(56),
        cost_estimate=cost(0, 0.1),
        name=name,
    )(sel, *rows, *weights, *start, *gains)


def activations(sel, other, weights, sums, gains):
    return pl.pallas_call(
        last_kernel,
        grid_spec=pltpu.PrefetchScalarGridSpec(
            num_scalar_prefetch=1,
            grid=(STEPS,),
            in_specs=row_specs(other, WIDTH)
            + weight_specs(WIDTH, 1)
            + [whole((512, 256))] * 3
            + [whole((512, 128))],
            out_specs=[whole((512, 896)), whole((512, 768))],
            scratch_shapes=[pltpu.VMEM((512, 256), F32)] * 3,
        ),
        out_shape=[shape((512, 896)), shape((512, 768))],
        compiler_params=params(56),
        cost_estimate=cost(2 * 128 * 768 * WIDTH * STEPS, 10),
        name="activations",
    )(sel, *other, *weights, *sums, gains)


def results(pieces, sel, acts, acts_other, weights, wall, half):
    return pl.pallas_call(
        functools.partial(results_kernel, pieces),
        in_specs=[SM] + [VM] * 6,
        out_specs=[VM] * len(pieces),
        out_shape=[shape((128 * len(group), half + 128)) for group in pieces],
        compiler_params=params(14),
        cost_estimate=cost(2 * 64 * sum(map(len, pieces)) * 1536 * half, 12),
        name="results",
    )(sel, acts, acts_other, *weights, wall)


def weight_grads(swapped, first, count, sel, rows, acts, before, room):
    width, half = WIDTH, WIDTH * STEPS
    at = 1 if swapped else 0
    up_spec = pl.BlockSpec((2, 1, 1, width, 128), lambda k, sel: (0, first + k, sel[at], 0, 0))
    down_spec = pl.BlockSpec((2, 128, width), lambda k, sel: (0, 0, 2 * (first + k) + sel[at]))
    up_shape = shape((2, STEPS, 2, width, 128))
    return pl.pallas_call(
        functools.partial(grads_kernel, swapped),
        grid_spec=pltpu.PrefetchScalarGridSpec(
            num_scalar_prefetch=1,
            grid=(count,),
            in_specs=row_specs(rows, width, first) + [whole((512, 768))] + [HB] * len(before),
            out_specs=[up_spec, up_spec, down_spec],
        ),
        out_shape=[up_shape, up_shape, shape((2, 128, 2 * half))],
        input_output_aliases={2 + len(rows) + i: i for i in range(len(before))},
        compiler_params=params(room),
        cost_estimate=cost(2 * 512 * 768 * width * count, 3.5 * count),
        name="weight_grads",
    )(sel, *rows, acts, *before)


def gate_weights(logits, slot_expert, chosen):
    experts = logits.shape[1]
    held = jnp.arange(experts, dtype=jnp.int32)[:, None] == slot_expert[None, :]
    picked = jnp.sum(jnp.where(held[None], logits[:, :, None], 0.0), axis=1)
    sig = jnp.where(chosen, jax.nn.sigmoid(picked), 0.0)
    return ROUTE_SCALE * sig / jnp.sum(sig, axis=1, keepdims=True)


def add(*values):
    total = values[0].astype(F32)
    for value in values[1:]:
        total = total + value.astype(F32)
    return total.astype(BF)


def per_device(tokens, cotangent, gate_logits, route_slot, slot_expert, w_gate, w_up, w_down):
    tok, wide = tokens.shape
    half = wide // 2
    width = half // STEPS
    slots = slot_expert.shape[0]
    z, core, y, x = (lax.axis_index(a) for a in AXES)
    line = y * NX + x
    sel = jnp.stack([core, 1 - core, line, 2 * (line ^ (NY * NX // 2)) + 1])
    weights = (
        w_gate.reshape(2, STEPS, 2, width, 128),
        w_up.reshape(2, STEPS, 2, width, 128),
        w_down,
    )
    high = lax.reduce_precision(gate_logits, 8, 7)
    middle = lax.reduce_precision(gate_logits - high, 8, 7)
    parts = (high, middle, gate_logits - high - middle, route_slot.astype(F32))
    extra = sum(
        lax.pad(part, 0.0, ((0, 0, 0), (24 * at, 128 - 24 * at - part.shape[1], 0)))
        for at, part in enumerate(parts)
    ).astype(BF)
    own = pack(sel, tokens, cotangent, extra)
    own, later = lax.optimization_barrier((own, sel))
    minus, plus, far = send(own, inner(1)), send(own, inner(-1)), send(own, inner(2))
    a, b = joined([own, plus]), joined([minus, far])
    a_minus, b_plus = send(a, outer(1)), send(b, outer(-1))
    b_minus, a_plus = send(b, outer(1)), send(a, outer(-1))
    a_far, b_far = send(a_minus, outer(1)), send(b_plus, outer(-1))
    wall = send(pack_weights(later, weights), other_core())

    near = [a, b, a_plus, b_plus, a_minus, b_minus]
    near_other = [send(piece, other_core()) for piece in near]
    sums = near_sums(sel, near, near_other, weights)
    (a_on, b_on), sums = lax.optimization_barrier(((a_far, b_far), sums))
    far_rows, far_other = [a_far, b_far], [send(a_on, other_core()), send(b_on, other_core())]
    rows, rows_other = near + far_rows, near_other + far_other
    experts = jnp.tile(jnp.arange(24, dtype=jnp.int32), 3)
    held = experts[:, None] == slot_expert[None, :]
    held = jnp.pad(held.astype(F32), ((0, 128 - 72), (0, 128 - slots))).astype(BF)
    *sums, gains = add_sums(
        "far_own", (6, 7), FAR_OWN, False, sel, far_rows, weights, sums, (*rows, held)
    )
    acts, acts_grad = activations(sel, far_other, weights, sums, gains)
    acts_other = send(acts, other_core())

    far_a, far_b = results(((6,), (7,)), sel, acts, acts_other, weights, wall, half)
    own_a, own_b, plus_a, plus_b, minus_b, minus_a = results(
        ((0,), (1,), (2,), (3,), (5,), (4,)), sel, acts, acts_other, weights, wall, half
    )
    own_a, acts_grad = lax.optimization_barrier((own_a, acts_grad))
    from_a, from_b = send(far_a, outer(1)), send(far_b, outer(-1))
    b_early, a_early = send(plus_b, outer(1)), send(minus_a, outer(-1))
    a_late = send(add(plus_a, from_a), outer(1))
    b_late = send(add(minus_b, from_b), outer(-1))
    grads = weight_grads(False, 0, 4, sel, rows, acts_grad, [], 52)
    grads = weight_grads(True, 0, 4, sel, rows_other, acts_grad, grads, 52)
    (a_late, b_late), grads = lax.optimization_barrier(((a_late, b_late), grads))
    keep = (own_a[:64], a_late[:64], a_early[:64])
    to_plus = add(own_a[64:], a_late[64:], a_early[64:])
    to_minus = add(own_b[:64], b_late[:64], b_early[:64])
    to_far = add(own_b[64:], b_late[64:], b_early[64:])
    total = add(
        *keep, send(to_plus, inner(1)), send(to_minus, inner(-1)), send(to_far, inner(2))
    )

    def block_for(by):
        block = lax.dynamic_slice(total, (0, (z + by) % NZ * width), (2 * tok, width))
        return joined([block, total[:, half:]], axis=1)

    last = block_for(0).astype(F32)
    for by in (1, 3, 2):
        last = last + send(block_for(by), along_z(by)).astype(F32)
    mixed, grad_tokens = last[:tok, :width].astype(BF), last[tok:, :width].astype(BF)
    home = sum(last[:tok, width + at : width + at + slots] for at in (0, slots, 2 * slots))
    chosen = jnp.any(
        route_slot[:, :, None] == jnp.arange(slots, dtype=jnp.int32)[None, None, :], axis=1
    )
    _, pull_back = jax.vjp(lambda lg: gate_weights(lg, slot_expert, chosen), gate_logits)
    grad_logits = pull_back(home)[0]
    return (
        mixed,
        grad_tokens,
        grad_logits,
        grads[0].reshape(w_gate.shape),
        grads[1].reshape(w_up.shape),
        grads[2],
    )


def solution(mesh):
    split = Mesh(mesh.devices.reshape(NZ, NC, NY, NX), AXES)
    local, group = ("y", "x"), ("z", "c")
    return jax.shard_map(
        per_device,
        mesh=split,
        in_specs=(
            P(local, None),
            P(local, None),
            P(local, None),
            P(local, None),
            P(),
            P(local, None, group),
            P(local, None, group),
            P(local, group, None),
        ),
        out_specs=(
            P(local, group),
            P(local, group),
            P(local, None),
            P(local, None, group),
            P(local, None, group),
            P(local, group, None),
        ),
        check_vma=False,
    )
```

```python
import functools

import jax
import jax.numpy as jnp
from jax import lax
from jax.experimental import pallas as pl
from jax.experimental.pallas import tpu as pltpu
from jax.sharding import Mesh
from jax.sharding import PartitionSpec as P

ROUTE_SCALE = 2.5
TOP = 8
ROUTE = 3 * 24
NZ, NC, NY, NX = 4, 2, 4, 4
AXES = ("z", "c", "y", "x")
STEPS = 4
BF, F32 = jnp.bfloat16, jnp.float32
NT = (((1,), (1,)), ((), ()))
TN = (((0,), (0,)), ((), ()))
RING = (0, 1, 3, 2)


def moves(step):
    pairs = []
    for z in range(NZ):
        for c in range(NC):
            for y in range(NY):
                for x in range(NX):
                    z2, c2, y2, x2 = step(z, c, y, x)
                    source = ((z * NC + c) * NY + y) * NX + x
                    target = ((z2 % NZ * NC + c2 % NC) * NY + y2 % NY) * NX + x2 % NX
                    pairs.append((source, target))
    return pairs


def outer(by):
    return moves(lambda z, c, y, x: (z, c, y + by, x) if c == 0 else (z, c, y, x + by))


def inner(by):
    return moves(lambda z, c, y, x: (z, c, y, x + by) if c == 0 else (z, c, y + by, x))


def along_z(by):
    return moves(lambda z, c, y, x: (z + by, c, y, x))


def other_core():
    return moves(lambda z, c, y, x: (z, c + 1, y, x))


def send(value, pairs):
    return lax.ppermute(value, AXES, pairs)


def joined(parts, axis=0):
    return jnp.concatenate(parts, axis=axis)


def rows_of(refs, blocks, second):
    parts = []
    for outer_at, inner_at in blocks:
        row = 64 * (inner_at % 2) + (32 if second else 0)
        parts.append(refs[2 * outer_at + inner_at // 2][row : row + 32, :])
    return joined(parts)


def turned(blocks):
    return [(b, a) for a, b in blocks]


ALL = [(a, b) for a in range(4) for b in range(4)]
NEAR_OWN = [(a, b) for a in range(3) for b in range(4)]
FAR_OWN = [(3, b) for b in range(4)]
NEAR_OTHER = [(a, b) for a in range(4) for b in range(3)]
FAR_OTHER = [(a, 3) for a in range(4)]


def pair(first, second):
    return joined([first, second], axis=1)


def weight_block(wg, wu, wd):
    gate, up = (pair(ref[0, 0, 0], ref[1, 0, 0]) for ref in (wg, wu))
    return gate, up, wd[...].reshape(-1, wd.shape[2])


def up_block(ref, k, half):
    return pair(ref[0, k, half], ref[1, k, half])


def down_block(ref, k, half, width):
    at = pl.multiple_of((2 * k + half) * width, 128)
    return ref[:, :, pl.ds(at, width)].reshape(-1, width)


def products(tok, cot, gate, up, down):
    first = jnp.dot(tok, gate, preferred_element_type=F32)
    second = jnp.dot(tok, up, preferred_element_type=F32)
    back = lax.dot_general(cot, down, NT, preferred_element_type=F32)
    return first, second, back


def pack_kernel(sel, tok, cot, logits, routes, packed, sems):
    rows, half = tok.shape[0], packed.shape[1] - 128
    width = half // STEPS
    copies = []
    for k in range(STEPS):
        at = pl.multiple_of((2 * k + sel[0]) * width, 128)
        for base, ref in enumerate((tok, cot)):
            target = packed.at[pl.ds(base * rows, rows), pl.ds(k * width, width)]
            copies.append(
                pltpu.make_async_copy(ref.at[:, pl.ds(at, width)], target, sems.at[len(copies)])
            )
            copies[-1].start()
    experts = logits.shape[0]
    high, middle, low = thirds(logits[...])
    extra = jnp.zeros((rows, 128), F32)
    for at, part in enumerate((high, middle, low, routes[...].astype(F32))):
        lane = lax.broadcasted_iota(jnp.int32, (part.shape[0], 128), 1)
        row = lax.broadcasted_iota(jnp.int32, (part.shape[0], 128), 0)
        here = jnp.where(lane == row + experts * at, 1.0, 0.0).astype(BF)
        extra += lax.dot_general(part.astype(BF), here, TN, preferred_element_type=F32)
    packed[:rows, half:] = extra.astype(BF)
    packed[rows:, half:] = jnp.zeros((rows, 128), BF)
    for one in copies:
        one.wait()


def pack_weights_kernel(sel, wg, wu, wd, wall):
    for base, ref in ((0, wg), (14, wu)):
        for slot in range(2):
            at = base + 7 * slot
            wall[0, at : at + 7] = ref[slot, 0, 0].reshape(7, 128, 128)
    for q in range(7):
        wall[0, 28 + 2 * q : 30 + 2 * q] = wd[:, :, 128 * q : 128 * q + 128]


def multiply(sums, rows, weights, blocks, swapped):
    where = turned(blocks) if swapped else blocks
    parts = products(
        rows_of(rows, where, False), rows_of(rows, where, True), *weight_block(*weights)
    )
    for ref, part in zip(sums, parts):
        for outer_at in sorted({o for o, _ in blocks}):
            inners = [i for o, i in blocks if o == outer_at]
            low = 32 * blocks.index((outer_at, inners[0]))
            to = 32 * (4 * outer_at + inners[0])
            ref[to : to + 32 * len(inners)] += part[low : low + 32 * len(inners)]


def near_kernel(sel, *refs):
    own, other, mine, theirs, sums = refs[:6], refs[6:12], refs[12:15], refs[15:18], refs[18:21]

    @pl.when(pl.program_id(0) == 0)
    def _():
        for ref in sums:
            ref[...] = jnp.zeros_like(ref)

    multiply(sums, own, mine, NEAR_OWN, False)
    multiply(sums, other, theirs, NEAR_OTHER, True)


def line_weights(extra, held, sel, gains):
    rows = rows_of(extra, ALL, False)
    picked = jnp.dot(rows, held[...], preferred_element_type=F32)
    lane = lax.broadcasted_iota(jnp.int32, picked.shape, 1)
    slot = lane.astype(F32)
    chosen = slot < 0
    for at in range(TOP):
        chosen = chosen | (slot == rows[:, ROUTE + at : ROUTE + at + 1].astype(F32))
    sig = jnp.where(chosen, jax.nn.sigmoid(picked), 0.0)
    weight = ROUTE_SCALE * sig / jnp.sum(sig, axis=1, keepdims=True)

    def column(at):
        return jnp.sum(jnp.where(lane == at, weight, 0.0), axis=1, keepdims=True)

    cold, hot, partner = column(2 * sel[2]), column(2 * sel[2] + 1), column(sel[3])
    gains[...] = jnp.where(lane == 0, cold, jnp.where(lane == 1, hot, hot + partner))


def thirds(value):
    high = value.astype(BF).astype(F32)
    middle = (value - high).astype(BF).astype(F32)
    return high, middle, value - high - middle


def far_kernel(sel, *refs):
    own, other = dict(zip((6, 7), refs)), dict(zip((6, 7), refs[2:]))
    mine, theirs, start, extra, held = refs[4:7], refs[7:10], refs[10:13], refs[13:21], refs[21]
    acts, acts_grad = refs[22:24]
    sums, gains = refs[24:27], refs[27]

    @pl.when(pl.program_id(0) == 0)
    def _():
        for ref, before in zip(sums, start):
            ref[...] = before[...]
        line_weights(extra, held, sel, gains)

    multiply(sums, own, mine, FAR_OWN, False)
    multiply(sums, other, theirs, FAR_OTHER, True)

    @pl.when(pl.program_id(0) == STEPS - 1)
    def _():
        finish(sums, gains, acts, acts_grad)


def finish(sums, gains, acts, acts_grad):
    lane = lax.broadcasted_iota(jnp.int32, (512, 128), 1)
    dots = jnp.zeros((512, 128), F32)
    for slot in range(2):
        units = slice(128 * slot, 128 * slot + 128)
        first, second, back = (ref[:, units] for ref in sums)
        mine = gains[:, slot : slot + 1]
        both = gains[:, 2 * slot : 2 * slot + 1]
        sig = jax.nn.sigmoid(first)
        silu = first * sig
        hidden = silu * second
        for at, part in enumerate(thirds(jnp.sum(hidden * back, axis=1, keepdims=True))):
            dots = jnp.where(lane == 2 * at + slot, part, dots)
        d_first = back * second * sig * (1.0 + first * (1.0 - sig))
        d_second = back * silu
        for at, value in ((0, hidden), (256, d_first), (512, d_second)):
            units = slice(at + 128 * slot, at + 128 * slot + 128)
            acts[:, units] = (value * mine).astype(BF)
            acts_grad[:, units] = (value * both).astype(BF)
    acts[:, 768:] = dots.astype(BF)


def results_kernel(pieces, sel, acts, acts_other, wg, wu, wd, wall, *outs):
    half = sel[0]
    blocks = [(p // 2, 2 * (p % 2) + b) for group in pieces for p in group for b in range(2)]
    places = [(at, 64 * row) for at, group in enumerate(pieces) for row in range(2 * len(group))]
    own = joined([acts[32 * (4 * a + b) : 32 * (4 * a + b) + 32, :] for a, b in blocks])
    other = joined([acts_other[32 * (4 * b + a) : 32 * (4 * b + a) + 32, :] for a, b in blocks])
    hidden = pair(own[:, :256], other[:, :256])
    grads = pair(own[:, 256:768], other[:, 256:768])
    total = outs[0].shape[1] - 128
    width = total // STEPS
    lane = lax.broadcasted_iota(jnp.int32, (own.shape[0], 128), 1)
    dots = jnp.zeros((own.shape[0], 128), F32)
    last = own[:, 768:].astype(F32) + other[:, 768:].astype(F32)
    for slot in range(2):
        mine = jnp.sum(jnp.where((lane < 6) & (lane % 2 == slot), last, 0.0), axis=1, keepdims=True)
        for at, part in enumerate(thirds(mine)):
            dots = jnp.where(lane == 32 * at + 2 * sel[2] + slot, part, dots)
    for block, (at, row) in enumerate(places):
        outs[at][row : row + 32, total:] = dots[32 * block : 32 * block + 32].astype(BF)
        outs[at][row + 32 : row + 64, total:] = jnp.zeros((32, 128), BF)
    for k in range(STEPS):
        cols = slice(k * width, k * width + width)
        down = joined([wall[k, 28 + 2 * q : 30 + 2 * q].reshape(256, 128) for q in range(7)], axis=1)
        down = joined([down_block(wd, k, half, width), down])
        up = [up_block(wg, k, half), up_block(wu, k, half)]
        up += [wall[k, at : at + 7].reshape(width, 128) for at in (0, 7, 14, 21)]
        out = jnp.dot(hidden, down, preferred_element_type=F32)
        grad = lax.dot_general(grads, joined(up, axis=1), NT, preferred_element_type=F32)
        for block, (at, row) in enumerate(places):
            here = slice(32 * block, 32 * block + 32)
            outs[at][row : row + 32, cols] = out[here].astype(BF)
            outs[at][row + 32 : row + 64, cols] = grad[here].astype(BF)


def grads_kernel(swapped, sel, *refs):
    rows, acts = refs[:8], refs[8]
    grad_gate, grad_up, grad_down = refs[-3:]
    blocks = turned(ALL) if swapped else ALL
    tok, cot = rows_of(rows, blocks, False), rows_of(rows, blocks, True)
    hid, d1, d2 = acts[:, :256], acts[:, 256:512], acts[:, 512:768]
    gate = lax.dot_general(tok, d1, TN, preferred_element_type=F32).astype(BF)
    up = lax.dot_general(tok, d2, TN, preferred_element_type=F32).astype(BF)
    down = lax.dot_general(hid, cot, TN, preferred_element_type=F32).astype(BF)
    for slot in range(2):
        units = slice(128 * slot, 128 * slot + 128)
        grad_gate[slot, 0, 0] = gate[:, units]
        grad_up[slot, 0, 0] = up[:, units]
        grad_down[slot] = down[units]


VM = pl.BlockSpec(memory_space=pltpu.VMEM)
SM = pl.BlockSpec(memory_space=pltpu.SMEM)
HB = pl.BlockSpec(memory_space=pltpu.HBM)


def whole(shape):
    return pl.BlockSpec(shape, lambda *_: (0,) * len(shape))


def params(mib):
    return pltpu.CompilerParams(vmem_limit_bytes=mib * 2**20)


def cost(flops, mib):
    return pl.CostEstimate(flops=int(flops), bytes_accessed=int(mib * 2**20), transcendentals=0)


def shape(dims, dtype=BF):
    return jax.ShapeDtypeStruct(dims, dtype)


def pack(sel, tokens, cotangent, logits, routes):
    tok, wide = tokens.shape
    return pl.pallas_call(
        pack_kernel,
        in_specs=[SM, HB, HB, VM, VM],
        out_specs=VM,
        out_shape=shape((2 * tok, wide // 2 + 128)),
        scratch_shapes=[pltpu.SemaphoreType.DMA((2 * STEPS,))],
        compiler_params=params(56),
        cost_estimate=cost(0, 2),
        name="pack",
    )(sel, tokens, cotangent, logits.T, routes.T)


def pack_weights(sel, weights):
    width = weights[0].shape[3]
    up_spec = pl.BlockSpec((2, 1, 1, width, 128), lambda k, sel: (0, k, sel[1], 0, 0))
    down_spec = pl.BlockSpec((2, 128, width), lambda k, sel: (0, 0, 2 * k + sel[1]))
    return pl.pallas_call(
        pack_weights_kernel,
        grid_spec=pltpu.PrefetchScalarGridSpec(
            num_scalar_prefetch=1,
            grid=(STEPS,),
            in_specs=[up_spec, up_spec, down_spec],
            out_specs=pl.BlockSpec((1, 42, 128, 128), lambda k, sel: (k, 0, 0, 0)),
        ),
        out_shape=shape((STEPS, 42, 128, 128)),
        compiler_params=params(56),
        cost_estimate=cost(0, 11),
        name="pack_weights",
    )(sel, *weights)


def weight_specs(width, which):
    up_spec = pl.BlockSpec((2, 1, 1, width, 128), lambda k, sel: (0, k, sel[which], 0, 0))
    down_spec = pl.BlockSpec((2, 128, width), lambda k, sel: (0, 0, 2 * k + sel[which]))
    return [up_spec, up_spec, down_spec]


def row_specs(rows, width, first=0):
    return [pl.BlockSpec((r.shape[0], width), lambda k, sel: (0, first + k)) for r in rows]


WIDTH = 896


def near_sums(sel, own, other, weights):
    return pl.pallas_call(
        near_kernel,
        grid_spec=pltpu.PrefetchScalarGridSpec(
            num_scalar_prefetch=1,
            grid=(STEPS,),
            in_specs=row_specs(own + other, WIDTH) + weight_specs(WIDTH, 0) + weight_specs(WIDTH, 1),
            out_specs=[whole((512, 256))] * 3,
        ),
        out_shape=[shape((512, 256), F32)] * 3,
        compiler_params=params(56),
        cost_estimate=cost(0, 0.1),
        name="near_sums",
    )(sel, *own, *other, *weights, *weights)


def activations(sel, own, other, weights, sums, held):
    extra = pl.BlockSpec((128, 128), lambda k, sel: (0, STEPS * WIDTH // 128))
    return pl.pallas_call(
        far_kernel,
        grid_spec=pltpu.PrefetchScalarGridSpec(
            num_scalar_prefetch=1,
            grid=(STEPS,),
            in_specs=row_specs(own[6:] + other, WIDTH)
            + weight_specs(WIDTH, 0)
            + weight_specs(WIDTH, 1)
            + [whole((512, 256))] * 3
            + [extra] * 8
            + [whole((128, 128))],
            out_specs=[whole((512, 896)), whole((512, 768))],
            scratch_shapes=[pltpu.VMEM((512, 256), F32)] * 3 + [pltpu.VMEM((512, 128), F32)],
        ),
        out_shape=[shape((512, 896)), shape((512, 768))],
        compiler_params=params(56),
        cost_estimate=cost(4 * 128 * 768 * WIDTH * STEPS, 15),
        name="activations",
    )(sel, *own[6:], *other, *weights, *weights, *sums, *own, held)


def results(pieces, sel, acts, acts_other, weights, wall, half):
    return pl.pallas_call(
        functools.partial(results_kernel, pieces),
        in_specs=[SM] + [VM] * 6,
        out_specs=[VM] * len(pieces),
        out_shape=[shape((128 * len(group), half + 128)) for group in pieces],
        compiler_params=params(14),
        cost_estimate=cost(2 * 64 * sum(map(len, pieces)) * 1536 * half, 12),
        name="results",
    )(sel, acts, acts_other, *weights, wall)


def weight_grads(swapped, first, count, sel, rows, acts, before, room):
    width, half = WIDTH, WIDTH * STEPS
    at = 1 if swapped else 0
    up_spec = pl.BlockSpec((2, 1, 1, width, 128), lambda k, sel: (0, first + k, sel[at], 0, 0))
    down_spec = pl.BlockSpec((2, 128, width), lambda k, sel: (0, 0, 2 * (first + k) + sel[at]))
    up_shape = shape((2, STEPS, 2, width, 128))
    return pl.pallas_call(
        functools.partial(grads_kernel, swapped),
        grid_spec=pltpu.PrefetchScalarGridSpec(
            num_scalar_prefetch=1,
            grid=(count,),
            in_specs=row_specs(rows, width, first) + [whole((512, 768))] + [HB] * len(before),
            out_specs=[up_spec, up_spec, down_spec],
        ),
        out_shape=[up_shape, up_shape, shape((2, 128, 2 * half))],
        input_output_aliases={2 + len(rows) + i: i for i in range(len(before))},
        compiler_params=params(room),
        cost_estimate=cost(2 * 512 * 768 * width * count, 3.5 * count),
        name="weight_grads",
    )(sel, *rows, acts, *before)


def gate_weights(logits, slot_expert, chosen):
    experts = logits.shape[1]
    held = jnp.arange(experts, dtype=jnp.int32)[:, None] == slot_expert[None, :]
    picked = jnp.sum(jnp.where(held[None], logits[:, :, None], 0.0), axis=1)
    sig = jnp.where(chosen, jax.nn.sigmoid(picked), 0.0)
    return ROUTE_SCALE * sig / jnp.sum(sig, axis=1, keepdims=True)


def add(*values):
    total = values[0].astype(F32)
    for value in values[1:]:
        total = total + value.astype(F32)
    return total.astype(BF)


def per_device(tokens, cotangent, gate_logits, route_slot, slot_expert, w_gate, w_up, w_down):
    tok, wide = tokens.shape
    half = wide // 2
    width = half // STEPS
    slots = slot_expert.shape[0]
    z, core, y, x = (lax.axis_index(a) for a in AXES)
    line = y * NX + x
    sel = jnp.stack([core, 1 - core, line, 2 * (line ^ (NY * NX // 2)) + 1])
    weights = (
        w_gate.reshape(2, STEPS, 2, width, 128),
        w_up.reshape(2, STEPS, 2, width, 128),
        w_down,
    )
    own = pack(sel, tokens, cotangent, gate_logits, route_slot)
    own, later = lax.optimization_barrier((own, sel))
    minus, plus, far = send(own, inner(1)), send(own, inner(-1)), send(own, inner(2))
    a, b = joined([own, plus]), joined([minus, far])
    a_minus, b_plus = send(a, outer(1)), send(b, outer(-1))
    b_minus, a_plus = send(b, outer(1)), send(a, outer(-1))
    a_far, b_far = send(a_minus, outer(1)), send(b_plus, outer(-1))
    wall = send(pack_weights(later, weights), other_core())

    near = [a, b, a_plus, b_plus, a_minus, b_minus]
    near_other = [send(piece, other_core()) for piece in near]
    sums = near_sums(sel, near, near_other, weights)
    (a_on, b_on), sums = lax.optimization_barrier(((a_far, b_far), sums))
    far_rows, far_other = [a_far, b_far], [send(a_on, other_core()), send(b_on, other_core())]
    rows, rows_other = near + far_rows, near_other + far_other
    experts = jnp.tile(jnp.arange(24, dtype=jnp.int32), 3)
    held = experts[:, None] == slot_expert[None, :]
    held = jnp.pad(held.astype(F32), ((0, 128 - 72), (0, 128 - slots))).astype(BF)
    acts, acts_grad = activations(sel, rows, far_other, weights, sums, held)
    acts_other = send(acts, other_core())

    far_a, far_b = results(((6,), (7,)), sel, acts, acts_other, weights, wall, half)
    own_a, own_b, plus_a, plus_b, minus_b, minus_a = results(
        ((0,), (1,), (2,), (3,), (5,), (4,)), sel, acts, acts_other, weights, wall, half
    )
    own_a, acts_grad = lax.optimization_barrier((own_a, acts_grad))
    from_a, from_b = send(far_a, outer(1)), send(far_b, outer(-1))
    b_early, a_early = send(plus_b, outer(1)), send(minus_a, outer(-1))
    a_late = send(add(plus_a, from_a), outer(1))
    b_late = send(add(minus_b, from_b), outer(-1))
    grads = weight_grads(False, 0, 4, sel, rows, acts_grad, [], 52)
    grads = weight_grads(True, 0, 4, sel, rows_other, acts_grad, grads, 52)
    (a_late, b_late), grads = lax.optimization_barrier(((a_late, b_late), grads))
    keep = (own_a[:64], a_late[:64], a_early[:64])
    to_plus = add(own_a[64:], a_late[64:], a_early[64:])
    to_minus = add(own_b[:64], b_late[:64], b_early[:64])
    to_far = add(own_b[64:], b_late[64:], b_early[64:])
    total = add(
        *keep, send(to_plus, inner(1)), send(to_minus, inner(-1)), send(to_far, inner(2))
    )

    def block_for(by):
        block = lax.dynamic_slice(total, (0, (z + by) % NZ * width), (2 * tok, width))
        return joined([block, total[:, half:]], axis=1)

    last = block_for(0).astype(F32)
    for by in (1, 3, 2):
        last = last + send(block_for(by), along_z(by)).astype(F32)
    mixed, grad_tokens = last[:tok, :width].astype(BF), last[tok:, :width].astype(BF)
    home = sum(last[:tok, width + at : width + at + slots] for at in (0, slots, 2 * slots))
    chosen = jnp.any(
        route_slot[:, :, None] == jnp.arange(slots, dtype=jnp.int32)[None, None, :], axis=1
    )
    _, pull_back = jax.vjp(lambda lg: gate_weights(lg, slot_expert, chosen), gate_logits)
    grad_logits = pull_back(home)[0]
    return (
        mixed,
        grad_tokens,
        grad_logits,
        grads[0].reshape(w_gate.shape),
        grads[1].reshape(w_up.shape),
        grads[2],
    )


def solution(mesh):
    split = Mesh(mesh.devices.reshape(NZ, NC, NY, NX), AXES)
    local, group = ("y", "x"), ("z", "c")
    return jax.shard_map(
        per_device,
        mesh=split,
        in_specs=(
            P(local, None),
            P(local, None),
            P(local, None),
            P(local, None),
            P(),
            P(local, None, group),
            P(local, None, group),
            P(local, group, None),
        ),
        out_specs=(
            P(local, group),
            P(local, group),
            P(local, None),
            P(local, None, group),
            P(local, None, group),
            P(local, group, None),
        ),
        check_vma=False,
    )
```

```python
import functools

import jax
import jax.numpy as jnp
from jax import lax
from jax.experimental import pallas as pl
from jax.experimental.pallas import tpu as pltpu
from jax.sharding import Mesh
from jax.sharding import PartitionSpec as P

ROUTE_SCALE = 2.5
TOP = 8
ROUTE = 3 * 24
NZ, NC, NY, NX = 4, 2, 4, 4
AXES = ("z", "c", "y", "x")
STEPS = 4
BF, F32 = jnp.bfloat16, jnp.float32
NT = (((1,), (1,)), ((), ()))
TN = (((0,), (0,)), ((), ()))
RING = (0, 1, 3, 2)


def moves(step):
    pairs = []
    for z in range(NZ):
        for c in range(NC):
            for y in range(NY):
                for x in range(NX):
                    z2, c2, y2, x2 = step(z, c, y, x)
                    source = ((z * NC + c) * NY + y) * NX + x
                    target = ((z2 % NZ * NC + c2 % NC) * NY + y2 % NY) * NX + x2 % NX
                    pairs.append((source, target))
    return pairs


def outer(by):
    return moves(lambda z, c, y, x: (z, c, y + by, x) if c == 0 else (z, c, y, x + by))


def inner(by):
    return moves(lambda z, c, y, x: (z, c, y, x + by) if c == 0 else (z, c, y + by, x))


def along_z(by):
    return moves(lambda z, c, y, x: (z + by, c, y, x))


def other_core():
    return moves(lambda z, c, y, x: (z, c + 1, y, x))


def send(value, pairs):
    return lax.ppermute(value, AXES, pairs)


def joined(parts, axis=0):
    return jnp.concatenate(parts, axis=axis)


def rows_of(refs, blocks, second):
    parts = []
    for outer_at, inner_at in blocks:
        row = 64 * (inner_at % 2) + (32 if second else 0)
        parts.append(refs[2 * outer_at + inner_at // 2][row : row + 32, :])
    return joined(parts)


def turned(blocks):
    return [(b, a) for a, b in blocks]


ALL = [(a, b) for a in range(4) for b in range(4)]
NEAR_OWN = [(a, b) for a in range(3) for b in range(4)]
FAR_OWN = [(3, b) for b in range(4)]
NEAR_OTHER = [(a, b) for a in range(4) for b in range(3)]
FAR_OTHER = [(a, 3) for a in range(4)]


def pair(first, second):
    return joined([first, second], axis=1)


def weight_block(wg, wu, wd):
    gate, up = (pair(ref[0, 0, 0], ref[1, 0, 0]) for ref in (wg, wu))
    return gate, up, wd[...].reshape(-1, wd.shape[2])


def up_block(ref, k, half):
    return pair(ref[0, k, half], ref[1, k, half])


def down_block(ref, k, half, width):
    at = pl.multiple_of((2 * k + half) * width, 128)
    return ref[:, :, pl.ds(at, width)].reshape(-1, width)


def products(tok, cot, gate, up, down):
    first = jnp.dot(tok, gate, preferred_element_type=F32)
    second = jnp.dot(tok, up, preferred_element_type=F32)
    back = lax.dot_general(cot, down, NT, preferred_element_type=F32)
    return first, second, back


def pack_kernel(sel, tok, cot, logits, routes, packed, sems):
    rows, half = tok.shape[0], packed.shape[1] - 128
    width = half // STEPS
    copies = []
    for k in range(STEPS):
        at = pl.multiple_of((2 * k + sel[0]) * width, 128)
        for base, ref in enumerate((tok, cot)):
            target = packed.at[pl.ds(base * rows, rows), pl.ds(k * width, width)]
            copies.append(
                pltpu.make_async_copy(ref.at[:, pl.ds(at, width)], target, sems.at[len(copies)])
            )
            copies[-1].start()
    experts = logits.shape[0]
    high, middle, low = thirds(logits[...])
    extra = jnp.zeros((rows, 128), F32)
    for at, part in enumerate((high, middle, low, routes[...].astype(F32))):
        lane = lax.broadcasted_iota(jnp.int32, (part.shape[0], 128), 1)
        row = lax.broadcasted_iota(jnp.int32, (part.shape[0], 128), 0)
        here = jnp.where(lane == row + experts * at, 1.0, 0.0).astype(BF)
        extra += lax.dot_general(part.astype(BF), here, TN, preferred_element_type=F32)
    packed[:rows, half:] = extra.astype(BF)
    packed[rows:, half:] = jnp.zeros((rows, 128), BF)
    for one in copies:
        one.wait()


def pack_weights_kernel(sel, wg, wu, wd, wall):
    for base, ref in ((0, wg), (14, wu)):
        for slot in range(2):
            at = base + 7 * slot
            wall[0, at : at + 7] = ref[slot, 0, 0].reshape(7, 128, 128)
    for q in range(7):
        wall[0, 28 + 2 * q : 30 + 2 * q] = wd[:, :, 128 * q : 128 * q + 128]


def multiply(sums, rows, weights, blocks, swapped):
    where = turned(blocks) if swapped else blocks
    parts = products(
        rows_of(rows, where, False), rows_of(rows, where, True), *weight_block(*weights)
    )
    for ref, part in zip(sums, parts):
        for outer_at in sorted({o for o, _ in blocks}):
            inners = [i for o, i in blocks if o == outer_at]
            low = 32 * blocks.index((outer_at, inners[0]))
            to = 32 * (4 * outer_at + inners[0])
            ref[to : to + 32 * len(inners)] += part[low : low + 32 * len(inners)]


def near_kernel(sel, *refs):
    own, other, mine, theirs, sums = refs[:6], refs[6:12], refs[12:15], refs[15:18], refs[18:21]

    @pl.when(pl.program_id(0) == 0)
    def _():
        for ref in sums:
            ref[...] = jnp.zeros_like(ref)

    multiply(sums, own, mine, NEAR_OWN, False)
    multiply(sums, other, theirs, NEAR_OTHER, True)


def line_weights(extra, held, sel, gains):
    rows = rows_of(extra, ALL, False)
    picked = jnp.dot(rows, held[...], preferred_element_type=F32)
    lane = lax.broadcasted_iota(jnp.int32, picked.shape, 1)
    slot = lane.astype(F32)
    chosen = slot < 0
    for at in range(TOP):
        chosen = chosen | (slot == rows[:, ROUTE + at : ROUTE + at + 1].astype(F32))
    sig = jnp.where(chosen, jax.nn.sigmoid(picked), 0.0)
    weight = ROUTE_SCALE * sig / jnp.sum(sig, axis=1, keepdims=True)

    def column(at):
        return jnp.sum(jnp.where(lane == at, weight, 0.0), axis=1, keepdims=True)

    cold, hot, partner = column(2 * sel[2]), column(2 * sel[2] + 1), column(sel[3])
    gains[...] = jnp.where(lane == 0, cold, jnp.where(lane == 1, hot, hot + partner))


def thirds(value):
    high = value.astype(BF).astype(F32)
    middle = (value - high).astype(BF).astype(F32)
    return high, middle, value - high - middle


def far_kernel(sel, *refs):
    own, other = dict(zip((6, 7), refs)), dict(zip((6, 7), refs[2:]))
    mine, theirs, start, extra, held = refs[4:7], refs[7:10], refs[10:13], refs[13:21], refs[21]
    acts, acts_grad = refs[22:24]
    sums, gains = refs[24:27], refs[27]

    @pl.when(pl.program_id(0) == 0)
    def _():
        for ref, before in zip(sums, start):
            ref[...] = before[...]
        line_weights(extra, held, sel, gains)

    multiply(sums, own, mine, FAR_OWN, False)
    multiply(sums, other, theirs, FAR_OTHER, True)

    @pl.when(pl.program_id(0) == STEPS - 1)
    def _():
        finish(sums, gains, acts, acts_grad)


def finish(sums, gains, acts, acts_grad):
    lane = lax.broadcasted_iota(jnp.int32, (512, 128), 1)
    dots = jnp.zeros((512, 128), F32)
    for slot in range(2):
        units = slice(128 * slot, 128 * slot + 128)
        first, second, back = (ref[:, units] for ref in sums)
        mine = gains[:, slot : slot + 1]
        both = gains[:, 2 * slot : 2 * slot + 1]
        sig = jax.nn.sigmoid(first)
        silu = first * sig
        hidden = silu * second
        for at, part in enumerate(thirds(jnp.sum(hidden * back, axis=1, keepdims=True))):
            dots = jnp.where(lane == 2 * at + slot, part, dots)
        d_first = back * second * sig * (1.0 + first * (1.0 - sig))
        d_second = back * silu
        for at, value in ((0, hidden), (256, d_first), (512, d_second)):
            units = slice(at + 128 * slot, at + 128 * slot + 128)
            acts[:, units] = (value * mine).astype(BF)
            acts_grad[:, units] = (value * both).astype(BF)
    acts[:, 768:] = dots.astype(BF)


def results_kernel(pieces, sel, acts, acts_other, wg, wu, wd, wall, *outs):
    half = sel[0]
    blocks = [(p // 2, 2 * (p % 2) + b) for group in pieces for p in group for b in range(2)]
    places = [(at, 64 * row) for at, group in enumerate(pieces) for row in range(2 * len(group))]
    own = joined([acts[32 * (4 * a + b) : 32 * (4 * a + b) + 32, :] for a, b in blocks])
    other = joined([acts_other[32 * (4 * b + a) : 32 * (4 * b + a) + 32, :] for a, b in blocks])
    hidden = pair(own[:, :256], other[:, :256])
    grads = pair(own[:, 256:768], other[:, 256:768])
    total = outs[0].shape[1] - 128
    width = total // STEPS
    lane = lax.broadcasted_iota(jnp.int32, (own.shape[0], 128), 1)
    dots = jnp.zeros((own.shape[0], 128), F32)
    last = own[:, 768:].astype(F32) + other[:, 768:].astype(F32)
    for slot in range(2):
        mine = jnp.sum(jnp.where((lane < 6) & (lane % 2 == slot), last, 0.0), axis=1, keepdims=True)
        for at, part in enumerate(thirds(mine)):
            dots = jnp.where(lane == 32 * at + 2 * sel[2] + slot, part, dots)
    for block, (at, row) in enumerate(places):
        outs[at][row : row + 32, total:] = dots[32 * block : 32 * block + 32].astype(BF)
        outs[at][row + 32 : row + 64, total:] = jnp.zeros((32, 128), BF)
    for k in range(STEPS):
        cols = slice(k * width, k * width + width)
        down = joined([wall[k, 28 + 2 * q : 30 + 2 * q].reshape(256, 128) for q in range(7)], axis=1)
        down = joined([down_block(wd, k, half, width), down])
        up = [up_block(wg, k, half), up_block(wu, k, half)]
        up += [wall[k, at : at + 7].reshape(width, 128) for at in (0, 7, 14, 21)]
        out = jnp.dot(hidden, down, preferred_element_type=F32)
        grad = lax.dot_general(grads, joined(up, axis=1), NT, preferred_element_type=F32)
        for block, (at, row) in enumerate(places):
            here = slice(32 * block, 32 * block + 32)
            outs[at][row : row + 32, cols] = out[here].astype(BF)
            outs[at][row + 32 : row + 64, cols] = grad[here].astype(BF)


def grads_kernel(swapped, sel, *refs):
    rows, acts = refs[:8], refs[8]
    grad_gate, grad_up, grad_down = refs[-3:]
    blocks = turned(ALL) if swapped else ALL
    tok, cot = rows_of(rows, blocks, False), rows_of(rows, blocks, True)
    hid, d1, d2 = acts[:, :256], acts[:, 256:512], acts[:, 512:768]
    gate = lax.dot_general(tok, d1, TN, preferred_element_type=F32).astype(BF)
    up = lax.dot_general(tok, d2, TN, preferred_element_type=F32).astype(BF)
    down = lax.dot_general(hid, cot, TN, preferred_element_type=F32).astype(BF)
    for slot in range(2):
        units = slice(128 * slot, 128 * slot + 128)
        grad_gate[slot, 0, 0] = gate[:, units]
        grad_up[slot, 0, 0] = up[:, units]
        grad_down[slot] = down[units]


VM = pl.BlockSpec(memory_space=pltpu.VMEM)
SM = pl.BlockSpec(memory_space=pltpu.SMEM)
HB = pl.BlockSpec(memory_space=pltpu.HBM)


def whole(shape):
    return pl.BlockSpec(shape, lambda *_: (0,) * len(shape))


def params(mib):
    return pltpu.CompilerParams(vmem_limit_bytes=mib * 2**20)


def cost(flops, mib):
    return pl.CostEstimate(flops=int(flops), bytes_accessed=int(mib * 2**20), transcendentals=0)


def shape(dims, dtype=BF):
    return jax.ShapeDtypeStruct(dims, dtype)


def pack(sel, tokens, cotangent, logits, routes):
    tok, wide = tokens.shape
    return pl.pallas_call(
        pack_kernel,
        in_specs=[SM, HB, HB, VM, VM],
        out_specs=VM,
        out_shape=shape((2 * tok, wide // 2 + 128)),
        scratch_shapes=[pltpu.SemaphoreType.DMA((2 * STEPS,))],
        compiler_params=params(56),
        cost_estimate=cost(0, 2),
        name="pack",
    )(sel, tokens, cotangent, logits.T, routes.T)


def pack_weights(sel, weights):
    width = weights[0].shape[3]
    up_spec = pl.BlockSpec((2, 1, 1, width, 128), lambda k, sel: (0, k, sel[1], 0, 0))
    down_spec = pl.BlockSpec((2, 128, width), lambda k, sel: (0, 0, 2 * k + sel[1]))
    return pl.pallas_call(
        pack_weights_kernel,
        grid_spec=pltpu.PrefetchScalarGridSpec(
            num_scalar_prefetch=1,
            grid=(STEPS,),
            in_specs=[up_spec, up_spec, down_spec],
            out_specs=pl.BlockSpec((1, 42, 128, 128), lambda k, sel: (k, 0, 0, 0)),
        ),
        out_shape=shape((STEPS, 42, 128, 128)),
        compiler_params=params(56),
        cost_estimate=cost(0, 11),
        name="pack_weights",
    )(sel, *weights)


def weight_specs(width, which):
    up_spec = pl.BlockSpec((2, 1, 1, width, 128), lambda k, sel: (0, k, sel[which], 0, 0))
    down_spec = pl.BlockSpec((2, 128, width), lambda k, sel: (0, 0, 2 * k + sel[which]))
    return [up_spec, up_spec, down_spec]


def row_specs(rows, width, first=0):
    return [pl.BlockSpec((r.shape[0], width), lambda k, sel: (0, first + k)) for r in rows]


WIDTH = 896


def near_sums(sel, own, other, weights):
    return pl.pallas_call(
        near_kernel,
        grid_spec=pltpu.PrefetchScalarGridSpec(
            num_scalar_prefetch=1,
            grid=(STEPS,),
            in_specs=row_specs(own + other, WIDTH) + weight_specs(WIDTH, 0) + weight_specs(WIDTH, 1),
            out_specs=[whole((512, 256))] * 3,
        ),
        out_shape=[shape((512, 256), F32)] * 3,
        compiler_params=params(56),
        cost_estimate=cost(0, 0.1),
        name="near_sums",
    )(sel, *own, *other, *weights, *weights)


def activations(sel, own, other, weights, sums, held):
    extra = pl.BlockSpec((128, 128), lambda k, sel: (0, STEPS * WIDTH // 128))
    return pl.pallas_call(
        far_kernel,
        grid_spec=pltpu.PrefetchScalarGridSpec(
            num_scalar_prefetch=1,
            grid=(STEPS,),
            in_specs=row_specs(own[6:] + other, WIDTH)
            + weight_specs(WIDTH, 0)
            + weight_specs(WIDTH, 1)
            + [whole((512, 256))] * 3
            + [extra] * 8
            + [whole((128, 128))],
            out_specs=[whole((512, 896)), whole((512, 768))],
            scratch_shapes=[pltpu.VMEM((512, 256), F32)] * 3 + [pltpu.VMEM((512, 128), F32)],
        ),
        out_shape=[shape((512, 896)), shape((512, 768))],
        compiler_params=params(56),
        cost_estimate=cost(4 * 128 * 768 * WIDTH * STEPS, 15),
        name="activations",
    )(sel, *own[6:], *other, *weights, *weights, *sums, *own, held)


def results(pieces, sel, acts, acts_other, weights, wall, half):
    return pl.pallas_call(
        functools.partial(results_kernel, pieces),
        in_specs=[SM] + [VM] * 6,
        out_specs=[VM] * len(pieces),
        out_shape=[shape((128 * len(group), half + 128)) for group in pieces],
        compiler_params=params(14),
        cost_estimate=cost(2 * 64 * sum(map(len, pieces)) * 1536 * half, 12),
        name="results",
    )(sel, acts, acts_other, *weights, wall)


def weight_grads(swapped, first, count, sel, rows, acts, before, room):
    width, half = WIDTH, WIDTH * STEPS
    at = 1 if swapped else 0
    up_spec = pl.BlockSpec((2, 1, 1, width, 128), lambda k, sel: (0, first + k, sel[at], 0, 0))
    down_spec = pl.BlockSpec((2, 128, width), lambda k, sel: (0, 0, 2 * (first + k) + sel[at]))
    up_shape = shape((2, STEPS, 2, width, 128))
    return pl.pallas_call(
        functools.partial(grads_kernel, swapped),
        grid_spec=pltpu.PrefetchScalarGridSpec(
            num_scalar_prefetch=1,
            grid=(count,),
            in_specs=row_specs(rows, width, first) + [whole((512, 768))] + [HB] * len(before),
            out_specs=[up_spec, up_spec, down_spec],
        ),
        out_shape=[up_shape, up_shape, shape((2, 128, 2 * half))],
        input_output_aliases={2 + len(rows) + i: i for i in range(len(before))},
        compiler_params=params(room),
        cost_estimate=cost(2 * 512 * 768 * width * count, 3.5 * count),
        name="weight_grads",
    )(sel, *rows, acts, *before)


def gate_weights(logits, slot_expert, chosen):
    experts = logits.shape[1]
    held = jnp.arange(experts, dtype=jnp.int32)[:, None] == slot_expert[None, :]
    picked = jnp.sum(jnp.where(held[None], logits[:, :, None], 0.0), axis=1)
    sig = jnp.where(chosen, jax.nn.sigmoid(picked), 0.0)
    return ROUTE_SCALE * sig / jnp.sum(sig, axis=1, keepdims=True)


def add(*values):
    total = values[0].astype(F32)
    for value in values[1:]:
        total = total + value.astype(F32)
    return total.astype(BF)


def per_device(tokens, cotangent, gate_logits, route_slot, slot_expert, w_gate, w_up, w_down):
    tok, wide = tokens.shape
    half = wide // 2
    width = half // STEPS
    slots = slot_expert.shape[0]
    z, core, y, x = (lax.axis_index(a) for a in AXES)
    line = y * NX + x
    sel = jnp.stack([core, 1 - core, line, 2 * (line ^ (NY * NX // 2)) + 1])
    weights = (
        w_gate.reshape(2, STEPS, 2, width, 128),
        w_up.reshape(2, STEPS, 2, width, 128),
        w_down,
    )
    own = pack(sel, tokens, cotangent, gate_logits, route_slot)
    own, later = lax.optimization_barrier((own, sel))
    minus, plus, far = send(own, inner(1)), send(own, inner(-1)), send(own, inner(2))
    a, b = joined([own, plus]), joined([minus, far])
    a_minus, b_plus = send(a, outer(1)), send(b, outer(-1))
    b_minus, a_plus = send(b, outer(1)), send(a, outer(-1))
    a_far, b_far = send(a_minus, outer(1)), send(b_plus, outer(-1))
    wall = send(pack_weights(later, weights), other_core())

    near = [a, b, a_plus, b_plus, a_minus, b_minus]
    near_other = [send(piece, other_core()) for piece in near]
    sums = near_sums(sel, near, near_other, weights)
    (a_on, b_on), sums = lax.optimization_barrier(((a_far, b_far), sums))
    far_rows, far_other = [a_far, b_far], [send(a_on, other_core()), send(b_on, other_core())]
    rows, rows_other = near + far_rows, near_other + far_other
    experts = jnp.tile(jnp.arange(24, dtype=jnp.int32), 3)
    held = experts[:, None] == slot_expert[None, :]
    held = jnp.pad(held.astype(F32), ((0, 128 - 72), (0, 128 - slots))).astype(BF)
    acts, acts_grad = activations(sel, rows, far_other, weights, sums, held)
    acts_other = send(acts, other_core())

    far_a, far_b = results(((6,), (7,)), sel, acts, acts_other, weights, wall, half)
    own_a, own_b, plus_a, plus_b, minus_b, minus_a = results(
        ((0,), (1,), (2,), (3,), (5,), (4,)), sel, acts, acts_other, weights, wall, half
    )
    own_a, acts_grad = lax.optimization_barrier((own_a, acts_grad))
    from_a, from_b = send(far_a, outer(1)), send(far_b, outer(-1))
    b_early, a_early = send(plus_b, outer(1)), send(minus_a, outer(-1))
    a_late = send(add(plus_a, from_a), outer(1))
    b_late = send(add(minus_b, from_b), outer(-1))
    grads = weight_grads(False, 0, 4, sel, rows, acts_grad, [], 52)
    (a_early, b_early), grads = lax.optimization_barrier(((a_early, b_early), grads))
    grads = weight_grads(True, 0, 4, sel, rows_other, acts_grad, grads, 52)
    (a_late, b_late), grads = lax.optimization_barrier(((a_late, b_late), grads))
    keep = (own_a[:64], a_late[:64], a_early[:64])
    to_plus = add(own_a[64:], a_late[64:], a_early[64:])
    to_minus = add(own_b[:64], b_late[:64], b_early[:64])
    to_far = add(own_b[64:], b_late[64:], b_early[64:])
    total = add(
        *keep, send(to_plus, inner(1)), send(to_minus, inner(-1)), send(to_far, inner(2))
    )

    def block_for(by):
        block = lax.dynamic_slice(total, (0, (z + by) % NZ * width), (2 * tok, width))
        return joined([block, total[:, half:]], axis=1)

    last = block_for(0).astype(F32)
    for by in (1, 3, 2):
        last = last + send(block_for(by), along_z(by)).astype(F32)
    mixed, grad_tokens = last[:tok, :width].astype(BF), last[tok:, :width].astype(BF)
    home = sum(last[:tok, width + at : width + at + slots] for at in (0, slots, 2 * slots))
    chosen = jnp.any(
        route_slot[:, :, None] == jnp.arange(slots, dtype=jnp.int32)[None, None, :], axis=1
    )
    _, pull_back = jax.vjp(lambda lg: gate_weights(lg, slot_expert, chosen), gate_logits)
    grad_logits = pull_back(home)[0]
    return (
        mixed,
        grad_tokens,
        grad_logits,
        grads[0].reshape(w_gate.shape),
        grads[1].reshape(w_up.shape),
        grads[2],
    )


def solution(mesh):
    split = Mesh(mesh.devices.reshape(NZ, NC, NY, NX), AXES)
    local, group = ("y", "x"), ("z", "c")
    return jax.shard_map(
        per_device,
        mesh=split,
        in_specs=(
            P(local, None),
            P(local, None),
            P(local, None),
            P(local, None),
            P(),
            P(local, None, group),
            P(local, None, group),
            P(local, group, None),
        ),
        out_specs=(
            P(local, group),
            P(local, group),
            P(local, None),
            P(local, None, group),
            P(local, None, group),
            P(local, group, None),
        ),
        check_vma=False,
    )
```
